256 devices in a mesh: batch: 16 (over z, y_hi), tile: 8 (over y_lo, x), cuts: 2 (over core).
Axes of the slice: x: 4, y: 4 (y_hi: 2, y_lo: 2; y = y_hi * 2 + y_lo), z: 8, core: 2. Of those that a mesh axis runs over, the one named last changes fastest.
Arguments:
- objects: float32 [2, 64, 2, 256, 256], P('cuts', 'tile'), may hold values from -5 to 5
- probe: float32 [4, 2, 256, 256], replicated, may hold values from -5 to 5
- measured: float32 [128, 256, 256], P(('batch', 'tile')), may hold values from 0 to 6
- send_list: int32 [16, 8, 8], P('batch', 'tile'), may hold values from 0 to 7
- corner_slot: int32 [128, 4], P(('batch', 'tile')), may hold values from 0 to 7
- offsets: int32 [128, 2], P(('batch', 'tile')), may hold values from 0 to 255
Outputs:
- new_objects: float32 [2, 64, 2, 256, 256], P('cuts', 'tile')
- new_probe: float32 [4, 2, 256, 256], P('cuts', None, 'tile')
The draws below stay inside these ranges and needn't reach their ends.
Inputs may be any that keep to these rules, and one draw needn't show every extreme that they name: `send_list`: local tile indices of the owner. `corner_slot`: indices of the owner within the group.
All inputs are finite; a program needn't handle non-finite values.
Results may differ from the reference program's by a relative error of at most 0.0003.
Values sent between devices are 32-bit elements; how exact they have to be, the bound alone decides.
No kernel may reach another device: no remote copies, remote signals or barrier semaphores. Data moves between devices by JAX's collectives and lax.ppermute only.
A program may use at most 128 MiB of HBM per device.

```python
import math
import jax
import jax.numpy as jnp
from jax import lax

PATCH = 256
MODES = 4
TILES_DEV = 8
POS_DEV = 1
SLICES = 2
TILES = 64
POSITIONS = 128
N_BATCH = 16
N_TILE = 8


def touch_ends(array, key, smallest, largest):
    longest = array.shape.index(max(array.shape))
    spots = []
    for shift in (0, 1):
        where = [jax.random.randint(jax.random.fold_in(key, axis), (), 0, length) for axis, length in enumerate(array.shape)]
        where[longest] = (where[longest] + shift) % array.shape[longest]
        spots.append(tuple(where))
    return array.at[spots[0]].set(smallest).at[spots[1]].set(largest)


def levels(own_key, extent, cuts, smallest, high):
    loudness = 1.0
    for axis_at, shards_of in cuts:
        heights = jax.random.uniform(jax.random.fold_in(jax.random.fold_in(own_key, 6), axis_at), (shards_of,), jnp.float32, smallest / len(cuts), high / len(cuts))
        loudness = loudness * jnp.repeat(jnp.exp(heights), extent[axis_at] // shards_of).reshape((-1,) + (1,) * (len(extent) - 1 - axis_at))
    return loudness


def normal_values(rng, extent, width, reach, shards=(), kind=jnp.bfloat16):
    values = jax.random.normal(rng, extent, jnp.float32) * width
    if len(shards) > 0:
        values = levels(rng, extent, shards, -0.22, 0.18) * values
    return jnp.clip(values, min=-reach, max=reach).astype(kind)


def setup_inputs(seed: int = 0) -> dict:
    keys = jax.random.split(jax.random.key(seed), 7)
    objects = normal_values(keys[0], (SLICES, TILES, 2, PATCH, PATCH), 0.8, 5.0, ((0, 2), (1, 8)), jnp.float32)
    probe = normal_values(keys[1], (MODES, 2, PATCH, PATCH), 0.5, 5.0, (), jnp.float32)
    measured = jnp.clip(6.0 * jax.random.uniform(keys[2], (POSITIONS, PATCH, PATCH), jnp.float32) ** levels(keys[2], (POSITIONS, PATCH, PATCH), ((0, 128),), -0.2, 0.2), 0.0, 6.0)
    send_list = touch_ends(jax.random.randint(keys[3], (N_BATCH, N_TILE, N_TILE), 0, TILES_DEV), jax.random.fold_in(keys[3], 1), 0, TILES_DEV - 1).astype(jnp.int32)
    corner_slot = touch_ends(jax.random.randint(keys[4], (POSITIONS, 4), 0, N_TILE), jax.random.fold_in(keys[4], 1), 0, N_TILE - 1).astype(jnp.int32)
    offsets = touch_ends(jax.random.randint(keys[5], (POSITIONS, 2), 0, PATCH), jax.random.fold_in(keys[5], 1), 0, PATCH - 1).astype(jnp.int32)
    return {"objects": objects, "probe": probe, "measured": measured, "send_list": send_list, "corner_slot": corner_slot, "offsets": offsets}


OBJECT_RATE = 0.02
PROBE_RATE = 0.05

def chirp_factor(length, dtype):
    counter = jnp.arange(length, dtype=jnp.int32)
    signed = jnp.where(counter < length // 2, counter, counter - length)
    quadric = signed * signed % (2 * length)
    angle = math.pi / length * quadric.astype(dtype)
    single = lax.complex(jnp.cos(angle), -jnp.sin(angle))
    return single[:, None] * single[None, :]

def reference(objects, probe, measured, send_list, corner_slot, offsets):
    length = PATCH
    tile_field = lax.complex(objects[:, :, 0], objects[:, :, 1])
    probe_field = lax.complex(probe[:, 0], probe[:, 1])
    transfer = chirp_factor(length, objects.dtype)
    batch_place = jnp.arange(POSITIONS, dtype=jnp.int32) // POS_DEV
    zero_index = jnp.zeros((), jnp.int32)

    def one_position(running, entries):
        tile_grad, probe_grad = running
        intensity_data, slot_row, start_cell, device_place = entries
        start_row = start_cell[0].astype(jnp.int32)
        start_col = start_cell[1].astype(jnp.int32)
        group_index = device_place // N_TILE
        member_index = device_place % N_TILE
        local_index = send_list[group_index, slot_row, member_index]
        tile_ids = (slot_row * TILES_DEV + local_index).astype(jnp.int32)
        corner_tiles = tile_field[:, tile_ids]
        region = corner_tiles.reshape(SLICES, 2, 2, length, length).transpose(0, 1, 3, 2, 4)
        region = region.reshape(SLICES, 2 * length, 2 * length)
        patch_pair = lax.dynamic_slice(region, (zero_index, start_row, start_col), (SLICES, length, length))
        first_patch = patch_pair[0]
        second_patch = patch_pair[1]
        spread = jnp.fft.ifft2(jnp.fft.fft2(probe_field * first_patch[None]) * transfer)
        far_wave = jnp.fft.fft2(second_patch[None] * spread, norm='ortho')
        intensity = lax.optimization_barrier(jnp.sum(jnp.real(far_wave) ** 2 + jnp.imag(far_wave) ** 2, axis=0))
        residual = intensity - intensity_data
        returned = jnp.fft.ifft2(residual[None] * far_wave, norm='ortho')
        grad_second = lax.optimization_barrier(jnp.sum(jnp.conj(spread) * returned, axis=0))
        spread_back = jnp.fft.ifft2(jnp.fft.fft2(jnp.conj(second_patch)[None] * returned) * jnp.conj(transfer))
        grad_first = lax.optimization_barrier(jnp.sum(jnp.conj(probe_field) * spread_back, axis=0))
        probe_grad = probe_grad + jnp.conj(first_patch)[None] * spread_back
        grad_pair = jnp.stack([grad_first, grad_second])
        zero_region = jnp.zeros((SLICES, 2 * length, 2 * length), grad_pair.dtype)
        region_grad = lax.dynamic_update_slice(zero_region, grad_pair, (zero_index, start_row, start_col))
        corner_grad = region_grad.reshape(SLICES, 2, length, 2, length).transpose(0, 1, 3, 2, 4)
        corner_grad = corner_grad.reshape(SLICES, 4, length, length)
        tile_grad = tile_grad.at[:, tile_ids].add(corner_grad)
        return ((tile_grad, probe_grad), None)
    start_state = (jnp.zeros_like(tile_field), jnp.zeros_like(probe_field))
    final_state, unused_output = lax.scan(one_position, start_state, (measured, corner_slot, offsets, batch_place))
    tile_grad, probe_grad = final_state
    new_tiles = tile_field - OBJECT_RATE * tile_grad
    new_modes = probe_field - PROBE_RATE / math.sqrt(POSITIONS) * probe_grad
    new_objects = jnp.stack([jnp.real(new_tiles), jnp.imag(new_tiles)], axis=2)
    new_probe = jnp.stack([jnp.real(new_modes), jnp.imag(new_modes)], axis=1)
    return (new_objects, new_probe)
```

```python
from functools import partial
import math

import jax
import jax.numpy as jnp
from jax import lax
from jax.experimental import pallas as pl
from jax.experimental.pallas import tpu as pltpu
from jax.sharding import PartitionSpec as P
import ml_dtypes
import numpy as np

OBJECT_RATE = 0.02
PROBE_RATE = 0.05
LANES = 128
BIG = pltpu.CompilerParams(vmem_limit_bytes=56 * 1024 * 1024)
F32 = jnp.float32
BF16 = jnp.bfloat16


def halves(matrix):
    upper = matrix.astype(ml_dtypes.bfloat16)
    lower = (matrix - upper.astype(np.float64)).astype(ml_dtypes.bfloat16)
    return upper, lower


def block_matrices(matrix):
    re, im = matrix.real, matrix.imag
    left = np.block([[re, -im], [im, re]])
    right = np.block([[re, im], [-im, re]])
    return halves(left) + halves(right)


def transform_tables(length):
    counter = np.arange(length)
    wave = np.exp(-2j * math.pi / length * (counter[:, None] * counter[None, :] % length))
    signed = np.where(counter < length // 2, counter, counter - length)
    chirp = np.exp(-1j * math.pi / length * (signed * signed % (2 * length)))
    fresnel = (np.conj(wave) * chirp[None, :]) @ wave / length
    return block_matrices(fresnel) + block_matrices(wave / math.sqrt(length))


def split(value):
    upper = value.astype(BF16)
    lower = (value - upper.astype(F32)).astype(BF16)
    return upper, lower


def dot(a, b):
    return jnp.dot(a, b, preferred_element_type=F32)


def two_sided(re, im, left, right):
    n = re.shape[0]
    upper, lower = split(jnp.concatenate([re, im], axis=0))
    rows = dot(left[0][...], upper) + dot(left[0][...], lower) + dot(left[1][...], upper)
    upper, lower = split(jnp.concatenate([rows[:n], rows[n:]], axis=1))
    both = dot(upper, right[0][...]) + dot(lower, right[0][...]) + dot(upper, right[1][...])
    return both[:, :n], both[:, n:]


def gather_kernel(pick_ref, tile_ref, out_ref):
    n = tile_ref.shape[-1]
    for part in range(2):
        for side in range(n // LANES):
            panel = part * (n // LANES) + side
            out_ref[0, panel * n : (panel + 1) * n, :] = tile_ref[0, part, :, side * LANES : (side + 1) * LANES]


def gather_tiles(pick, tiles):
    count = pick.shape[0]
    n = tiles.shape[-1]
    rows = 2 * n * (n // LANES)
    return pl.pallas_call(
        gather_kernel,
        grid_spec=pltpu.PrefetchScalarGridSpec(
            num_scalar_prefetch=1,
            grid=(count,),
            in_specs=[pl.BlockSpec((1, 2, n, n), lambda i, pick: (pick[i], 0, 0, 0))],
            out_specs=pl.BlockSpec((1, rows, LANES), lambda i, pick: (i, 0, 0)),
        ),
        out_shape=jax.ShapeDtypeStruct((count, rows, LANES), F32),
        compiler_params=BIG,
        name="gather_tiles",
    )(pick, tiles)


def select_kernel(n, info_ref, c0_ref, c1_ref, c2_ref, c3_ref, out_ref):
    y0, x0 = info_ref[4], info_ref[5]
    sides = n // LANES
    for panel in range(2 * sides):
        rows = slice(panel * n, (panel + 1) * n)
        u = lax.broadcasted_iota(jnp.int32, (n, LANES), 0)
        v = lax.broadcasted_iota(jnp.int32, (n, LANES), 1) + (panel % sides) * LANES
        low, right = u < y0, v < x0
        upper = jnp.where(right, c1_ref[0, rows, :], c0_ref[0, rows, :])
        lower = jnp.where(right, c3_ref[0, rows, :], c2_ref[0, rows, :])
        out_ref[rows, :] = jnp.where(low, lower, upper)


def select_corners(info, arrived, n):
    rows = arrived.shape[1]
    spec = lambda k: pl.BlockSpec((1, rows, LANES), lambda i, info: (info[k], 0, 0))
    return pl.pallas_call(
        partial(select_kernel, n),
        grid_spec=pltpu.PrefetchScalarGridSpec(
            num_scalar_prefetch=1,
            grid=(1,),
            in_specs=[spec(0), spec(1), spec(2), spec(3)],
            out_specs=pl.BlockSpec((rows, LANES), lambda i, info: (0, 0)),
        ),
        out_shape=jax.ShapeDtypeStruct((rows, LANES), F32),
        compiler_params=BIG,
        name="select_corners",
    )(info, arrived, arrived, arrived, arrived)


def wave_kernel(
    info_ref, own_ref, other_ref, probe_ref, data_ref, meta_ref,
    pl0, pl1, pr0, pr1, fl0, fl1, fr0, fr1,
    out_ref, spread, far, rolled, weight, total, q0, q1,
):
    n = data_ref.shape[-1]
    modes = probe_ref.shape[0]
    half = modes // 2
    sides = n // LANES
    groups = out_ref.shape[0]
    batches = 2 * sides * n // 8 // groups
    y0, x0, cut = info_ref[4], info_ref[5], info_ref[6]
    y_back, x_back = lax.rem(n - y0, n), lax.rem(n - x0, n)
    first = cut == 0
    prop_left, prop_right = (pl0, pl1), (pr0, pr1)
    far_left, far_right = (fl0, fl1), (fr0, fr1)
    for panel in range(2 * sides):
        part, side = panel // sides, panel % sides
        own = own_ref[panel * n : (panel + 1) * n, :]
        other = other_ref[panel * n : (panel + 1) * n, :]
        lanes = slice(side * LANES, (side + 1) * LANES)
        q0[part, :, lanes] = jnp.where(first, own, other)
        q1[part, :, lanes] = jnp.where(first, other, own)
    weight[...] = -data_ref[0]

    def forward(m, carry):
        pre = pltpu.roll(pltpu.roll(probe_ref[m, 0], y0, 0), x0, 1)
        pim = pltpu.roll(pltpu.roll(probe_ref[m, 1], y0, 0), x0, 1)
        rolled[m, 0], rolled[m, 1] = pre, pim
        re, im = two_sided(
            pre * q0[0] - pim * q0[1], pre * q0[1] + pim * q0[0], prop_left, prop_right
        )
        spread[m, 0], spread[m, 1] = re, im
        re, im = two_sided(q1[0] * re - q1[1] * im, q1[0] * im + q1[1] * re, far_left, far_right)
        far[m, 0], far[m, 1] = re, im
        weight[...] += re * re + im * im
        return carry

    lax.fori_loop(0, modes, forward, 0)
    total[...] = jnp.zeros_like(total)

    def backward(m, carry):
        cre, cim = two_sided(
            weight[...] * far[m, 0], weight[...] * far[m, 1], far_right, far_left
        )

        @pl.when(jnp.logical_not(first))
        def _():
            sre, sim = spread[m, 0], spread[m, 1]
            total[0] += sre * cre + sim * cim
            total[1] += sre * cim - sim * cre

        @pl.when(jnp.logical_or(first, m >= half))
        def _():
            zre, zim = two_sided(
                q1[0] * cre + q1[1] * cim, q1[0] * cim - q1[1] * cre, prop_right, prop_left
            )

            @pl.when(first)
            def _():
                pre, pim = rolled[m, 0], rolled[m, 1]
                total[0] += pre * zre + pim * zim
                total[1] += pre * zim - pim * zre

            @pl.when(lax.div(m, half) == cut)
            def _():
                slot = lax.rem(m, half)
                parts = (q0[0] * zre + q0[1] * zim, q0[0] * zim - q0[1] * zre)
                for part in range(2):
                    term = pltpu.roll(pltpu.roll(parts[part], y_back, 0), x_back, 1)
                    rows = n // groups
                    for side in range(sides):
                        base = batches * 8 + (slot * 2 + part) * sides * rows + side * rows
                        base = pl.multiple_of(base, 8)
                        for t in range(groups):
                            out_ref[t, pl.ds(base, rows), :] = term[
                                t * rows : (t + 1) * rows, side * LANES : (side + 1) * LANES
                            ]

        return carry

    lax.fori_loop(0, modes, backward, 0)
    for j in range(2 * sides * n // 8):
        b, t = j // groups, j % groups
        panel, row = divmod(j * 8, n)
        part, side = panel // sides, panel % sides
        out_ref[t, b * 8 : (b + 1) * 8, :] = total[
            part, row : row + 8, side * LANES : (side + 1) * LANES
        ]
    rows = out_ref.shape[1]
    for t in range(groups):
        out_ref[t, rows - 8 : rows, :] = meta_ref[...]


def wave_terms(info, own, other, probe, measured, meta, groups):
    n = probe.shape[-1]
    modes = probe.shape[0]
    tables = [jnp.asarray(table) for table in transform_tables(n)]
    g_rows = 2 * n * n // LANES // groups
    rows = g_rows + modes * n * n // LANES // groups + 8
    whole = pl.BlockSpec(memory_space=pltpu.VMEM)
    return pl.pallas_call(
        wave_kernel,
        in_specs=[pl.BlockSpec(memory_space=pltpu.SMEM)] + [whole] * (5 + len(tables)),
        out_specs=whole,
        out_shape=jax.ShapeDtypeStruct((groups, rows, LANES), F32),
        scratch_shapes=[
            pltpu.VMEM((modes, 2, n, n), F32),
            pltpu.VMEM((modes, 2, n, n), F32),
            pltpu.VMEM((modes, 2, n, n), F32),
            pltpu.VMEM((n, n), F32),
            pltpu.VMEM((2, n, n), F32),
            pltpu.VMEM((2, n, n), F32),
            pltpu.VMEM((2, n, n), F32),
        ],
        compiler_params=BIG,
        name="wave_terms",
    )(info, own, other, probe, measured, meta, *tables)


def regroup_kernel(g_tiles, p_rows, in_ref, out_ref):
    groups = in_ref.shape[0]
    batches = out_ref.shape[0]
    last = in_ref.shape[1] - 8
    for b in range(batches):
        for t in range(groups):
            out_ref[b, t * 8 : (t + 1) * 8, :] = in_ref[t, b * 8 : (b + 1) * 8, :]
        base = g_tiles * 8 + b * p_rows
        term = in_ref[0, base : base + p_rows, :]
        for t in range(1, groups):
            term = term + in_ref[t, base : base + p_rows, :]
        out_ref[b, groups * 8 : groups * 8 + p_rows, :] = term
        for t in range(groups):
            row = groups * 8 + p_rows + t
            out_ref[b, row : row + 1, :] = in_ref[t, last : last + 1, :]


def regroup(pieces, batches):
    groups, rows, _ = pieces.shape
    p_rows = (rows - 8 - batches * 8) // batches
    whole = pl.BlockSpec(memory_space=pltpu.VMEM)
    return pl.pallas_call(
        partial(regroup_kernel, batches, p_rows),
        in_specs=[whole],
        out_specs=whole,
        out_shape=jax.ShapeDtypeStruct((batches, groups * 8 + p_rows + 8, LANES), F32),
        compiler_params=BIG,
        name="regroup",
    )(pieces)


def reduce_kernel(n, groups, p_rows, info_ref, table_ref, in_ref, out_ref, acc):
    batches = in_ref.shape[0]
    tiles = acc.shape[1] // 8
    sides = n // LANES
    place = info_ref[7]
    panel, row = lax.div(place * 8, n), lax.rem(place * 8, n)
    u = lax.broadcasted_iota(jnp.int32, (8, LANES), 0) + row
    v = lax.broadcasted_iota(jnp.int32, (8, LANES), 1) + lax.rem(panel, sides) * LANES
    acc[...] = jnp.zeros_like(acc)

    def one_batch(b, carry):
        for t in range(groups):
            at = (b * groups + t) * 8
            value = in_ref[b, t * 8 : (t + 1) * 8, :]
            low, right = u < table_ref[at + 4], v < table_ref[at + 5]
            lower, upper = jnp.where(low, value, 0.0), jnp.where(low, 0.0, value)
            corners = (
                jnp.where(right, 0.0, upper),
                jnp.where(right, upper, 0.0),
                jnp.where(right, 0.0, lower),
                jnp.where(right, lower, 0.0),
            )
            for k in range(4):
                where = pl.ds(pl.multiple_of(table_ref[at + k] * 8, 8), 8)
                acc[k, where, :] += corners[k]
        return carry

    lax.fori_loop(0, batches, one_batch, 0)
    per_owner = tiles // groups * 8
    probe_sum = in_ref[0, groups * 8 : groups * 8 + p_rows, :]
    for b in range(1, batches):
        probe_sum = probe_sum + in_ref[b, groups * 8 : groups * 8 + p_rows, :]
    for o in range(groups):
        rows = slice(o * per_owner, (o + 1) * per_owner)
        summed = (acc[0, rows, :] + acc[1, rows, :]) + (acc[2, rows, :] + acc[3, rows, :])
        for copy in range(2):
            out_ref[copy * groups + o, :per_owner, :] = summed
            out_ref[copy * groups + o, per_owner:, :] = probe_sum


def reduce_positions(info, table, pieces, n, groups, tiles):
    p_rows = pieces.shape[1] - groups * 8 - 8
    whole = pl.BlockSpec(memory_space=pltpu.VMEM)
    smem = pl.BlockSpec(memory_space=pltpu.SMEM)
    return pl.pallas_call(
        partial(reduce_kernel, n, groups, p_rows),
        in_specs=[smem, smem, whole],
        out_specs=whole,
        out_shape=jax.ShapeDtypeStruct((2 * groups, tiles * 8 // groups + p_rows, LANES), F32),
        scratch_shapes=[pltpu.VMEM((4, tiles * 8, LANES), F32)],
        compiler_params=BIG,
        name="reduce_positions",
    )(info, table, pieces)


def pack_kernel(p_rows, place_ref, in_ref, out_ref):
    groups = in_ref.shape[0] // 2
    t_rows = in_ref.shape[1] - p_rows
    for h in range(2):
        for t in range(groups):
            out_ref[h, t * t_rows : (t + 1) * t_rows, :] = in_ref[h * groups + t, :t_rows, :]
        out_ref[h, groups * t_rows :, :] = in_ref[h * groups + place_ref[0], t_rows:, :]


def pack(place, pieces, p_rows):
    groups = pieces.shape[0] // 2
    rows = groups * (pieces.shape[1] - p_rows) + p_rows
    whole = pl.BlockSpec(memory_space=pltpu.VMEM)
    return pl.pallas_call(
        partial(pack_kernel, p_rows),
        in_specs=[pl.BlockSpec(memory_space=pltpu.SMEM), whole],
        out_specs=whole,
        out_shape=jax.ShapeDtypeStruct((2, rows, LANES), F32),
        compiler_params=BIG,
        name="pack",
    )(place, pieces)


def update_kernel(groups, probe_rate, where_ref, *refs):
    tile_ref, grad_ref, probe_ref, pgrad_ref = refs[:4]
    new_tile_ref, new_probe_ref = refs[-2:]
    count = tile_ref.shape[0]
    for t in range(groups):
        for l in range(count):
            at = (t * count + l) * 8
            rows = slice(t * 8, (t + 1) * 8)
            new_tile_ref[l, 0, rows, :] = (
                tile_ref[l, 0, rows, :] - OBJECT_RATE * grad_ref[at : at + 8, :]
            )
    new_probe_ref[0, 0] = probe_ref[0, 0] - probe_rate * pgrad_ref[...]


def update(where, tiles, chunk, probe, state, groups, p_rows, probe_rate, half):
    count, _, n, _ = tiles.shape
    rows = groups * 8
    row_blocks = n // rows
    sides = n // LANES
    strips = n // groups // p_rows
    main = chunk.shape[0] - p_rows

    def tile_at(i, w):
        panel = w[0] // row_blocks
        return (0, panel // sides, lax.rem(w[0], row_blocks), lax.rem(panel, sides))

    def own_probe_at(w):
        strip = lax.rem(w[0], strips)
        panel = w[0] // strips
        return panel // sides // 2, lax.rem(panel // sides, 2), strip, lax.rem(panel, sides)

    def new_probe_at(i, w):
        return own_probe_at(w)

    def probe_at(i, w):
        m, part, strip, side = own_probe_at(w)
        return m + w[1] * half, part, strip + w[2] * strips, side

    tile_spec = pl.BlockSpec((count, 1, rows, LANES), tile_at)
    in_specs = [
        tile_spec,
        pl.BlockSpec((main, LANES), lambda i, w: (0, 0)),
        pl.BlockSpec((1, 1, p_rows, LANES), probe_at),
        pl.BlockSpec((p_rows, LANES), lambda i, w: (main // p_rows, 0)),
    ]
    operands = [tiles, chunk, probe, chunk]
    aliases = {}
    if state is not None:
        in_specs += [pl.BlockSpec(memory_space=pl.ANY)] * 2
        operands += list(state)
        aliases = {5: 0, 6: 1}
    return pl.pallas_call(
        partial(update_kernel, groups, probe_rate),
        grid_spec=pltpu.PrefetchScalarGridSpec(
            num_scalar_prefetch=1,
            grid=(1,),
            in_specs=in_specs,
            out_specs=[tile_spec, pl.BlockSpec((1, 1, p_rows, LANES), new_probe_at)],
        ),
        out_shape=[
            jax.ShapeDtypeStruct(tiles.shape, F32),
            jax.ShapeDtypeStruct((half, 2, n // groups, n), F32),
        ],
        input_output_aliases=aliases,
        compiler_params=BIG,
        cost_estimate=pl.CostEstimate(
            flops=2 * main * LANES, bytes_accessed=12 * main * LANES, transcendentals=0
        ),
        name="update",
    )(where, *operands)


def local(objects, probe, measured, send_list, corner_slot, offsets):
    n = probe.shape[-1]
    half = probe.shape[0] // 2
    groups = lax.axis_size("tile")
    batches = lax.axis_size("batch")
    z_size = batches // 2
    cut = lax.axis_index("cuts")
    member = lax.axis_index("tile")
    batch = lax.axis_index("batch")
    tiles = objects[0]
    tile_count = tiles.shape[0]
    info = jnp.concatenate(
        [
            corner_slot.reshape(-1),
            offsets.reshape(-1),
            jnp.stack([cut, batch * groups + member]).astype(jnp.int32),
        ]
    )
    meta_row = jnp.concatenate(
        [send_list.reshape(-1), corner_slot.reshape(-1), offsets.reshape(-1)]
    ).astype(F32)
    meta = jnp.zeros((8, LANES), F32).at[0, : meta_row.shape[0]].set(meta_row)

    with jax.named_scope("fetch_tiles"):
        outgoing = gather_tiles(send_list.reshape(-1), tiles)
        arrived = lax.all_to_all(outgoing, "tile", split_axis=0, concat_axis=0, tiled=True)
        own = select_corners(info, arrived, n)
        other = lax.ppermute(own, "cuts", [(0, 1), (1, 0)])
    with jax.named_scope("waves"):
        pieces = wave_terms(info, own, other, probe, measured, meta, groups)
    with jax.named_scope("return_terms"):
        pieces = lax.all_to_all(pieces, "tile", split_axis=0, concat_axis=0, tiled=True)
        pieces = regroup(pieces, batches)
        pieces = lax.all_to_all(pieces, "batch", split_axis=0, concat_axis=0, tiled=True)
        last = pieces.shape[1] - 8
        notes = pieces[:, last:, : meta_row.shape[0]].astype(jnp.int32)
        lists, slots, starts = notes[..., :groups], notes[..., groups : groups + 4], notes[..., groups + 4 :]
        owners = jnp.arange(groups, dtype=jnp.int32)
        chosen = slots[:, None, :, :] == owners[None, :, None, None]
        sent = jnp.sum(jnp.where(chosen, lists[:, :, :, None], 0), axis=1)
        table = jnp.concatenate(
            [slots * tile_count + sent, starts, jnp.zeros_like(starts)], axis=-1
        ).reshape(-1)
        p_rows = last - groups * 8
        summed = reduce_positions(info, table, pieces, n, groups, groups * tile_count)
        planes = [
            [(z * 2 + h) * groups + t for h in range(2) for t in range(groups)]
            for z in range(z_size)
        ]
        summed = lax.all_to_all(
            summed, ("batch", "tile"), split_axis=0, concat_axis=0, axis_index_groups=planes, tiled=True
        )
        packed = pack(member.reshape(1).astype(jnp.int32), summed, p_rows)
    with jax.named_scope("spread_sums"):
        onward = [(i, (i + 2) % batches) for i in range(batches)]
        backward = [(i, (i - 2) % batches) for i in range(batches)]
        z = batch // 2
        rate = PROBE_RATE / math.sqrt(batches * groups * measured.shape[0])
        found = []
        ahead = [packed[0], packed[1]]
        behind = [packed[0], packed[1]]
        for h in range(2):
            found.append((z, h, packed[h]))
        for step in range(1, z_size // 2 + 1):
            final = step == z_size // 2
            for h in range(2):
                if not (final and h == 1):
                    ahead[h] = lax.ppermute(ahead[h], "batch", onward)
                    found.append((z - step, h, ahead[h]))
                if not (final and h == 0):
                    behind[h] = lax.ppermute(behind[h], "batch", backward)
                    found.append((z + step, h, behind[h]))
        state = None
        for place, h, chunk in found:
            row = lax.rem(place + z_size, z_size) * 2 + h
            where = jnp.stack([row, cut, member]).astype(jnp.int32)
            state = update(where, tiles, chunk, probe, state, groups, p_rows, rate, half)
    return (state[0][None], state[1])


def solution(mesh):
    in_specs = (
        P("cuts", "tile", None, None, None),
        P(),
        P(("batch", "tile"), None, None),
        P("batch", "tile", None),
        P(("batch", "tile"), None),
        P(("batch", "tile"), None),
    )
    out_specs = (P("cuts", "tile", None, None, None), P("cuts", None, "tile", None))
    return jax.shard_map(local, mesh=mesh, in_specs=in_specs, out_specs=out_specs, check_vma=False)
```

```python
from functools import partial
import math

import jax
import jax.numpy as jnp
from jax import lax
from jax.experimental import pallas as pl
from jax.experimental.pallas import tpu as pltpu
from jax.sharding import PartitionSpec as P
import ml_dtypes
import numpy as np

OBJECT_RATE = 0.02
PROBE_RATE = 0.05
LANES = 128
BIG = pltpu.CompilerParams(vmem_limit_bytes=56 * 1024 * 1024)
F32 = jnp.float32
BF16 = jnp.bfloat16


def halves(matrix):
    upper = matrix.astype(ml_dtypes.bfloat16)
    lower = (matrix - upper.astype(np.float64)).astype(ml_dtypes.bfloat16)
    return upper, lower


def block_matrices(matrix):
    re, im = matrix.real, matrix.imag
    left = np.block([[re, -im], [im, re]])
    right = np.block([[re, im], [-im, re]])
    return halves(left) + halves(right)


def transform_tables(length):
    counter = np.arange(length)
    wave = np.exp(-2j * math.pi / length * (counter[:, None] * counter[None, :] % length))
    signed = np.where(counter < length // 2, counter, counter - length)
    chirp = np.exp(-1j * math.pi / length * (signed * signed % (2 * length)))
    fresnel = (np.conj(wave) * chirp[None, :]) @ wave / length
    return block_matrices(fresnel) + block_matrices(wave / math.sqrt(length))


def split(value):
    upper = value.astype(BF16)
    lower = (value - upper.astype(F32)).astype(BF16)
    return upper, lower


def dot(a, b):
    return jnp.dot(a, b, preferred_element_type=F32)


def two_sided(fields, left, right):
    n = fields[0][0].shape[0]
    parts = [jnp.concatenate([field[part] for field in fields], axis=1) for part in range(2)]
    upper, lower = split(jnp.concatenate(parts, axis=0))
    rows = dot(left[0][...], upper) + dot(left[0][...], lower) + dot(left[1][...], upper)
    stacked = [
        jnp.concatenate([rows[:n, i * n : (i + 1) * n], rows[n:, i * n : (i + 1) * n]], axis=1)
        for i in range(len(fields))
    ]
    upper, lower = split(jnp.concatenate(stacked, axis=0))
    both = dot(upper, right[0][...]) + dot(lower, right[0][...]) + dot(upper, right[1][...])
    return [
        (both[i * n : (i + 1) * n, :n], both[i * n : (i + 1) * n, n:]) for i in range(len(fields))
    ]


def times(a, b):
    return a[0] * b[0] - a[1] * b[1], a[0] * b[1] + a[1] * b[0]


def conj_times(a, b):
    return a[0] * b[0] + a[1] * b[1], a[0] * b[1] - a[1] * b[0]


def gather_kernel(pick_ref, tile_ref, out_ref):
    n = tile_ref.shape[-1]
    for part in range(2):
        for side in range(n // LANES):
            panel = part * (n // LANES) + side
            out_ref[0, panel * n : (panel + 1) * n, :] = tile_ref[0, part, :, side * LANES : (side + 1) * LANES]


def gather_tiles(pick, tiles):
    count = pick.shape[0]
    n = tiles.shape[-1]
    rows = 2 * n * (n // LANES)
    return pl.pallas_call(
        gather_kernel,
        grid_spec=pltpu.PrefetchScalarGridSpec(
            num_scalar_prefetch=1,
            grid=(count,),
            in_specs=[pl.BlockSpec((1, 2, n, n), lambda i, pick: (pick[i], 0, 0, 0))],
            out_specs=pl.BlockSpec((1, rows, LANES), lambda i, pick: (i, 0, 0)),
        ),
        out_shape=jax.ShapeDtypeStruct((count, rows, LANES), F32),
        compiler_params=BIG,
        name="gather_tiles",
    )(pick, tiles)


def select_kernel(n, info_ref, c0_ref, c1_ref, c2_ref, c3_ref, out_ref):
    y0, x0 = info_ref[4], info_ref[5]
    sides = n // LANES
    for panel in range(2 * sides):
        rows = slice(panel * n, (panel + 1) * n)
        u = lax.broadcasted_iota(jnp.int32, (n, LANES), 0)
        v = lax.broadcasted_iota(jnp.int32, (n, LANES), 1) + (panel % sides) * LANES
        low, right = u < y0, v < x0
        upper = jnp.where(right, c1_ref[0, rows, :], c0_ref[0, rows, :])
        lower = jnp.where(right, c3_ref[0, rows, :], c2_ref[0, rows, :])
        out_ref[rows, :] = jnp.where(low, lower, upper)


def select_corners(info, arrived, n):
    rows = arrived.shape[1]
    spec = lambda k: pl.BlockSpec((1, rows, LANES), lambda i, info: (info[k], 0, 0))
    return pl.pallas_call(
        partial(select_kernel, n),
        grid_spec=pltpu.PrefetchScalarGridSpec(
            num_scalar_prefetch=1,
            grid=(1,),
            in_specs=[spec(0), spec(1), spec(2), spec(3)],
            out_specs=pl.BlockSpec((rows, LANES), lambda i, info: (0, 0)),
        ),
        out_shape=jax.ShapeDtypeStruct((rows, LANES), F32),
        compiler_params=BIG,
        name="select_corners",
    )(info, arrived, arrived, arrived, arrived)


def wave_kernel(
    info_ref, own_ref, other_ref, probe_ref, data_ref, meta_ref,
    pl0, pl1, pr0, pr1, fl0, fl1, fr0, fr1,
    out_ref, spread, far, rolled, weight, total, q0, q1,
):
    n = data_ref.shape[-1]
    modes = probe_ref.shape[0]
    half = modes // 2
    sides = n // LANES
    groups = out_ref.shape[0]
    batches = 2 * sides * n // 8 // groups
    y0, x0, cut = info_ref[4], info_ref[5], info_ref[6]
    y_back, x_back = lax.rem(n - y0, n), lax.rem(n - x0, n)
    first = cut == 0
    prop_left, prop_right = (pl0, pl1), (pr0, pr1)
    far_left, far_right = (fl0, fl1), (fr0, fr1)
    for panel in range(2 * sides):
        part, side = panel // sides, panel % sides
        own = own_ref[panel * n : (panel + 1) * n, :]
        other = other_ref[panel * n : (panel + 1) * n, :]
        lanes = slice(side * LANES, (side + 1) * LANES)
        q0[part, :, lanes] = jnp.where(first, own, other)
        q1[part, :, lanes] = jnp.where(first, other, own)
    weight[...] = -data_ref[0]
    for m in range(modes):
        for part in range(2):
            rolled[m, part] = pltpu.roll(pltpu.roll(probe_ref[m, part], y0, 0), x0, 1)
    pairs = [range(i * half, (i + 1) * half) for i in range(2)]

    for pair in pairs:
        lit = [times((rolled[m, 0], rolled[m, 1]), (q0[0], q0[1])) for m in pair]
        waves = two_sided(lit, prop_left, prop_right)
        exits = []
        for m, wave in zip(pair, waves):
            spread[m, 0], spread[m, 1] = wave
            exits.append(times((q1[0], q1[1]), wave))
        waves = two_sided(exits, far_left, far_right)
        power = jnp.zeros((n, n), F32)
        for m, wave in zip(pair, waves):
            far[m, 0], far[m, 1] = wave
            power = power + (wave[0] * wave[0] + wave[1] * wave[1])
        weight[...] += power

    total[...] = jnp.zeros_like(total)
    for place, pair in enumerate(pairs):
        weighted = [(weight[...] * far[m, 0], weight[...] * far[m, 1]) for m in pair]
        chis = two_sided(weighted, far_right, far_left)
        for m, chi in zip(pair, chis):
            far[m, 0], far[m, 1] = chi

        @pl.when(jnp.logical_not(first))
        def _():
            for m in pair:
                term = conj_times((spread[m, 0], spread[m, 1]), (far[m, 0], far[m, 1]))
                total[0] += term[0]
                total[1] += term[1]

        @pl.when(jnp.logical_or(first, place == 1))
        def _():
            backs = [conj_times((q1[0], q1[1]), (far[m, 0], far[m, 1])) for m in pair]
            zetas = two_sided(backs, prop_right, prop_left)

            @pl.when(first)
            def _():
                for m, zeta in zip(pair, zetas):
                    term = conj_times((rolled[m, 0], rolled[m, 1]), zeta)
                    total[0] += term[0]
                    total[1] += term[1]

            @pl.when(place == cut)
            def _():
                rows = n // groups
                for slot, zeta in enumerate(zetas):
                    parts = conj_times((q0[0], q0[1]), zeta)
                    for part in range(2):
                        term = pltpu.roll(pltpu.roll(parts[part], y_back, 0), x_back, 1)
                        for side in range(sides):
                            base = batches * 8 + ((slot * 2 + part) * sides + side) * rows
                            for t in range(groups):
                                out_ref[t, base : base + rows, :] = term[
                                    t * rows : (t + 1) * rows, side * LANES : (side + 1) * LANES
                                ]

    for j in range(2 * sides * n // 8):
        b, t = j // groups, j % groups
        panel, row = divmod(j * 8, n)
        part, side = panel // sides, panel % sides
        out_ref[t, b * 8 : (b + 1) * 8, :] = total[
            part, row : row + 8, side * LANES : (side + 1) * LANES
        ]
    rows = out_ref.shape[1]
    for t in range(groups):
        out_ref[t, rows - 8 : rows, :] = meta_ref[...]


def wave_terms(info, own, other, probe, measured, meta, groups):
    n = probe.shape[-1]
    modes = probe.shape[0]
    tables = [jnp.asarray(table) for table in transform_tables(n)]
    g_rows = 2 * n * n // LANES // groups
    rows = g_rows + modes * n * n // LANES // groups + 8
    whole = pl.BlockSpec(memory_space=pltpu.VMEM)
    return pl.pallas_call(
        wave_kernel,
        in_specs=[pl.BlockSpec(memory_space=pltpu.SMEM)] + [whole] * (5 + len(tables)),
        out_specs=whole,
        out_shape=jax.ShapeDtypeStruct((groups, rows, LANES), F32),
        scratch_shapes=[
            pltpu.VMEM((modes, 2, n, n), F32),
            pltpu.VMEM((modes, 2, n, n), F32),
            pltpu.VMEM((modes, 2, n, n), F32),
            pltpu.VMEM((n, n), F32),
            pltpu.VMEM((2, n, n), F32),
            pltpu.VMEM((2, n, n), F32),
            pltpu.VMEM((2, n, n), F32),
        ],
        compiler_params=BIG,
        name="wave_terms",
    )(info, own, other, probe, measured, meta, *tables)


def regroup_kernel(g_tiles, p_rows, in_ref, out_ref):
    groups = in_ref.shape[0]
    batches = out_ref.shape[0]
    last = in_ref.shape[1] - 8
    for b in range(batches):
        for t in range(groups):
            out_ref[b, t * 8 : (t + 1) * 8, :] = in_ref[t, b * 8 : (b + 1) * 8, :]
        base = g_tiles * 8 + b * p_rows
        term = in_ref[0, base : base + p_rows, :]
        for t in range(1, groups):
            term = term + in_ref[t, base : base + p_rows, :]
        out_ref[b, groups * 8 : groups * 8 + p_rows, :] = term
        for t in range(groups):
            row = groups * 8 + p_rows + t
            out_ref[b, row : row + 1, :] = in_ref[t, last : last + 1, :]


def regroup(pieces, batches):
    groups, rows, _ = pieces.shape
    p_rows = (rows - 8 - batches * 8) // batches
    whole = pl.BlockSpec(memory_space=pltpu.VMEM)
    return pl.pallas_call(
        partial(regroup_kernel, batches, p_rows),
        in_specs=[whole],
        out_specs=whole,
        out_shape=jax.ShapeDtypeStruct((batches, groups * 8 + p_rows + 8, LANES), F32),
        compiler_params=BIG,
        name="regroup",
    )(pieces)


def reduce_kernel(n, groups, p_rows, info_ref, table_ref, in_ref, out_ref, acc):
    batches = in_ref.shape[0]
    tiles = acc.shape[1] // 8
    sides = n // LANES
    place = info_ref[7]
    panel, row = lax.div(place * 8, n), lax.rem(place * 8, n)
    u = lax.broadcasted_iota(jnp.int32, (8, LANES), 0) + row
    v = lax.broadcasted_iota(jnp.int32, (8, LANES), 1) + lax.rem(panel, sides) * LANES
    acc[...] = jnp.zeros_like(acc)

    def one_batch(b, carry):
        for t in range(groups):
            at = (b * groups + t) * 8
            value = in_ref[b, t * 8 : (t + 1) * 8, :]
            low, right = u < table_ref[at + 4], v < table_ref[at + 5]
            lower, upper = jnp.where(low, value, 0.0), jnp.where(low, 0.0, value)
            corners = (
                jnp.where(right, 0.0, upper),
                jnp.where(right, upper, 0.0),
                jnp.where(right, 0.0, lower),
                jnp.where(right, lower, 0.0),
            )
            for k in range(4):
                where = pl.ds(pl.multiple_of(table_ref[at + k] * 8, 8), 8)
                acc[k, where, :] += corners[k]
        return carry

    lax.fori_loop(0, batches, one_batch, 0)
    per_owner = tiles // groups * 8
    probe_sum = in_ref[0, groups * 8 : groups * 8 + p_rows, :]
    for b in range(1, batches):
        probe_sum = probe_sum + in_ref[b, groups * 8 : groups * 8 + p_rows, :]
    for o in range(groups):
        rows = slice(o * per_owner, (o + 1) * per_owner)
        summed = (acc[0, rows, :] + acc[1, rows, :]) + (acc[2, rows, :] + acc[3, rows, :])
        for copy in range(2):
            out_ref[copy * groups + o, :per_owner, :] = summed
            out_ref[copy * groups + o, per_owner:, :] = probe_sum


def reduce_positions(info, table, pieces, n, groups, tiles):
    p_rows = pieces.shape[1] - groups * 8 - 8
    whole = pl.BlockSpec(memory_space=pltpu.VMEM)
    smem = pl.BlockSpec(memory_space=pltpu.SMEM)
    return pl.pallas_call(
        partial(reduce_kernel, n, groups, p_rows),
        in_specs=[smem, smem, whole],
        out_specs=whole,
        out_shape=jax.ShapeDtypeStruct((2 * groups, tiles * 8 // groups + p_rows, LANES), F32),
        scratch_shapes=[pltpu.VMEM((4, tiles * 8, LANES), F32)],
        compiler_params=BIG,
        name="reduce_positions",
    )(info, table, pieces)


def pack_kernel(p_rows, place_ref, in_ref, *out_refs):
    groups = in_ref.shape[0] // 2
    t_rows = in_ref.shape[1] - p_rows
    for h in range(2):
        for t in range(groups):
            for l in range(t_rows // 8):
                at = (l * groups + t) * 8
                out_refs[h][at : at + 8, :] = in_ref[h * groups + t, l * 8 : (l + 1) * 8, :]
        out_refs[h][groups * t_rows :, :] = in_ref[h * groups + place_ref[0], t_rows:, :]


def pack(place, pieces, p_rows):
    groups = pieces.shape[0] // 2
    rows = groups * (pieces.shape[1] - p_rows) + p_rows
    whole = pl.BlockSpec(memory_space=pltpu.VMEM)
    return pl.pallas_call(
        partial(pack_kernel, p_rows),
        in_specs=[pl.BlockSpec(memory_space=pltpu.SMEM), whole],
        out_specs=[whole, whole],
        out_shape=[jax.ShapeDtypeStruct((rows, LANES), F32)] * 2,
        compiler_params=BIG,
        name="pack",
    )(place, pieces)


def update_kernel(probe_rate, half, p_rows, where_ref, tile_ref, probe_ref, *refs):
    count = (len(refs) - 2) // 2
    grads, pgrads = refs[:count], refs[count : 2 * count]
    new_tile_ref, new_probe_ref = refs[2 * count :]
    n = tile_ref.shape[-1]
    sides = n // LANES
    rows = grads[0].shape[0]
    row_blocks = n // rows
    for i in range(count):
        batch = where_ref[i]
        panel = lax.div(batch, row_blocks)
        part, side = lax.div(panel, sides), lax.rem(panel, sides)
        at = pl.ds(pl.multiple_of(lax.rem(batch, row_blocks) * rows, rows), rows)
        lanes = pl.ds(pl.multiple_of(side * LANES, LANES), LANES)
        new_tile_ref[0, part, at, lanes] = (
            tile_ref[0, part, at, lanes] - OBJECT_RATE * grads[i][...]
        )

    @pl.when(pl.program_id(0) == 0)
    def _():
        strips = new_probe_ref.shape[2] // p_rows
        for i in range(count):
            batch = where_ref[i]
            panel = lax.div(batch, strips)
            field, side = lax.div(panel, sides), lax.rem(panel, sides)
            m, part = lax.div(field, 2), lax.rem(field, 2)
            at = pl.ds(pl.multiple_of(lax.rem(batch, strips) * p_rows, p_rows), p_rows)
            lanes = pl.ds(pl.multiple_of(side * LANES, LANES), LANES)
            new_probe_ref[m, part, at, lanes] = (
                probe_ref[m, part, at, lanes] - probe_rate * pgrads[i][...]
            )


def update(where, tiles, probe, chunks, groups, p_rows, probe_rate):
    count, _, n, _ = tiles.shape
    half = probe.shape[0] // 2
    batches = len(chunks)
    rows = groups * 8
    main = chunks[0].shape[0] - p_rows
    tile_spec = pl.BlockSpec((1, 2, n, n), lambda i, w: (i, 0, 0, 0))
    probe_shape = (half, 2, n // groups, n)
    in_specs = [
        tile_spec,
        pl.BlockSpec(probe_shape, lambda i, w: (w[batches], 0, w[batches + 1], 0)),
    ]
    in_specs += [pl.BlockSpec((rows, LANES), lambda i, w: (i, 0))] * batches
    in_specs += [pl.BlockSpec((p_rows, LANES), lambda i, w: (main // p_rows, 0))] * batches
    return pl.pallas_call(
        partial(update_kernel, probe_rate, half, p_rows),
        grid_spec=pltpu.PrefetchScalarGridSpec(
            num_scalar_prefetch=1,
            grid=(count,),
            in_specs=in_specs,
            out_specs=[tile_spec, pl.BlockSpec(probe_shape, lambda i, w: (0, 0, 0, 0))],
        ),
        out_shape=[jax.ShapeDtypeStruct(tiles.shape, F32), jax.ShapeDtypeStruct(probe_shape, F32)],
        compiler_params=BIG,
        name="update",
    )(where, tiles, probe, *chunks, *chunks)


def local(objects, probe, measured, send_list, corner_slot, offsets):
    n = probe.shape[-1]
    half = probe.shape[0] // 2
    groups = lax.axis_size("tile")
    batches = lax.axis_size("batch")
    z_size = batches // 2
    cut = lax.axis_index("cuts")
    member = lax.axis_index("tile")
    batch = lax.axis_index("batch")
    tiles = objects[0]
    tile_count = tiles.shape[0]
    info = jnp.concatenate(
        [
            corner_slot.reshape(-1),
            offsets.reshape(-1),
            jnp.stack([cut, batch * groups + member]).astype(jnp.int32),
        ]
    )
    meta_row = jnp.concatenate(
        [send_list.reshape(-1), corner_slot.reshape(-1), offsets.reshape(-1)]
    ).astype(F32)
    meta = jnp.zeros((8, LANES), F32).at[0, : meta_row.shape[0]].set(meta_row)

    with jax.named_scope("fetch_tiles"):
        outgoing = gather_tiles(send_list.reshape(-1), tiles)
        arrived = lax.all_to_all(outgoing, "tile", split_axis=0, concat_axis=0, tiled=True)
        own = select_corners(info, arrived, n)
        other = lax.ppermute(own, "cuts", [(0, 1), (1, 0)])
    with jax.named_scope("waves"):
        pieces = wave_terms(info, own, other, probe, measured, meta, groups)
    with jax.named_scope("return_terms"):
        pieces = lax.all_to_all(pieces, "tile", split_axis=0, concat_axis=0, tiled=True)
        pieces = regroup(pieces, batches)
        pieces = lax.all_to_all(pieces, "batch", split_axis=0, concat_axis=0, tiled=True)
        last = pieces.shape[1] - 8
        notes = pieces[:, last:, : meta_row.shape[0]].astype(jnp.int32)
        lists, slots, starts = notes[..., :groups], notes[..., groups : groups + 4], notes[..., groups + 4 :]
        owners = jnp.arange(groups, dtype=jnp.int32)
        chosen = slots[:, None, :, :] == owners[None, :, None, None]
        sent = jnp.sum(jnp.where(chosen, lists[:, :, :, None], 0), axis=1)
        table = jnp.concatenate(
            [slots * tile_count + sent, starts, jnp.zeros_like(starts)], axis=-1
        ).reshape(-1)
        p_rows = last - groups * 8
        summed = reduce_positions(info, table, pieces, n, groups, groups * tile_count)
        planes = [
            [(z * 2 + h) * groups + t for h in range(2) for t in range(groups)]
            for z in range(z_size)
        ]
        summed = lax.all_to_all(
            summed, ("batch", "tile"), split_axis=0, concat_axis=0, axis_index_groups=planes, tiled=True
        )
        packed = pack(member.reshape(1).astype(jnp.int32), summed, p_rows)
    with jax.named_scope("spread_sums"):
        onward = [(i, (i + 2) % batches) for i in range(batches)]
        backward = [(i, (i - 2) % batches) for i in range(batches)]
        z = batch // 2
        rate = PROBE_RATE / math.sqrt(batches * groups * measured.shape[0])
        found = []
        ahead = [packed[0], packed[1]]
        behind = [packed[0], packed[1]]
        for h in range(2):
            found.append((z, h, packed[h]))
        for step in range(1, z_size // 2 + 1):
            final = step == z_size // 2
            for h in range(2):
                if not (final and h == 1):
                    ahead[h] = lax.ppermute(ahead[h], "batch", onward)
                    found.append((z - step, h, ahead[h]))
                if not (final and h == 0):
                    behind[h] = lax.ppermute(behind[h], "batch", backward)
                    found.append((z + step, h, behind[h]))
        places = [lax.rem(place + z_size, z_size) * 2 + h for place, h, _ in found]
        where = jnp.stack(places + [cut, member]).astype(jnp.int32)
        new_tiles, new_probe = update(
            where, tiles, probe, [chunk for _, _, chunk in found], groups, p_rows, rate
        )
    return (new_tiles[None], new_probe)


def solution(mesh):
    in_specs = (
        P("cuts", "tile", None, None, None),
        P(),
        P(("batch", "tile"), None, None),
        P("batch", "tile", None),
        P(("batch", "tile"), None),
        P(("batch", "tile"), None),
    )
    out_specs = (P("cuts", "tile", None, None, None), P("cuts", None, "tile", None))
    return jax.shard_map(local, mesh=mesh, in_specs=in_specs, out_specs=out_specs, check_vma=False)
```

```python
from functools import partial
import math

import jax
import jax.numpy as jnp
from jax import lax
from jax.experimental import pallas as pl
from jax.experimental.pallas import tpu as pltpu
from jax.sharding import PartitionSpec as P
import ml_dtypes
import numpy as np

OBJECT_RATE = 0.02
PROBE_RATE = 0.05
LANES = 128
BIG = pltpu.CompilerParams(vmem_limit_bytes=32 * 1024 * 1024)
SMALL = pltpu.CompilerParams(vmem_limit_bytes=14 * 1024 * 1024)
F32 = jnp.float32
BF16 = jnp.bfloat16


def halves(matrix):
    upper = matrix.astype(ml_dtypes.bfloat16)
    lower = (matrix - upper.astype(np.float64)).astype(ml_dtypes.bfloat16)
    return upper, lower


def block_matrices(matrix):
    re, im = matrix.real, matrix.imag
    left = np.block([[re, -im], [im, re]])
    right = np.block([[re, im], [-im, re]])
    return halves(left) + halves(right)


def transform_tables(length):
    counter = np.arange(length)
    wave = np.exp(-2j * math.pi / length * (counter[:, None] * counter[None, :] % length))
    signed = np.where(counter < length // 2, counter, counter - length)
    chirp = np.exp(-1j * math.pi / length * (signed * signed % (2 * length)))
    fresnel = (np.conj(wave) * chirp[None, :]) @ wave / length
    return block_matrices(fresnel) + block_matrices(wave / math.sqrt(length))


def split(value):
    upper = value.astype(BF16)
    lower = (value - upper.astype(F32)).astype(BF16)
    return upper, lower


def dot(a, b):
    return jnp.dot(a, b, preferred_element_type=F32)


def two_sided(fields, left, right):
    n = fields[0][0].shape[0]
    parts = [jnp.concatenate([field[part] for field in fields], axis=1) for part in range(2)]
    upper, lower = split(jnp.concatenate(parts, axis=0))
    rows = dot(left[0][...], upper) + dot(left[0][...], lower) + dot(left[1][...], upper)
    stacked = [
        jnp.concatenate([rows[:n, i * n : (i + 1) * n], rows[n:, i * n : (i + 1) * n]], axis=1)
        for i in range(len(fields))
    ]
    upper, lower = split(jnp.concatenate(stacked, axis=0))
    both = dot(upper, right[0][...]) + dot(lower, right[0][...]) + dot(upper, right[1][...])
    return [
        (both[i * n : (i + 1) * n, :n], both[i * n : (i + 1) * n, n:]) for i in range(len(fields))
    ]


def times(a, b):
    return a[0] * b[0] - a[1] * b[1], a[0] * b[1] + a[1] * b[0]


def conj_times(a, b):
    return a[0] * b[0] + a[1] * b[1], a[0] * b[1] - a[1] * b[0]


def gather_kernel(pick_ref, tile_ref, out_ref):
    n = tile_ref.shape[-1]
    for side in range(n // LANES):
        out_ref[0, side * n : (side + 1) * n, :] = tile_ref[0, 0, :, side * LANES : (side + 1) * LANES]


def gather_parts(pick, tiles, part):
    count = pick.shape[0]
    n = tiles.shape[-1]
    rows = n * (n // LANES)
    return pl.pallas_call(
        gather_kernel,
        grid_spec=pltpu.PrefetchScalarGridSpec(
            num_scalar_prefetch=1,
            grid=(count,),
            in_specs=[pl.BlockSpec((1, 1, n, n), lambda i, pick: (pick[i], part, 0, 0))],
            out_specs=pl.BlockSpec((1, rows, LANES), lambda i, pick: (i, 0, 0)),
        ),
        out_shape=jax.ShapeDtypeStruct((count, rows, LANES), F32),
        compiler_params=SMALL,
        name="gather_parts",
    )(pick, tiles)


def select_kernel(note_ref, own_ref, re_ref, im_ref, out_ref):
    n = own_ref.shape[-1]
    sides = n // LANES
    y0, x0, here, near = note_ref[4], note_ref[5], note_ref[6], note_ref[7]
    for side in range(sides):
        u = lax.broadcasted_iota(jnp.int32, (n, LANES), 0)
        v = lax.broadcasted_iota(jnp.int32, (n, LANES), 1) + side * LANES
        low, right = u < y0, v < x0
        owner = jnp.where(
            low,
            jnp.where(right, note_ref[3], note_ref[2]),
            jnp.where(right, note_ref[1], note_ref[0]),
        )
        lanes = slice(side * LANES, (side + 1) * LANES)
        for part, far_ref in enumerate((re_ref, im_ref)):
            far = far_ref[0, side * n : (side + 1) * n, :]
            panel = part * sides + side
            out_ref[panel * n : (panel + 1) * n, :] = jnp.where(
                owner == here,
                own_ref[0, part, :, lanes],
                jnp.where(owner == near, far, 0.0),
            )


def select_cells(note, tiles, real, imag):
    n = tiles.shape[-1]
    rows = n * (n // LANES)
    return pl.pallas_call(
        select_kernel,
        grid_spec=pltpu.PrefetchScalarGridSpec(
            num_scalar_prefetch=1,
            grid=(1,),
            in_specs=[
                pl.BlockSpec((1, 2, n, n), lambda i, note: (note[8], 0, 0, 0)),
                pl.BlockSpec((1, rows, LANES), lambda i, note: (note[9], 0, 0)),
                pl.BlockSpec((1, rows, LANES), lambda i, note: (note[9], 0, 0)),
            ],
            out_specs=pl.BlockSpec((2 * rows, LANES), lambda i, note: (0, 0)),
        ),
        out_shape=jax.ShapeDtypeStruct((2 * rows, LANES), F32),
        compiler_params=SMALL,
        name="select_cells",
    )(note, tiles, real, imag)


def fetch(tiles, send_row, note):
    groups = lax.axis_size("tile")
    batches = lax.axis_size("batch")
    width = groups // 2
    member = lax.axis_index("tile")
    column, lower = lax.rem(member, width), lax.div(member, width)
    near = lax.rem(member + width, groups)
    lists = send_row.reshape(2, width)
    far_row = lax.ppermute(send_row, "batch", [(i, i ^ 1) for i in range(batches)])
    along = lambda d: [
        (y * width + x, y * width + (x + d) % width) for y in range(2) for x in range(width)
    ]
    notes = {0: note}
    for d in range(1, width):
        notes[d] = lax.ppermute(note, "tile", along(-d))
    across = lambda row: lax.dynamic_index_in_dim(row.reshape(2, width), 1 - lower, 0, keepdims=False)
    same = [(t, (t + width) % groups) for t in range(groups)]
    other = []
    for b in range(batches):
        for t in range(groups):
            y = (b % 2) * 2 + t // width
            step = (y + 1) % 4 if y % 2 == 1 else (y - 1) % 4
            other.append(
                (b * groups + t, (b // 2 * 2 + step // 2) * groups + step % 2 * width + t % width)
            )
    real = lax.ppermute(gather_parts(across(send_row), tiles, 0), "tile", same)
    imag = lax.ppermute(gather_parts(across(far_row), tiles, 1), ("batch", "tile"), other)
    mine = lax.dynamic_index_in_dim(lists, lower, 0, keepdims=False)
    total = None
    for d in (2, 1, 3, 0):
        x = lax.rem(column + d, width)
        pick = lax.dynamic_index_in_dim(mine, x, 0, keepdims=False)
        extra = jnp.stack([member, near, pick, x]).astype(jnp.int32)
        cells = select_cells(jnp.concatenate([notes[d], extra]), tiles, real, imag)
        if d:
            cells = lax.ppermute(cells, "tile", along(d))
        total = cells if total is None else total + cells
    return total


def wave_kernel(
    info_ref, own_ref, other_ref, probe_ref, data_ref, meta_ref,
    pl0, pl1, pr0, pr1, fl0, fl1, fr0, fr1,
    out_ref, spread, far, rolled, weight, total, q0, q1,
):
    n = data_ref.shape[-1]
    modes = probe_ref.shape[0]
    half = modes // 2
    sides = n // LANES
    groups = out_ref.shape[0]
    batches = 2 * sides * n // 8 // groups
    y0, x0, cut = info_ref[4], info_ref[5], info_ref[6]
    y_back, x_back = lax.rem(n - y0, n), lax.rem(n - x0, n)
    first = cut == 0
    prop_left, prop_right = (pl0, pl1), (pr0, pr1)
    far_left, far_right = (fl0, fl1), (fr0, fr1)
    for panel in range(2 * sides):
        part, side = panel // sides, panel % sides
        own = own_ref[panel * n : (panel + 1) * n, :]
        other = other_ref[panel * n : (panel + 1) * n, :]
        lanes = slice(side * LANES, (side + 1) * LANES)
        q0[part, :, lanes] = jnp.where(first, own, other)
        q1[part, :, lanes] = jnp.where(first, other, own)
    weight[...] = -data_ref[0]
    for m in range(modes):
        for part in range(2):
            rolled[m, part] = pltpu.roll(pltpu.roll(probe_ref[m, part], y0, 0), x0, 1)
    pairs = [range(i * half, (i + 1) * half) for i in range(2)]

    for pair in pairs:
        lit = [times((rolled[m, 0], rolled[m, 1]), (q0[0], q0[1])) for m in pair]
        waves = two_sided(lit, prop_left, prop_right)
        exits = []
        for m, wave in zip(pair, waves):
            spread[m, 0], spread[m, 1] = wave
            exits.append(times((q1[0], q1[1]), wave))
        waves = two_sided(exits, far_left, far_right)
        power = jnp.zeros((n, n), F32)
        for m, wave in zip(pair, waves):
            far[m, 0], far[m, 1] = wave
            power = power + (wave[0] * wave[0] + wave[1] * wave[1])
        weight[...] += power

    total[...] = jnp.zeros_like(total)
    for place, pair in enumerate(pairs):
        weighted = [(weight[...] * far[m, 0], weight[...] * far[m, 1]) for m in pair]
        chis = two_sided(weighted, far_right, far_left)
        for m, chi in zip(pair, chis):
            far[m, 0], far[m, 1] = chi

        @pl.when(jnp.logical_not(first))
        def _():
            for m in pair:
                term = conj_times((spread[m, 0], spread[m, 1]), (far[m, 0], far[m, 1]))
                total[0] += term[0]
                total[1] += term[1]

        @pl.when(jnp.logical_or(first, place == 1))
        def _():
            backs = [conj_times((q1[0], q1[1]), (far[m, 0], far[m, 1])) for m in pair]
            zetas = two_sided(backs, prop_right, prop_left)

            @pl.when(first)
            def _():
                for m, zeta in zip(pair, zetas):
                    term = conj_times((rolled[m, 0], rolled[m, 1]), zeta)
                    total[0] += term[0]
                    total[1] += term[1]

            @pl.when(place == cut)
            def _():
                rows = n // groups
                for slot, zeta in enumerate(zetas):
                    parts = conj_times((q0[0], q0[1]), zeta)
                    for part in range(2):
                        term = pltpu.roll(pltpu.roll(parts[part], y_back, 0), x_back, 1)
                        for side in range(sides):
                            base = batches * 8 + ((slot * 2 + part) * sides + side) * rows
                            for t in range(groups):
                                out_ref[t, base : base + rows, :] = term[
                                    t * rows : (t + 1) * rows, side * LANES : (side + 1) * LANES
                                ]

    for j in range(2 * sides * n // 8):
        b, t = j // groups, j % groups
        panel, row = divmod(j * 8, n)
        part, side = panel // sides, panel % sides
        out_ref[t, b * 8 : (b + 1) * 8, :] = total[
            part, row : row + 8, side * LANES : (side + 1) * LANES
        ]
    rows = out_ref.shape[1]
    for t in range(groups):
        out_ref[t, rows - 8 : rows, :] = meta_ref[...]


def wave_terms(info, own, other, probe, measured, meta, groups):
    n = probe.shape[-1]
    modes = probe.shape[0]
    tables = [jnp.asarray(table) for table in transform_tables(n)]
    g_rows = 2 * n * n // LANES // groups
    rows = g_rows + modes * n * n // LANES // groups + 8
    whole = pl.BlockSpec(memory_space=pltpu.VMEM)
    return pl.pallas_call(
        wave_kernel,
        in_specs=[pl.BlockSpec(memory_space=pltpu.SMEM)] + [whole] * (5 + len(tables)),
        out_specs=whole,
        out_shape=jax.ShapeDtypeStruct((groups, rows, LANES), F32),
        scratch_shapes=[
            pltpu.VMEM((modes, 2, n, n), F32),
            pltpu.VMEM((modes, 2, n, n), F32),
            pltpu.VMEM((modes, 2, n, n), F32),
            pltpu.VMEM((n, n), F32),
            pltpu.VMEM((2, n, n), F32),
            pltpu.VMEM((2, n, n), F32),
            pltpu.VMEM((2, n, n), F32),
        ],
        compiler_params=BIG,
        name="wave_terms",
    )(info, own, other, probe, measured, meta, *tables)


def regroup_kernel(g_tiles, p_rows, in_ref, out_ref):
    groups = in_ref.shape[0]
    batches = out_ref.shape[0]
    last = in_ref.shape[1] - 8
    for b in range(batches):
        for t in range(groups):
            out_ref[b, t * 8 : (t + 1) * 8, :] = in_ref[t, b * 8 : (b + 1) * 8, :]
        base = g_tiles * 8 + b * p_rows
        term = in_ref[0, base : base + p_rows, :]
        for t in range(1, groups):
            term = term + in_ref[t, base : base + p_rows, :]
        out_ref[b, groups * 8 : groups * 8 + p_rows, :] = term
        for t in range(groups):
            row = groups * 8 + p_rows + t
            out_ref[b, row : row + 1, :] = in_ref[t, last : last + 1, :]


def regroup(pieces, batches):
    groups, rows, _ = pieces.shape
    p_rows = (rows - 8 - batches * 8) // batches
    whole = pl.BlockSpec(memory_space=pltpu.VMEM)
    return pl.pallas_call(
        partial(regroup_kernel, batches, p_rows),
        in_specs=[whole],
        out_specs=whole,
        out_shape=jax.ShapeDtypeStruct((batches, groups * 8 + p_rows + 8, LANES), F32),
        compiler_params=SMALL,
        name="regroup",
    )(pieces)


def reduce_kernel(n, groups, p_rows, info_ref, table_ref, in_ref, out_ref, acc):
    batches = in_ref.shape[0]
    tiles = acc.shape[1] // 8
    sides = n // LANES
    place = info_ref[7]
    panel, row = lax.div(place * 8, n), lax.rem(place * 8, n)
    u = lax.broadcasted_iota(jnp.int32, (8, LANES), 0) + row
    v = lax.broadcasted_iota(jnp.int32, (8, LANES), 1) + lax.rem(panel, sides) * LANES
    acc[...] = jnp.zeros_like(acc)

    def one_batch(b, carry):
        for t in range(groups):
            at = (b * groups + t) * 8
            value = in_ref[b, t * 8 : (t + 1) * 8, :]
            low, right = u < table_ref[at + 4], v < table_ref[at + 5]
            lower, upper = jnp.where(low, value, 0.0), jnp.where(low, 0.0, value)
            corners = (
                jnp.where(right, 0.0, upper),
                jnp.where(right, upper, 0.0),
                jnp.where(right, 0.0, lower),
                jnp.where(right, lower, 0.0),
            )
            for k in range(4):
                where = pl.ds(pl.multiple_of(table_ref[at + k] * 8, 8), 8)
                acc[k, where, :] += corners[k]
        return carry

    lax.fori_loop(0, batches, one_batch, 0)
    per_owner = tiles // groups * 8
    probe_sum = in_ref[0, groups * 8 : groups * 8 + p_rows, :]
    for b in range(1, batches):
        probe_sum = probe_sum + in_ref[b, groups * 8 : groups * 8 + p_rows, :]
    for o in range(groups):
        rows = slice(o * per_owner, (o + 1) * per_owner)
        summed = (acc[0, rows, :] + acc[1, rows, :]) + (acc[2, rows, :] + acc[3, rows, :])
        for copy in range(2):
            out_ref[copy * groups + o, :per_owner, :] = summed
            out_ref[copy * groups + o, per_owner:, :] = probe_sum


def reduce_positions(info, table, pieces, n, groups, tiles):
    p_rows = pieces.shape[1] - groups * 8 - 8
    whole = pl.BlockSpec(memory_space=pltpu.VMEM)
    smem = pl.BlockSpec(memory_space=pltpu.SMEM)
    return pl.pallas_call(
        partial(reduce_kernel, n, groups, p_rows),
        in_specs=[smem, smem, whole],
        out_specs=whole,
        out_shape=jax.ShapeDtypeStruct((2 * groups, tiles * 8 // groups + p_rows, LANES), F32),
        scratch_shapes=[pltpu.VMEM((4, tiles * 8, LANES), F32)],
        compiler_params=SMALL,
        name="reduce_positions",
    )(info, table, pieces)


def pack_kernel(p_rows, place_ref, in_ref, *out_refs):
    groups = in_ref.shape[0] // 2
    t_rows = in_ref.shape[1] - p_rows
    for h in range(2):
        for t in range(groups):
            for l in range(t_rows // 8):
                at = (l * groups + t) * 8
                out_refs[h][at : at + 8, :] = in_ref[h * groups + t, l * 8 : (l + 1) * 8, :]
        out_refs[h][groups * t_rows :, :] = in_ref[h * groups + place_ref[0], t_rows:, :]


def pack(place, pieces, p_rows):
    groups = pieces.shape[0] // 2
    rows = groups * (pieces.shape[1] - p_rows) + p_rows
    whole = pl.BlockSpec(memory_space=pltpu.VMEM)
    return pl.pallas_call(
        partial(pack_kernel, p_rows),
        in_specs=[pl.BlockSpec(memory_space=pltpu.SMEM), whole],
        out_specs=[whole, whole],
        out_shape=[jax.ShapeDtypeStruct((rows, LANES), F32)] * 2,
        compiler_params=SMALL,
        name="pack",
    )(place, pieces)


def update_kernel(probe_rate, half, p_rows, where_ref, tile_ref, probe_ref, *refs):
    count = (len(refs) - 2) // 2
    grads, pgrads = refs[:count], refs[count : 2 * count]
    new_tile_ref, new_probe_ref = refs[2 * count :]
    n = tile_ref.shape[-1]
    sides = n // LANES
    rows = grads[0].shape[0]
    row_blocks = n // rows
    for i in range(count):
        batch = where_ref[i]
        panel = lax.div(batch, row_blocks)
        part, side = lax.div(panel, sides), lax.rem(panel, sides)
        at = pl.ds(pl.multiple_of(lax.rem(batch, row_blocks) * rows, rows), rows)
        lanes = pl.ds(pl.multiple_of(side * LANES, LANES), LANES)
        new_tile_ref[0, part, at, lanes] = (
            tile_ref[0, part, at, lanes] - OBJECT_RATE * grads[i][...]
        )

    @pl.when(pl.program_id(0) == 0)
    def _():
        strips = new_probe_ref.shape[2] // p_rows
        for i in range(count):
            batch = where_ref[i]
            panel = lax.div(batch, strips)
            field, side = lax.div(panel, sides), lax.rem(panel, sides)
            m, part = lax.div(field, 2), lax.rem(field, 2)
            at = pl.ds(pl.multiple_of(lax.rem(batch, strips) * p_rows, p_rows), p_rows)
            lanes = pl.ds(pl.multiple_of(side * LANES, LANES), LANES)
            new_probe_ref[m, part, at, lanes] = (
                probe_ref[m, part, at, lanes] - probe_rate * pgrads[i][...]
            )


def update(where, tiles, probe, chunks, groups, p_rows, probe_rate):
    count, _, n, _ = tiles.shape
    half = probe.shape[0] // 2
    batches = len(chunks)
    rows = groups * 8
    main = chunks[0].shape[0] - p_rows
    tile_spec = pl.BlockSpec((1, 2, n, n), lambda i, w: (i, 0, 0, 0))
    probe_shape = (half, 2, n // groups, n)
    in_specs = [
        tile_spec,
        pl.BlockSpec(probe_shape, lambda i, w: (w[batches], 0, w[batches + 1], 0)),
    ]
    in_specs += [pl.BlockSpec((rows, LANES), lambda i, w: (i, 0))] * batches
    in_specs += [pl.BlockSpec((p_rows, LANES), lambda i, w: (main // p_rows, 0))] * batches
    return pl.pallas_call(
        partial(update_kernel, probe_rate, half, p_rows),
        grid_spec=pltpu.PrefetchScalarGridSpec(
            num_scalar_prefetch=1,
            grid=(count,),
            in_specs=in_specs,
            out_specs=[tile_spec, pl.BlockSpec(probe_shape, lambda i, w: (0, 0, 0, 0))],
        ),
        out_shape=[jax.ShapeDtypeStruct(tiles.shape, F32), jax.ShapeDtypeStruct(probe_shape, F32)],
        compiler_params=SMALL,
        name="update",
    )(where, tiles, probe, *chunks, *chunks)


def local(objects, probe, measured, send_list, corner_slot, offsets):
    n = probe.shape[-1]
    half = probe.shape[0] // 2
    groups = lax.axis_size("tile")
    batches = lax.axis_size("batch")
    z_size = batches // 2
    cut = lax.axis_index("cuts")
    member = lax.axis_index("tile")
    batch = lax.axis_index("batch")
    tiles = objects[0]
    tile_count = tiles.shape[0]
    info = jnp.concatenate(
        [
            corner_slot.reshape(-1),
            offsets.reshape(-1),
            jnp.stack([cut, batch * groups + member]).astype(jnp.int32),
        ]
    )
    meta_row = jnp.concatenate(
        [send_list.reshape(-1), corner_slot.reshape(-1), offsets.reshape(-1)]
    ).astype(F32)
    meta = jnp.zeros((8, LANES), F32).at[0, : meta_row.shape[0]].set(meta_row)

    with jax.named_scope("fetch_tiles"):
        note = jnp.concatenate([corner_slot.reshape(-1), offsets.reshape(-1)])
        own = fetch(tiles, send_list.reshape(-1), note)
        other = lax.ppermute(own, "cuts", [(0, 1), (1, 0)])
    with jax.named_scope("waves"):
        pieces = wave_terms(info, own, other, probe, measured, meta, groups)
    with jax.named_scope("return_terms"):
        pieces = lax.all_to_all(pieces, "tile", split_axis=0, concat_axis=0, tiled=True)
        pieces = regroup(pieces, batches)
        pieces = lax.all_to_all(pieces, "batch", split_axis=0, concat_axis=0, tiled=True)
        last = pieces.shape[1] - 8
        notes = pieces[:, last:, : meta_row.shape[0]].astype(jnp.int32)
        lists, slots, starts = notes[..., :groups], notes[..., groups : groups + 4], notes[..., groups + 4 :]
        owners = jnp.arange(groups, dtype=jnp.int32)
        chosen = slots[:, None, :, :] == owners[None, :, None, None]
        sent = jnp.sum(jnp.where(chosen, lists[:, :, :, None], 0), axis=1)
        table = jnp.concatenate(
            [slots * tile_count + sent, starts, jnp.zeros_like(starts)], axis=-1
        ).reshape(-1)
        p_rows = last - groups * 8
        summed = reduce_positions(info, table, pieces, n, groups, groups * tile_count)
        planes = [
            [(z * 2 + h) * groups + t for h in range(2) for t in range(groups)]
            for z in range(z_size)
        ]
        summed = lax.all_to_all(
            summed, ("batch", "tile"), split_axis=0, concat_axis=0, axis_index_groups=planes, tiled=True
        )
        packed = pack(member.reshape(1).astype(jnp.int32), summed, p_rows)
    with jax.named_scope("spread_sums"):
        onward = [(i, (i + 2) % batches) for i in range(batches)]
        backward = [(i, (i - 2) % batches) for i in range(batches)]
        z = batch // 2
        rate = PROBE_RATE / math.sqrt(batches * groups * measured.shape[0])
        found = []
        ahead = [packed[0], packed[1]]
        behind = [packed[0], packed[1]]
        for h in range(2):
            found.append((z, h, packed[h]))
        for step in range(1, z_size // 2 + 1):
            final = step == z_size // 2
            for h in range(2):
                if not (final and h == 1):
                    ahead[h] = lax.ppermute(ahead[h], "batch", onward)
                    found.append((z - step, h, ahead[h]))
                if not (final and h == 0):
                    behind[h] = lax.ppermute(behind[h], "batch", backward)
                    found.append((z + step, h, behind[h]))
        places = [lax.rem(place + z_size, z_size) * 2 + h for place, h, _ in found]
        where = jnp.stack(places + [cut, member]).astype(jnp.int32)
        new_tiles, new_probe = update(
            where, tiles, probe, [chunk for _, _, chunk in found], groups, p_rows, rate
        )
    return (new_tiles[None], new_probe)


def solution(mesh):
    in_specs = (
        P("cuts", "tile", None, None, None),
        P(),
        P(("batch", "tile"), None, None),
        P("batch", "tile", None),
        P(("batch", "tile"), None),
        P(("batch", "tile"), None),
    )
    out_specs = (P("cuts", "tile", None, None, None), P("cuts", None, "tile", None))
    return jax.shard_map(local, mesh=mesh, in_specs=in_specs, out_specs=out_specs, check_vma=False)
```

```python
from functools import partial
import math

import jax
import jax.numpy as jnp
from jax import lax
from jax.experimental import pallas as pl
from jax.experimental.pallas import tpu as pltpu
from jax.sharding import PartitionSpec as P
import ml_dtypes
import numpy as np

OBJECT_RATE = 0.02
PROBE_RATE = 0.05
LANES = 128
BIG = pltpu.CompilerParams(vmem_limit_bytes=32 * 1024 * 1024)
SMALL = pltpu.CompilerParams(vmem_limit_bytes=14 * 1024 * 1024)
F32 = jnp.float32
BF16 = jnp.bfloat16


def halves(matrix):
    upper = matrix.astype(ml_dtypes.bfloat16)
    lower = (matrix - upper.astype(np.float64)).astype(ml_dtypes.bfloat16)
    return upper, lower


def block_matrices(matrix):
    re, im = matrix.real, matrix.imag
    left = np.block([[re, -im], [im, re]])
    right = np.block([[re, im], [-im, re]])
    return halves(left) + halves(right)


def transform_tables(length):
    counter = np.arange(length)
    wave = np.exp(-2j * math.pi / length * (counter[:, None] * counter[None, :] % length))
    signed = np.where(counter < length // 2, counter, counter - length)
    chirp = np.exp(-1j * math.pi / length * (signed * signed % (2 * length)))
    fresnel = (np.conj(wave) * chirp[None, :]) @ wave / length
    return block_matrices(fresnel) + block_matrices(wave / math.sqrt(length))


def split(value):
    upper = value.astype(BF16)
    lower = (value - upper.astype(F32)).astype(BF16)
    return upper, lower


def dot(a, b):
    return jnp.dot(a, b, preferred_element_type=F32)


def two_sided(fields, left, right):
    n = fields[0][0].shape[0]
    parts = [jnp.concatenate([field[part] for field in fields], axis=1) for part in range(2)]
    upper, lower = split(jnp.concatenate(parts, axis=0))
    rows = dot(left[0][...], upper) + dot(left[0][...], lower) + dot(left[1][...], upper)
    stacked = [
        jnp.concatenate([rows[:n, i * n : (i + 1) * n], rows[n:, i * n : (i + 1) * n]], axis=1)
        for i in range(len(fields))
    ]
    upper, lower = split(jnp.concatenate(stacked, axis=0))
    both = dot(upper, right[0][...]) + dot(lower, right[0][...]) + dot(upper, right[1][...])
    return [
        (both[i * n : (i + 1) * n, :n], both[i * n : (i + 1) * n, n:]) for i in range(len(fields))
    ]


def times(a, b):
    return a[0] * b[0] - a[1] * b[1], a[0] * b[1] + a[1] * b[0]


def conj_times(a, b):
    return a[0] * b[0] + a[1] * b[1], a[0] * b[1] - a[1] * b[0]


SMEM = pl.BlockSpec(memory_space=pltpu.SMEM)
VMEM = pl.BlockSpec(memory_space=pltpu.VMEM)
HBM = pl.BlockSpec(memory_space=pltpu.HBM)
ANY = pl.BlockSpec(memory_space=pl.ANY)


def in_hbm(value):
    return pltpu.with_memory_space_constraint(value, pltpu.HBM)


def in_vmem(value):
    return pltpu.with_memory_space_constraint(value, pltpu.VMEM)


def pick_kernel(near, part, ids_ref, list_ref, tile_ref, out_ref, sems):
    width = out_ref.shape[0]
    lower = lax.div(ids_ref[2], width)
    row = 1 - lower if near else lower
    copies = []
    for i in range(width):
        tile = tile_ref.at[list_ref[0, 0, row * width + i]]
        copy = pltpu.make_async_copy(
            tile if part is None else tile.at[part], out_ref.at[i], sems.at[i]
        )
        copy.start()
        copies.append(copy)
    for copy in copies:
        copy.wait()


def pick_tiles(ids, send_list, tiles, near, part=None):
    width = send_list.shape[-1] // 2
    shape = tiles.shape[1:] if part is None else tiles.shape[2:]
    return pl.pallas_call(
        partial(pick_kernel, near, part),
        in_specs=[SMEM, SMEM, HBM],
        out_specs=ANY,
        out_shape=jax.ShapeDtypeStruct((width,) + shape, F32),
        scratch_shapes=[pltpu.SemaphoreType.DMA((width,))],
        compiler_params=SMALL,
        name="pick_tiles",
    )(ids, send_list, in_hbm(tiles))


def select_kernel(wanted, ids_ref, *refs):
    steps = sorted({step for pieces in wanted for step, _, _ in pieces})
    notes = dict(zip(steps, refs))
    own_ref, re_ref, im_ref = refs[len(steps) : len(steps) + 3]
    terms = refs[len(steps) + 3 : len(refs) - len(wanted)]
    outs = refs[len(refs) - len(wanted) :]
    n = own_ref.shape[-1]
    width = own_ref.shape[0]
    sides = n // LANES
    here = ids_ref[2]
    near = lax.rem(here + width, 2 * width)
    for pieces, out_ref in zip(wanted, outs):
        for place, (step, part, added) in enumerate(pieces):
            note = notes[step]
            x = lax.rem(lax.rem(here, width) + step, width)
            near_ref = im_ref if part else re_ref
            for side in range(sides):
                u = lax.broadcasted_iota(jnp.int32, (n, LANES), 0)
                v = lax.broadcasted_iota(jnp.int32, (n, LANES), 1) + side * LANES
                low, right = u < note[0, 4], v < note[0, 5]
                owner = jnp.where(
                    low,
                    jnp.where(right, note[0, 3], note[0, 2]),
                    jnp.where(right, note[0, 1], note[0, 0]),
                )
                lanes = slice(side * LANES, (side + 1) * LANES)
                value = jnp.where(
                    owner == here,
                    own_ref[x, part, :, lanes],
                    jnp.where(owner == near, near_ref[x, :, lanes], 0.0),
                )
                if added is not None:
                    for index in added:
                        value = value + terms[index][side * n : (side + 1) * n, :]
                at = (place * sides + side) * n
                out_ref[at : at + n, :] = value


def select_cells(ids, notes, sources, wanted, terms=()):
    n = sources[0].shape[-1]
    rows = n * (n // LANES)
    steps = sorted({step for pieces in wanted for step, _, _ in pieces})
    return pl.pallas_call(
        partial(select_kernel, wanted),
        in_specs=[SMEM] * (1 + len(steps)) + [VMEM] * (3 + len(terms)),
        out_specs=[VMEM] * len(wanted),
        out_shape=[jax.ShapeDtypeStruct((rows * len(pieces), LANES), F32) for pieces in wanted],
        compiler_params=SMALL,
        name="select_cells",
    )(ids, *[notes[step] for step in steps], *sources, *terms)


def fetch(ids, tiles, send_list, note, ready):
    groups = lax.axis_size("tile")
    batches = lax.axis_size("batch")
    width = groups // 2
    along = lambda d: [
        (y * width + x, y * width + (x + d) % width) for y in range(2) for x in range(width)
    ]
    send = lambda block, d: lax.ppermute(block, "tile", along(d))
    far_list = lax.ppermute(send_list, "batch", [(i, i ^ 1) for i in range(batches)])
    same = [(t, (t + width) % groups) for t in range(groups)]
    other = []
    for b in range(batches):
        for t in range(groups):
            y = (b % 2) * 2 + t // width
            step = (y + 1) % 4 if y % 2 == 1 else (y - 1) % 4
            other.append(
                (b * groups + t, (b // 2 * 2 + step // 2) * groups + step % 2 * width + t % width)
            )
    real = lax.ppermute(pick_tiles(ids, send_list, tiles, True, 0), "tile", same)
    imag = lax.ppermute(pick_tiles(ids, far_list, tiles, True, 1), ("batch", "tile"), other)
    notes = {0: note}
    for d in range(1, width):
        notes[d] = send(note, -d)
    notes, ready = lax.optimization_barrier((notes, ready))
    sources = (pick_tiles(ids, send_list, tiles, False), real, imag)
    far_re, far_im = select_cells(ids, notes, sources, [[(2, 0, None)], [(2, 1, None)]])
    far_re, far_im = send(far_re, 1), send(far_im, -1)
    up_im, down_re = select_cells(ids, notes, sources, [[(1, 1, None)], [(3, 0, None)]])
    up_im, down_re = send(up_im, 1), send(down_re, -1)
    up_re, down_im = select_cells(
        ids, notes, sources, [[(1, 0, (0,))], [(3, 1, (1,))]], (far_re, far_im)
    )
    up_re, down_im = send(up_re, 1), send(down_im, -1)
    own = select_cells(
        ids, notes, sources, [[(0, 0, (0, 1)), (0, 1, (2, 3))]], (up_re, down_re, up_im, down_im)
    )[0]
    return own, ready


def roll_kernel(start_ref, probe_ref, out_ref):
    for m in range(probe_ref.shape[0]):
        for part in range(2):
            value = pltpu.roll(probe_ref[m, part], start_ref[0, 0], 0)
            out_ref[m, part] = pltpu.roll(value, start_ref[0, 1], 1)


def roll_probe(offsets, probe):
    return pl.pallas_call(
        roll_kernel,
        in_specs=[SMEM, VMEM],
        out_specs=VMEM,
        out_shape=jax.ShapeDtypeStruct(probe.shape, F32),
        compiler_params=SMALL,
        name="roll_probe",
    )(offsets, probe)


def wave_kernel(
    info_ref, own_ref, other_ref, rolled, data_ref, meta_ref, table_ref,
    out_ref, spread, far, weight, total, q0, q1, tables, sems,
):
    copies = [
        pltpu.make_async_copy(table_ref.at[i], tables.at[i], sems.at[i])
        for i in range(tables.shape[0])
    ]
    for copy in copies:
        copy.start()
    n = data_ref.shape[-1]
    modes = rolled.shape[0]
    half = modes // 2
    sides = n // LANES
    groups = out_ref.shape[0]
    batches = 2 * sides * n // 8 // groups
    cut = info_ref[6]
    y_back, x_back = lax.rem(n - info_ref[4], n), lax.rem(n - info_ref[5], n)
    first = cut == 0
    prop_left, prop_right = (tables.at[0], tables.at[1]), (tables.at[2], tables.at[3])
    far_left, far_right = (tables.at[4], tables.at[5]), (tables.at[6], tables.at[7])
    for panel in range(2 * sides):
        part, side = panel // sides, panel % sides
        own = own_ref[panel * n : (panel + 1) * n, :]
        other = other_ref[panel * n : (panel + 1) * n, :]
        lanes = slice(side * LANES, (side + 1) * LANES)
        q0[part, :, lanes] = jnp.where(first, own, other)
        q1[part, :, lanes] = jnp.where(first, other, own)
    weight[...] = -data_ref[0]
    for copy in copies:
        copy.wait()
    pairs = [range(i * half, (i + 1) * half) for i in range(2)]

    for pair in pairs:
        lit = [times((rolled[m, 0], rolled[m, 1]), (q0[0], q0[1])) for m in pair]
        waves = two_sided(lit, prop_left, prop_right)
        exits = []
        for m, wave in zip(pair, waves):
            spread[m, 0], spread[m, 1] = wave
            exits.append(times((q1[0], q1[1]), wave))
        waves = two_sided(exits, far_left, far_right)
        power = jnp.zeros((n, n), F32)
        for m, wave in zip(pair, waves):
            far[m, 0], far[m, 1] = wave
            power = power + (wave[0] * wave[0] + wave[1] * wave[1])
        weight[...] += power

    total[...] = jnp.zeros_like(total)
    for place, pair in enumerate(pairs):
        weighted = [(weight[...] * far[m, 0], weight[...] * far[m, 1]) for m in pair]
        chis = two_sided(weighted, far_right, far_left)
        for m, chi in zip(pair, chis):
            far[m, 0], far[m, 1] = chi

        @pl.when(jnp.logical_not(first))
        def _():
            for m in pair:
                term = conj_times((spread[m, 0], spread[m, 1]), (far[m, 0], far[m, 1]))
                total[0] += term[0]
                total[1] += term[1]

        @pl.when(jnp.logical_or(first, place == 1))
        def _():
            backs = [conj_times((q1[0], q1[1]), (far[m, 0], far[m, 1])) for m in pair]
            zetas = two_sided(backs, prop_right, prop_left)

            @pl.when(first)
            def _():
                for m, zeta in zip(pair, zetas):
                    term = conj_times((rolled[m, 0], rolled[m, 1]), zeta)
                    total[0] += term[0]
                    total[1] += term[1]

            @pl.when(place == cut)
            def _():
                rows = n // groups
                for slot, zeta in enumerate(zetas):
                    parts = conj_times((q0[0], q0[1]), zeta)
                    for part in range(2):
                        term = pltpu.roll(pltpu.roll(parts[part], y_back, 0), x_back, 1)
                        for side in range(sides):
                            base = batches * 8 + ((slot * 2 + part) * sides + side) * rows
                            for t in range(groups):
                                out_ref[t, base : base + rows, :] = term[
                                    t * rows : (t + 1) * rows, side * LANES : (side + 1) * LANES
                                ]

    for j in range(2 * sides * n // 8):
        b, t = j // groups, j % groups
        panel, row = divmod(j * 8, n)
        part, side = panel // sides, panel % sides
        out_ref[t, b * 8 : (b + 1) * 8, :] = total[
            part, row : row + 8, side * LANES : (side + 1) * LANES
        ]
    rows = out_ref.shape[1]
    for t in range(groups):
        out_ref[t, rows - 8 : rows, :] = meta_ref[...]


def wave_terms(info, own, other, rolled, measured, meta, groups):
    n = rolled.shape[-1]
    modes = rolled.shape[0]
    tables = jnp.asarray(np.stack(transform_tables(n)))
    g_rows = 2 * n * n // LANES // groups
    rows = g_rows + modes * n * n // LANES // groups + 8
    return pl.pallas_call(
        wave_kernel,
        in_specs=[SMEM] + [VMEM] * 5 + [HBM],
        out_specs=VMEM,
        out_shape=jax.ShapeDtypeStruct((groups, rows, LANES), F32),
        scratch_shapes=[
            pltpu.VMEM((modes, 2, n, n), F32),
            pltpu.VMEM((modes, 2, n, n), F32),
            pltpu.VMEM((n, n), F32),
            pltpu.VMEM((2, n, n), F32),
            pltpu.VMEM((2, n, n), F32),
            pltpu.VMEM((2, n, n), F32),
            pltpu.VMEM(tables.shape, BF16),
            pltpu.SemaphoreType.DMA((tables.shape[0],)),
        ],
        compiler_params=BIG,
        name="wave_terms",
    )(info, own, other, rolled, measured, meta, in_hbm(tables))


def regroup_kernel(g_tiles, p_rows, in_ref, out_ref):
    groups = in_ref.shape[0]
    batches = out_ref.shape[0]
    last = in_ref.shape[1] - 8
    for b in range(batches):
        for t in range(groups):
            out_ref[b, t * 8 : (t + 1) * 8, :] = in_ref[t, b * 8 : (b + 1) * 8, :]
        base = g_tiles * 8 + b * p_rows
        term = in_ref[0, base : base + p_rows, :]
        for t in range(1, groups):
            term = term + in_ref[t, base : base + p_rows, :]
        out_ref[b, groups * 8 : groups * 8 + p_rows, :] = term
        for t in range(groups):
            row = groups * 8 + p_rows + t
            out_ref[b, row : row + 1, :] = in_ref[t, last : last + 1, :]


def regroup(pieces, batches):
    groups, rows, _ = pieces.shape
    p_rows = (rows - 8 - batches * 8) // batches
    whole = pl.BlockSpec(memory_space=pltpu.VMEM)
    return pl.pallas_call(
        partial(regroup_kernel, batches, p_rows),
        in_specs=[whole],
        out_specs=whole,
        out_shape=jax.ShapeDtypeStruct((batches, groups * 8 + p_rows + 8, LANES), F32),
        compiler_params=SMALL,
        name="regroup",
    )(pieces)


def reduce_kernel(n, groups, p_rows, info_ref, table_ref, in_ref, out_ref, acc):
    batches = in_ref.shape[0]
    tiles = acc.shape[1] // 8
    sides = n // LANES
    place = info_ref[7]
    panel, row = lax.div(place * 8, n), lax.rem(place * 8, n)
    u = lax.broadcasted_iota(jnp.int32, (8, LANES), 0) + row
    v = lax.broadcasted_iota(jnp.int32, (8, LANES), 1) + lax.rem(panel, sides) * LANES
    acc[...] = jnp.zeros_like(acc)

    def one_batch(b, carry):
        for t in range(groups):
            at = (b * groups + t) * 8
            value = in_ref[b, t * 8 : (t + 1) * 8, :]
            low, right = u < table_ref[at + 4], v < table_ref[at + 5]
            lower, upper = jnp.where(low, value, 0.0), jnp.where(low, 0.0, value)
            corners = (
                jnp.where(right, 0.0, upper),
                jnp.where(right, upper, 0.0),
                jnp.where(right, 0.0, lower),
                jnp.where(right, lower, 0.0),
            )
            for k in range(4):
                where = pl.ds(pl.multiple_of(table_ref[at + k] * 8, 8), 8)
                acc[k, where, :] += corners[k]
        return carry

    lax.fori_loop(0, batches, one_batch, 0)
    per_owner = tiles // groups * 8
    probe_sum = in_ref[0, groups * 8 : groups * 8 + p_rows, :]
    for b in range(1, batches):
        probe_sum = probe_sum + in_ref[b, groups * 8 : groups * 8 + p_rows, :]
    for o in range(groups):
        rows = slice(o * per_owner, (o + 1) * per_owner)
        summed = (acc[0, rows, :] + acc[1, rows, :]) + (acc[2, rows, :] + acc[3, rows, :])
        for copy in range(2):
            out_ref[copy * groups + o, :per_owner, :] = summed
            out_ref[copy * groups + o, per_owner:, :] = probe_sum


def reduce_positions(info, table, pieces, n, groups, tiles):
    p_rows = pieces.shape[1] - groups * 8 - 8
    whole = pl.BlockSpec(memory_space=pltpu.VMEM)
    smem = pl.BlockSpec(memory_space=pltpu.SMEM)
    return pl.pallas_call(
        partial(reduce_kernel, n, groups, p_rows),
        in_specs=[smem, smem, whole],
        out_specs=whole,
        out_shape=jax.ShapeDtypeStruct((2 * groups, tiles * 8 // groups + p_rows, LANES), F32),
        scratch_shapes=[pltpu.VMEM((4, tiles * 8, LANES), F32)],
        compiler_params=SMALL,
        name="reduce_positions",
    )(info, table, pieces)


def pack_kernel(p_rows, place_ref, in_ref, *out_refs):
    groups = in_ref.shape[0] // 2
    t_rows = in_ref.shape[1] - p_rows
    for h in range(2):
        for t in range(groups):
            for l in range(t_rows // 8):
                at = (l * groups + t) * 8
                out_refs[h][at : at + 8, :] = in_ref[h * groups + t, l * 8 : (l + 1) * 8, :]
        out_refs[h][groups * t_rows :, :] = in_ref[h * groups + place_ref[0], t_rows:, :]


def pack(place, pieces, p_rows):
    groups = pieces.shape[0] // 2
    rows = groups * (pieces.shape[1] - p_rows) + p_rows
    whole = pl.BlockSpec(memory_space=pltpu.VMEM)
    return pl.pallas_call(
        partial(pack_kernel, p_rows),
        in_specs=[pl.BlockSpec(memory_space=pltpu.SMEM), whole],
        out_specs=[whole, whole],
        out_shape=[jax.ShapeDtypeStruct((rows, LANES), F32)] * 2,
        compiler_params=SMALL,
        name="pack",
    )(place, pieces)


def update_kernel(probe_rate, p_rows, where_ref, tile_ref, probe_ref, *refs):
    batches = where_ref.shape[0] - 2
    grads = refs[:batches]
    new_tile_ref, new_probe_ref, held, held_probe, in_sems, out_sems, probe_sem = refs[batches:]
    count, _, n, _ = held.shape
    half, _, strip_rows, _ = held_probe.shape
    sides = n // LANES
    groups = n // strip_rows
    rows = groups * 8
    row_blocks = n // rows
    strips = strip_rows // p_rows
    arrivals, leavings = [], []
    for l in range(count):
        arrivals.append(pltpu.make_async_copy(tile_ref.at[l], held.at[l], in_sems.at[l]))
        leavings.append(pltpu.make_async_copy(held.at[l], new_tile_ref.at[l], out_sems.at[l]))
    cut, member = where_ref[batches], where_ref[batches + 1]
    at = pl.ds(pl.multiple_of(member * strip_rows, strip_rows), strip_rows)
    probe_copy = pltpu.make_async_copy(
        probe_ref.at[pl.ds(cut * half, half), :, at, :], held_probe, probe_sem
    )
    for copy in arrivals:
        copy.start()
    probe_copy.start()
    for l in range(count):
        arrivals[l].wait()
        for i in range(batches):
            batch = where_ref[i]
            panel = lax.div(batch, row_blocks)
            part, side = lax.div(panel, sides), lax.rem(panel, sides)
            at = pl.ds(pl.multiple_of(lax.rem(batch, row_blocks) * rows, rows), rows)
            lanes = pl.ds(pl.multiple_of(side * LANES, LANES), LANES)
            held[l, part, at, lanes] = (
                held[l, part, at, lanes] - OBJECT_RATE * grads[i][l * rows : (l + 1) * rows, :]
            )
        leavings[l].start()
    probe_copy.wait()
    for i in range(batches):
        batch = where_ref[i]
        panel = lax.div(batch, strips)
        field, side = lax.div(panel, sides), lax.rem(panel, sides)
        m, part = lax.div(field, 2), lax.rem(field, 2)
        at = pl.ds(pl.multiple_of(lax.rem(batch, strips) * p_rows, p_rows), p_rows)
        lanes = pl.ds(pl.multiple_of(side * LANES, LANES), LANES)
        new_probe_ref[m, part, at, lanes] = (
            held_probe[m, part, at, lanes] - probe_rate * grads[i][count * rows :, :]
        )
    for copy in leavings:
        copy.wait()


def update(where, tiles, probe, chunks, groups, p_rows, probe_rate):
    count, _, n, _ = tiles.shape
    probe_shape = (probe.shape[0] // 2, 2, n // groups, n)
    return pl.pallas_call(
        partial(update_kernel, probe_rate, p_rows),
        in_specs=[SMEM, HBM, HBM] + [VMEM] * len(chunks),
        out_specs=[HBM, VMEM],
        out_shape=[jax.ShapeDtypeStruct(tiles.shape, F32), jax.ShapeDtypeStruct(probe_shape, F32)],
        scratch_shapes=[
            pltpu.VMEM(tiles.shape, F32),
            pltpu.VMEM(probe_shape, F32),
            pltpu.SemaphoreType.DMA((count,)),
            pltpu.SemaphoreType.DMA((count,)),
            pltpu.SemaphoreType.DMA,
        ],
        compiler_params=SMALL,
        name="update",
    )(where, in_hbm(tiles), in_hbm(probe), *map(in_vmem, chunks))


def local(objects, probe, measured, send_list, corner_slot, offsets):
    n = probe.shape[-1]
    half = probe.shape[0] // 2
    groups = lax.axis_size("tile")
    batches = lax.axis_size("batch")
    z_size = batches // 2
    cut = lax.axis_index("cuts")
    member = lax.axis_index("tile")
    batch = lax.axis_index("batch")
    tiles = objects[0]
    tile_count = tiles.shape[0]
    info = jnp.concatenate(
        [
            corner_slot.reshape(-1),
            offsets.reshape(-1),
            jnp.stack([cut, batch * groups + member]).astype(jnp.int32),
        ]
    )
    meta_row = jnp.concatenate(
        [send_list.reshape(-1), corner_slot.reshape(-1), offsets.reshape(-1)]
    ).astype(F32)
    meta = jnp.zeros((8, LANES), F32).at[0, : meta_row.shape[0]].set(meta_row)

    with jax.named_scope("fetch_tiles"):
        ids = jnp.stack([cut, batch, member]).astype(jnp.int32)
        note = jnp.concatenate([corner_slot, offsets], axis=1)
        ready = (roll_probe(offsets, probe), info, meta)
        own, (rolled, info, meta) = fetch(ids, tiles, send_list, note, ready)
        other = lax.ppermute(own, "cuts", [(0, 1), (1, 0)])
    with jax.named_scope("waves"):
        pieces = wave_terms(info, own, other, rolled, measured, meta, groups)
    with jax.named_scope("return_terms"):
        pieces = lax.all_to_all(pieces, "tile", split_axis=0, concat_axis=0, tiled=True)
        pieces = regroup(pieces, batches)
        pieces = lax.all_to_all(pieces, "batch", split_axis=0, concat_axis=0, tiled=True)
        last = pieces.shape[1] - 8
        notes = pieces[:, last:, : meta_row.shape[0]].astype(jnp.int32)
        lists, slots, starts = notes[..., :groups], notes[..., groups : groups + 4], notes[..., groups + 4 :]
        owners = jnp.arange(groups, dtype=jnp.int32)
        chosen = slots[:, None, :, :] == owners[None, :, None, None]
        sent = jnp.sum(jnp.where(chosen, lists[:, :, :, None], 0), axis=1)
        table = jnp.concatenate(
            [slots * tile_count + sent, starts, jnp.zeros_like(starts)], axis=-1
        ).reshape(-1)
        p_rows = last - groups * 8
        summed = reduce_positions(info, table, pieces, n, groups, groups * tile_count)
        planes = [
            [(z * 2 + h) * groups + t for h in range(2) for t in range(groups)]
            for z in range(z_size)
        ]
        summed = lax.all_to_all(
            summed, ("batch", "tile"), split_axis=0, concat_axis=0, axis_index_groups=planes, tiled=True
        )
        packed = pack(member.reshape(1).astype(jnp.int32), summed, p_rows)
    with jax.named_scope("spread_sums"):
        onward = [(i, (i + 2) % batches) for i in range(batches)]
        backward = [(i, (i - 2) % batches) for i in range(batches)]
        z = batch // 2
        rate = PROBE_RATE / math.sqrt(batches * groups * measured.shape[0])
        found = []
        ahead = [packed[0], packed[1]]
        behind = [packed[0], packed[1]]
        for h in range(2):
            found.append((z, h, packed[h]))
        for step in range(1, z_size // 2 + 1):
            final = step == z_size // 2
            for h in range(2):
                if not (final and h == 1):
                    ahead[h] = lax.ppermute(ahead[h], "batch", onward)
                    found.append((z - step, h, ahead[h]))
                if not (final and h == 0):
                    behind[h] = lax.ppermute(behind[h], "batch", backward)
                    found.append((z + step, h, behind[h]))
        places = [lax.rem(place + z_size, z_size) * 2 + h for place, h, _ in found]
        where = jnp.stack(places + [cut, member]).astype(jnp.int32)
        new_tiles, new_probe = update(
            where, tiles, probe, [chunk for _, _, chunk in found], groups, p_rows, rate
        )
    return (new_tiles[None], new_probe)


def solution(mesh):
    in_specs = (
        P("cuts", "tile", None, None, None),
        P(),
        P(("batch", "tile"), None, None),
        P("batch", "tile", None),
        P(("batch", "tile"), None),
        P(("batch", "tile"), None),
    )
    out_specs = (P("cuts", "tile", None, None, None), P("cuts", None, "tile", None))
    return jax.shard_map(local, mesh=mesh, in_specs=in_specs, out_specs=out_specs, check_vma=False)
```

```python
from functools import partial
import math

import jax
import jax.numpy as jnp
from jax import lax
from jax.experimental import pallas as pl
from jax.experimental.pallas import tpu as pltpu
from jax.sharding import PartitionSpec as P
import ml_dtypes
import numpy as np

OBJECT_RATE = 0.02
PROBE_RATE = 0.05
LANES = 128
BIG = pltpu.CompilerParams(vmem_limit_bytes=32 * 1024 * 1024)
SMALL = pltpu.CompilerParams(vmem_limit_bytes=14 * 1024 * 1024)
F32 = jnp.float32
BF16 = jnp.bfloat16


def halves(matrix):
    upper = matrix.astype(ml_dtypes.bfloat16)
    lower = (matrix - upper.astype(np.float64)).astype(ml_dtypes.bfloat16)
    return upper, lower


def block_matrices(matrix):
    re, im = matrix.real, matrix.imag
    left = np.block([[re, -im], [im, re]])
    right = np.block([[re, im], [-im, re]])
    return halves(left) + halves(right)


def transform_tables(length):
    counter = np.arange(length)
    wave = np.exp(-2j * math.pi / length * (counter[:, None] * counter[None, :] % length))
    signed = np.where(counter < length // 2, counter, counter - length)
    chirp = np.exp(-1j * math.pi / length * (signed * signed % (2 * length)))
    fresnel = (np.conj(wave) * chirp[None, :]) @ wave / length
    return block_matrices(fresnel) + block_matrices(wave / math.sqrt(length))


def split(value):
    upper = value.astype(BF16)
    lower = (value - upper.astype(F32)).astype(BF16)
    return upper, lower


def dot(a, b):
    return jnp.dot(a, b, preferred_element_type=F32)


def two_sided(fields, left, right):
    n = fields[0][0].shape[0]
    parts = [jnp.concatenate([field[part] for field in fields], axis=1) for part in range(2)]
    upper, lower = split(jnp.concatenate(parts, axis=0))
    rows = dot(left[0][...], upper) + dot(left[0][...], lower) + dot(left[1][...], upper)
    stacked = [
        jnp.concatenate([rows[:n, i * n : (i + 1) * n], rows[n:, i * n : (i + 1) * n]], axis=1)
        for i in range(len(fields))
    ]
    upper, lower = split(jnp.concatenate(stacked, axis=0))
    both = dot(upper, right[0][...]) + dot(lower, right[0][...]) + dot(upper, right[1][...])
    return [
        (both[i * n : (i + 1) * n, :n], both[i * n : (i + 1) * n, n:]) for i in range(len(fields))
    ]


def times(a, b):
    return a[0] * b[0] - a[1] * b[1], a[0] * b[1] + a[1] * b[0]


def conj_times(a, b):
    return a[0] * b[0] + a[1] * b[1], a[0] * b[1] - a[1] * b[0]


SMEM = pl.BlockSpec(memory_space=pltpu.SMEM)
VMEM = pl.BlockSpec(memory_space=pltpu.VMEM)
HBM = pl.BlockSpec(memory_space=pltpu.HBM)


def in_hbm(value):
    return pltpu.with_memory_space_constraint(value, pltpu.HBM)


def in_vmem(value):
    return pltpu.with_memory_space_constraint(value, pltpu.VMEM)


def pick_kernel(near, steps, ids_ref, list_ref, tile_ref, out_ref, sems):
    width = list_ref.shape[-1] // 2
    lower, column = lax.div(ids_ref[2], width), lax.rem(ids_ref[2], width)
    row = 1 - lower if near else lower
    copies = []
    for i, step in enumerate(steps):
        member = row * width + lax.rem(column + step, width)
        copy = pltpu.make_async_copy(
            tile_ref.at[list_ref[0, 0, member]], out_ref.at[i], sems.at[i]
        )
        copy.start()
        copies.append(copy)
    for copy in copies:
        copy.wait()


def pick_tiles(ids, send_list, tiles, near, steps):
    return pl.pallas_call(
        partial(pick_kernel, near, steps),
        in_specs=[SMEM, SMEM, HBM],
        out_specs=VMEM,
        out_shape=jax.ShapeDtypeStruct((len(steps),) + tiles.shape[1:], F32),
        scratch_shapes=[pltpu.SemaphoreType.DMA((len(steps),))],
        compiler_params=SMALL,
        name="pick_tiles",
    )(ids, send_list, in_hbm(tiles))


def select_kernel(wanted, places, groups, ids_ref, *refs):
    steps = sorted({step for pieces in wanted for step, _, _ in pieces})
    arrays = sorted({places[step][1] for step in steps})
    notes = dict(zip(steps, refs))
    own_ref = refs[len(steps)]
    nears = dict(zip(arrays, refs[len(steps) + 1 :]))
    terms = refs[len(steps) + 1 + len(arrays) : len(refs) - len(wanted)]
    outs = refs[len(refs) - len(wanted) :]
    n = own_ref.shape[-1]
    sides = n // LANES
    here = ids_ref[2]
    near = lax.rem(here + groups // 2, groups)
    for pieces, out_ref in zip(wanted, outs):
        for place, (step, part, added) in enumerate(pieces):
            note = notes[step]
            own_at, array, near_at = places[step]
            for side in range(sides):
                u = lax.broadcasted_iota(jnp.int32, (n, LANES), 0)
                v = lax.broadcasted_iota(jnp.int32, (n, LANES), 1) + side * LANES
                low, right = u < note[0, 4], v < note[0, 5]
                owner = jnp.where(
                    low,
                    jnp.where(right, note[0, 3], note[0, 2]),
                    jnp.where(right, note[0, 1], note[0, 0]),
                )
                lanes = slice(side * LANES, (side + 1) * LANES)
                value = jnp.where(
                    owner == here,
                    own_ref[own_at, part, :, lanes],
                    jnp.where(owner == near, nears[array][near_at, part, :, lanes], 0.0),
                )
                for index in added:
                    value = value + terms[index][side * n : (side + 1) * n, :]
                at = (place * sides + side) * n
                out_ref[at : at + n, :] = value


def select_cells(ids, notes, own, nears, places, wanted, terms=()):
    n = own.shape[-1]
    rows = n * (n // LANES)
    steps = sorted({step for pieces in wanted for step, _, _ in pieces})
    arrays = sorted({places[step][1] for step in steps})
    return pl.pallas_call(
        partial(select_kernel, wanted, places, lax.axis_size("tile")),
        in_specs=[SMEM] * (1 + len(steps)) + [VMEM] * (1 + len(arrays) + len(terms)),
        out_specs=[VMEM] * len(wanted),
        out_shape=[jax.ShapeDtypeStruct((rows * len(pieces), LANES), F32) for pieces in wanted],
        compiler_params=SMALL,
        name="select_cells",
    )(ids, *[notes[step] for step in steps], own, *[nears[i] for i in arrays], *terms)


def fetch(ids, tiles, send_list, note, ready):
    groups = lax.axis_size("tile")
    batches = lax.axis_size("batch")
    width = groups // 2
    along = lambda d: [
        (y * width + x, y * width + (x + d) % width) for y in range(2) for x in range(width)
    ]
    send = lambda block, d: lax.ppermute(block, "tile", along(d))
    far_list = lax.ppermute(send_list, "batch", [(i, i ^ 1) for i in range(batches)])
    same = [(t, (t + width) % groups) for t in range(groups)]
    other = []
    for b in range(batches):
        for t in range(groups):
            y = (b % 2) * 2 + t // width
            step = (y + 1) % 4 if y % 2 == 1 else (y - 1) % 4
            other.append(
                (b * groups + t, (b // 2 * 2 + step // 2) * groups + step % 2 * width + t % width)
            )
    places = {2: (0, 0, 0), 1: (1, 0, 1), 3: (2, 1, 0), 0: (3, 1, 1)}
    first = pick_tiles(ids, send_list, tiles, True, (2, 1))
    first, far_list = lax.optimization_barrier((first, far_list))
    nears = [
        lax.ppermute(first, "tile", same),
        lax.ppermute(pick_tiles(ids, far_list, tiles, True, (3, 0)), ("batch", "tile"), other),
    ]
    notes = {0: note}
    for d in range(1, width):
        notes[d] = send(note, -d)
    own = pick_tiles(ids, send_list, tiles, False, (2, 1, 3, 0))
    own, notes, ready = lax.optimization_barrier((own, notes, ready))
    select = lambda wanted, terms=(): select_cells(ids, notes, own, nears, places, wanted, terms)
    far_re, far_im = select([[(2, 0, ())], [(2, 1, ())]])
    far_re, far_im = send(far_re, 1), send(far_im, -1)
    up_im = send(select([[(1, 1, ())]])[0], 1)
    down_re = send(select([[(3, 0, ())]])[0], -1)
    up_re = send(select([[(1, 0, (0,))]], (far_re,))[0], 1)
    down_im = send(select([[(3, 1, (0,))]], (far_im,))[0], -1)
    patch = select([[(0, 0, (0, 1)), (0, 1, (2, 3))]], (up_re, down_re, up_im, down_im))[0]
    return patch, ready


def roll_kernel(start_ref, probe_ref, out_ref):
    for m in range(probe_ref.shape[0]):
        for part in range(2):
            value = pltpu.roll(probe_ref[m, part], start_ref[0, 0], 0)
            out_ref[m, part] = pltpu.roll(value, start_ref[0, 1], 1)


def roll_probe(offsets, probe):
    return pl.pallas_call(
        roll_kernel,
        in_specs=[SMEM, VMEM],
        out_specs=VMEM,
        out_shape=jax.ShapeDtypeStruct(probe.shape, F32),
        compiler_params=SMALL,
        name="roll_probe",
    )(offsets, probe)


def wave_kernel(
    info_ref, own_ref, other_ref, rolled, data_ref, meta_ref, table_ref,
    out_ref, spread, far, weight, total, q0, q1, tables, sems,
):
    copies = [
        pltpu.make_async_copy(table_ref.at[i], tables.at[i], sems.at[i])
        for i in range(tables.shape[0])
    ]
    for copy in copies:
        copy.start()
    n = data_ref.shape[-1]
    modes = rolled.shape[0]
    half = modes // 2
    sides = n // LANES
    groups = out_ref.shape[0]
    batches = 2 * sides * n // 8 // groups
    cut = info_ref[6]
    y_back, x_back = lax.rem(n - info_ref[4], n), lax.rem(n - info_ref[5], n)
    first = cut == 0
    prop_left, prop_right = (tables.at[0], tables.at[1]), (tables.at[2], tables.at[3])
    far_left, far_right = (tables.at[4], tables.at[5]), (tables.at[6], tables.at[7])
    for panel in range(2 * sides):
        part, side = panel // sides, panel % sides
        own = own_ref[panel * n : (panel + 1) * n, :]
        other = other_ref[panel * n : (panel + 1) * n, :]
        lanes = slice(side * LANES, (side + 1) * LANES)
        q0[part, :, lanes] = jnp.where(first, own, other)
        q1[part, :, lanes] = jnp.where(first, other, own)
    weight[...] = -data_ref[0]
    for copy in copies:
        copy.wait()
    pairs = [range(i * half, (i + 1) * half) for i in range(2)]

    for pair in pairs:
        lit = [times((rolled[m, 0], rolled[m, 1]), (q0[0], q0[1])) for m in pair]
        waves = two_sided(lit, prop_left, prop_right)
        exits = []
        for m, wave in zip(pair, waves):
            spread[m, 0], spread[m, 1] = wave
            exits.append(times((q1[0], q1[1]), wave))
        waves = two_sided(exits, far_left, far_right)
        power = jnp.zeros((n, n), F32)
        for m, wave in zip(pair, waves):
            far[m, 0], far[m, 1] = wave
            power = power + (wave[0] * wave[0] + wave[1] * wave[1])
        weight[...] += power

    total[...] = jnp.zeros_like(total)
    for place, pair in enumerate(pairs):
        weighted = [(weight[...] * far[m, 0], weight[...] * far[m, 1]) for m in pair]
        chis = two_sided(weighted, far_right, far_left)
        for m, chi in zip(pair, chis):
            far[m, 0], far[m, 1] = chi

        @pl.when(jnp.logical_not(first))
        def _():
            for m in pair:
                term = conj_times((spread[m, 0], spread[m, 1]), (far[m, 0], far[m, 1]))
                total[0] += term[0]
                total[1] += term[1]

        @pl.when(jnp.logical_or(first, place == 1))
        def _():
            backs = [conj_times((q1[0], q1[1]), (far[m, 0], far[m, 1])) for m in pair]
            zetas = two_sided(backs, prop_right, prop_left)

            @pl.when(first)
            def _():
                for m, zeta in zip(pair, zetas):
                    term = conj_times((rolled[m, 0], rolled[m, 1]), zeta)
                    total[0] += term[0]
                    total[1] += term[1]

            @pl.when(place == cut)
            def _():
                rows = n // groups
                for slot, zeta in enumerate(zetas):
                    parts = conj_times((q0[0], q0[1]), zeta)
                    for part in range(2):
                        term = pltpu.roll(pltpu.roll(parts[part], y_back, 0), x_back, 1)
                        for side in range(sides):
                            base = batches * 8 + ((slot * 2 + part) * sides + side) * rows
                            for t in range(groups):
                                out_ref[t, base : base + rows, :] = term[
                                    t * rows : (t + 1) * rows, side * LANES : (side + 1) * LANES
                                ]

    for j in range(2 * sides * n // 8):
        b, t = j // groups, j % groups
        panel, row = divmod(j * 8, n)
        part, side = panel // sides, panel % sides
        out_ref[t, b * 8 : (b + 1) * 8, :] = total[
            part, row : row + 8, side * LANES : (side + 1) * LANES
        ]
    rows = out_ref.shape[1]
    for t in range(groups):
        out_ref[t, rows - 8 : rows, :] = meta_ref[...]


def wave_terms(info, own, other, rolled, measured, meta, groups):
    n = rolled.shape[-1]
    modes = rolled.shape[0]
    tables = jnp.asarray(np.stack(transform_tables(n)))
    g_rows = 2 * n * n // LANES // groups
    rows = g_rows + modes * n * n // LANES // groups + 8
    return pl.pallas_call(
        wave_kernel,
        in_specs=[SMEM] + [VMEM] * 5 + [HBM],
        out_specs=VMEM,
        out_shape=jax.ShapeDtypeStruct((groups, rows, LANES), F32),
        scratch_shapes=[
            pltpu.VMEM((modes, 2, n, n), F32),
            pltpu.VMEM((modes, 2, n, n), F32),
            pltpu.VMEM((n, n), F32),
            pltpu.VMEM((2, n, n), F32),
            pltpu.VMEM((2, n, n), F32),
            pltpu.VMEM((2, n, n), F32),
            pltpu.VMEM(tables.shape, BF16),
            pltpu.SemaphoreType.DMA((tables.shape[0],)),
        ],
        compiler_params=BIG,
        name="wave_terms",
    )(info, own, other, rolled, measured, meta, in_hbm(tables))


def regroup_kernel(g_tiles, p_rows, in_ref, out_ref):
    groups = in_ref.shape[0]
    batches = out_ref.shape[0]
    last = in_ref.shape[1] - 8
    for b in range(batches):
        for t in range(groups):
            out_ref[b, t * 8 : (t + 1) * 8, :] = in_ref[t, b * 8 : (b + 1) * 8, :]
        base = g_tiles * 8 + b * p_rows
        term = in_ref[0, base : base + p_rows, :]
        for t in range(1, groups):
            term = term + in_ref[t, base : base + p_rows, :]
        out_ref[b, groups * 8 : groups * 8 + p_rows, :] = term
        for t in range(groups):
            row = groups * 8 + p_rows + t
            out_ref[b, row : row + 1, :] = in_ref[t, last : last + 1, :]


def regroup(pieces, batches):
    groups, rows, _ = pieces.shape
    p_rows = (rows - 8 - batches * 8) // batches
    whole = pl.BlockSpec(memory_space=pltpu.VMEM)
    return pl.pallas_call(
        partial(regroup_kernel, batches, p_rows),
        in_specs=[whole],
        out_specs=whole,
        out_shape=jax.ShapeDtypeStruct((batches, groups * 8 + p_rows + 8, LANES), F32),
        compiler_params=SMALL,
        name="regroup",
    )(pieces)


def reduce_kernel(n, groups, p_rows, info_ref, table_ref, in_ref, out_ref, acc):
    batches = in_ref.shape[0]
    tiles = acc.shape[1] // 8
    sides = n // LANES
    place = info_ref[7]
    panel, row = lax.div(place * 8, n), lax.rem(place * 8, n)
    u = lax.broadcasted_iota(jnp.int32, (8, LANES), 0) + row
    v = lax.broadcasted_iota(jnp.int32, (8, LANES), 1) + lax.rem(panel, sides) * LANES
    acc[...] = jnp.zeros_like(acc)

    def one_batch(b, carry):
        for t in range(groups):
            at = (b * groups + t) * 8
            value = in_ref[b, t * 8 : (t + 1) * 8, :]
            low, right = u < table_ref[at + 4], v < table_ref[at + 5]
            lower, upper = jnp.where(low, value, 0.0), jnp.where(low, 0.0, value)
            corners = (
                jnp.where(right, 0.0, upper),
                jnp.where(right, upper, 0.0),
                jnp.where(right, 0.0, lower),
                jnp.where(right, lower, 0.0),
            )
            for k in range(4):
                where = pl.ds(pl.multiple_of(table_ref[at + k] * 8, 8), 8)
                acc[k, where, :] += corners[k]
        return carry

    lax.fori_loop(0, batches, one_batch, 0)
    per_owner = tiles // groups * 8
    probe_sum = in_ref[0, groups * 8 : groups * 8 + p_rows, :]
    for b in range(1, batches):
        probe_sum = probe_sum + in_ref[b, groups * 8 : groups * 8 + p_rows, :]
    for o in range(groups):
        rows = slice(o * per_owner, (o + 1) * per_owner)
        summed = (acc[0, rows, :] + acc[1, rows, :]) + (acc[2, rows, :] + acc[3, rows, :])
        for copy in range(2):
            out_ref[copy * groups + o, :per_owner, :] = summed
            out_ref[copy * groups + o, per_owner:, :] = probe_sum


def reduce_positions(info, table, pieces, n, groups, tiles):
    p_rows = pieces.shape[1] - groups * 8 - 8
    whole = pl.BlockSpec(memory_space=pltpu.VMEM)
    smem = pl.BlockSpec(memory_space=pltpu.SMEM)
    return pl.pallas_call(
        partial(reduce_kernel, n, groups, p_rows),
        in_specs=[smem, smem, whole],
        out_specs=whole,
        out_shape=jax.ShapeDtypeStruct((2 * groups, tiles * 8 // groups + p_rows, LANES), F32),
        scratch_shapes=[pltpu.VMEM((4, tiles * 8, LANES), F32)],
        compiler_params=SMALL,
        name="reduce_positions",
    )(info, table, pieces)


def pack_kernel(p_rows, place_ref, in_ref, *out_refs):
    groups = in_ref.shape[0] // 2
    t_rows = in_ref.shape[1] - p_rows
    for h in range(2):
        for t in range(groups):
            for l in range(t_rows // 8):
                at = (l * groups + t) * 8
                out_refs[h][at : at + 8, :] = in_ref[h * groups + t, l * 8 : (l + 1) * 8, :]
        out_refs[h][groups * t_rows :, :] = in_ref[h * groups + place_ref[0], t_rows:, :]


def pack(place, pieces, p_rows):
    groups = pieces.shape[0] // 2
    rows = groups * (pieces.shape[1] - p_rows) + p_rows
    whole = pl.BlockSpec(memory_space=pltpu.VMEM)
    return pl.pallas_call(
        partial(pack_kernel, p_rows),
        in_specs=[pl.BlockSpec(memory_space=pltpu.SMEM), whole],
        out_specs=[whole, whole],
        out_shape=[jax.ShapeDtypeStruct((rows, LANES), F32)] * 2,
        compiler_params=SMALL,
        name="pack",
    )(place, pieces)


def update_kernel(probe_rate, p_rows, where_ref, tile_ref, probe_ref, *refs):
    batches = where_ref.shape[0] - 2
    grads = refs[:batches]
    new_tile_ref, new_probe_ref, held, held_probe, in_sems, out_sems, probe_sem = refs[batches:]
    count, _, n, _ = held.shape
    half, _, strip_rows, _ = held_probe.shape
    sides = n // LANES
    groups = n // strip_rows
    rows = groups * 8
    row_blocks = n // rows
    strips = strip_rows // p_rows
    arrivals, leavings = [], []
    for l in range(count):
        arrivals.append(pltpu.make_async_copy(tile_ref.at[l], held.at[l], in_sems.at[l]))
        leavings.append(pltpu.make_async_copy(held.at[l], new_tile_ref.at[l], out_sems.at[l]))
    cut, member = where_ref[batches], where_ref[batches + 1]
    at = pl.ds(pl.multiple_of(member * strip_rows, strip_rows), strip_rows)
    probe_copy = pltpu.make_async_copy(
        probe_ref.at[pl.ds(cut * half, half), :, at, :], held_probe, probe_sem
    )
    for copy in arrivals:
        copy.start()
    probe_copy.start()
    for l in range(count):
        arrivals[l].wait()
        for i in range(batches):
            batch = where_ref[i]
            panel = lax.div(batch, row_blocks)
            part, side = lax.div(panel, sides), lax.rem(panel, sides)
            at = pl.ds(pl.multiple_of(lax.rem(batch, row_blocks) * rows, rows), rows)
            lanes = pl.ds(pl.multiple_of(side * LANES, LANES), LANES)
            held[l, part, at, lanes] = (
                held[l, part, at, lanes] - OBJECT_RATE * grads[i][l * rows : (l + 1) * rows, :]
            )
        leavings[l].start()
    probe_copy.wait()
    for i in range(batches):
        batch = where_ref[i]
        panel = lax.div(batch, strips)
        field, side = lax.div(panel, sides), lax.rem(panel, sides)
        m, part = lax.div(field, 2), lax.rem(field, 2)
        at = pl.ds(pl.multiple_of(lax.rem(batch, strips) * p_rows, p_rows), p_rows)
        lanes = pl.ds(pl.multiple_of(side * LANES, LANES), LANES)
        new_probe_ref[m, part, at, lanes] = (
            held_probe[m, part, at, lanes] - probe_rate * grads[i][count * rows :, :]
        )
    for copy in leavings:
        copy.wait()


def update(where, tiles, probe, chunks, groups, p_rows, probe_rate):
    count, _, n, _ = tiles.shape
    probe_shape = (probe.shape[0] // 2, 2, n // groups, n)
    return pl.pallas_call(
        partial(update_kernel, probe_rate, p_rows),
        in_specs=[SMEM, HBM, HBM] + [VMEM] * len(chunks),
        out_specs=[HBM, VMEM],
        out_shape=[jax.ShapeDtypeStruct(tiles.shape, F32), jax.ShapeDtypeStruct(probe_shape, F32)],
        scratch_shapes=[
            pltpu.VMEM(tiles.shape, F32),
            pltpu.VMEM(probe_shape, F32),
            pltpu.SemaphoreType.DMA((count,)),
            pltpu.SemaphoreType.DMA((count,)),
            pltpu.SemaphoreType.DMA,
        ],
        compiler_params=SMALL,
        name="update",
    )(where, in_hbm(tiles), in_hbm(probe), *map(in_vmem, chunks))


def local(objects, probe, measured, send_list, corner_slot, offsets):
    n = probe.shape[-1]
    half = probe.shape[0] // 2
    groups = lax.axis_size("tile")
    batches = lax.axis_size("batch")
    z_size = batches // 2
    cut = lax.axis_index("cuts")
    member = lax.axis_index("tile")
    batch = lax.axis_index("batch")
    tiles = objects[0]
    tile_count = tiles.shape[0]
    info = jnp.concatenate(
        [
            corner_slot.reshape(-1),
            offsets.reshape(-1),
            jnp.stack([cut, batch * groups + member]).astype(jnp.int32),
        ]
    )
    meta_row = jnp.concatenate(
        [send_list.reshape(-1), corner_slot.reshape(-1), offsets.reshape(-1)]
    ).astype(F32)
    meta = jnp.zeros((8, LANES), F32).at[0, : meta_row.shape[0]].set(meta_row)

    with jax.named_scope("fetch_tiles"):
        ids = jnp.stack([cut, batch, member]).astype(jnp.int32)
        note = jnp.concatenate([corner_slot, offsets], axis=1)
        ready = (roll_probe(offsets, probe), info, meta)
        own, (rolled, info, meta) = fetch(ids, tiles, send_list, note, ready)
        other = lax.ppermute(own, "cuts", [(0, 1), (1, 0)])
    with jax.named_scope("waves"):
        pieces = wave_terms(info, own, other, rolled, measured, meta, groups)
    with jax.named_scope("return_terms"):
        pieces = lax.all_to_all(pieces, "tile", split_axis=0, concat_axis=0, tiled=True)
        pieces = regroup(pieces, batches)
        pieces = lax.all_to_all(pieces, "batch", split_axis=0, concat_axis=0, tiled=True)
        last = pieces.shape[1] - 8
        notes = pieces[:, last:, : meta_row.shape[0]].astype(jnp.int32)
        lists, slots, starts = notes[..., :groups], notes[..., groups : groups + 4], notes[..., groups + 4 :]
        owners = jnp.arange(groups, dtype=jnp.int32)
        chosen = slots[:, None, :, :] == owners[None, :, None, None]
        sent = jnp.sum(jnp.where(chosen, lists[:, :, :, None], 0), axis=1)
        table = jnp.concatenate(
            [slots * tile_count + sent, starts, jnp.zeros_like(starts)], axis=-1
        ).reshape(-1)
        p_rows = last - groups * 8
        summed = reduce_positions(info, table, pieces, n, groups, groups * tile_count)
        planes = [
            [(z * 2 + h) * groups + t for h in range(2) for t in range(groups)]
            for z in range(z_size)
        ]
        summed = lax.all_to_all(
            summed, ("batch", "tile"), split_axis=0, concat_axis=0, axis_index_groups=planes, tiled=True
        )
        packed = pack(member.reshape(1).astype(jnp.int32), summed, p_rows)
    with jax.named_scope("spread_sums"):
        onward = [(i, (i + 2) % batches) for i in range(batches)]
        backward = [(i, (i - 2) % batches) for i in range(batches)]
        z = batch // 2
        rate = PROBE_RATE / math.sqrt(batches * groups * measured.shape[0])
        found = []
        ahead = [packed[0], packed[1]]
        behind = [packed[0], packed[1]]
        for h in range(2):
            found.append((z, h, packed[h]))
        for step in range(1, z_size // 2 + 1):
            final = step == z_size // 2
            for h in range(2):
                if not (final and h == 1):
                    ahead[h] = lax.ppermute(ahead[h], "batch", onward)
                    found.append((z - step, h, ahead[h]))
                if not (final and h == 0):
                    behind[h] = lax.ppermute(behind[h], "batch", backward)
                    found.append((z + step, h, behind[h]))
        places = [lax.rem(place + z_size, z_size) * 2 + h for place, h, _ in found]
        where = jnp.stack(places + [cut, member]).astype(jnp.int32)
        new_tiles, new_probe = update(
            where, tiles, probe, [chunk for _, _, chunk in found], groups, p_rows, rate
        )
    return (new_tiles[None], new_probe)


def solution(mesh):
    in_specs = (
        P("cuts", "tile", None, None, None),
        P(),
        P(("batch", "tile"), None, None),
        P("batch", "tile", None),
        P(("batch", "tile"), None),
        P(("batch", "tile"), None),
    )
    out_specs = (P("cuts", "tile", None, None, None), P("cuts", None, "tile", None))
    return jax.shard_map(local, mesh=mesh, in_specs=in_specs, out_specs=out_specs, check_vma=False)
```

```python
from functools import partial
import math

import jax
import jax.numpy as jnp
from jax import lax
from jax.experimental import pallas as pl
from jax.experimental.pallas import tpu as pltpu
from jax.sharding import PartitionSpec as P
import ml_dtypes
import numpy as np

OBJECT_RATE = 0.02
PROBE_RATE = 0.05
LANES = 128
BIG = pltpu.CompilerParams(vmem_limit_bytes=32 * 1024 * 1024)
SMALL = pltpu.CompilerParams(vmem_limit_bytes=14 * 1024 * 1024)
F32 = jnp.float32
BF16 = jnp.bfloat16


def halves(matrix):
    upper = matrix.astype(ml_dtypes.bfloat16)
    lower = (matrix - upper.astype(np.float64)).astype(ml_dtypes.bfloat16)
    return upper, lower


def block_matrices(matrix):
    re, im = matrix.real, matrix.imag
    left = np.block([[re, -im], [im, re]])
    right = np.block([[re, im], [-im, re]])
    return halves(left) + halves(right)


def transform_tables(length):
    counter = np.arange(length)
    wave = np.exp(-2j * math.pi / length * (counter[:, None] * counter[None, :] % length))
    signed = np.where(counter < length // 2, counter, counter - length)
    chirp = np.exp(-1j * math.pi / length * (signed * signed % (2 * length)))
    fresnel = (np.conj(wave) * chirp[None, :]) @ wave / length
    return block_matrices(fresnel) + block_matrices(wave / math.sqrt(length))


def split(value):
    upper = value.astype(BF16)
    lower = (value - upper.astype(F32)).astype(BF16)
    return upper, lower


def dot(a, b):
    return jnp.dot(a, b, preferred_element_type=F32)


def two_sided(fields, left, right):
    n = fields[0][0].shape[0]
    parts = [jnp.concatenate([field[part] for field in fields], axis=1) for part in range(2)]
    upper, lower = split(jnp.concatenate(parts, axis=0))
    rows = dot(left[0][...], upper) + dot(left[0][...], lower) + dot(left[1][...], upper)
    stacked = [
        jnp.concatenate([rows[:n, i * n : (i + 1) * n], rows[n:, i * n : (i + 1) * n]], axis=1)
        for i in range(len(fields))
    ]
    upper, lower = split(jnp.concatenate(stacked, axis=0))
    both = dot(upper, right[0][...]) + dot(lower, right[0][...]) + dot(upper, right[1][...])
    return [
        (both[i * n : (i + 1) * n, :n], both[i * n : (i + 1) * n, n:]) for i in range(len(fields))
    ]


def times(a, b):
    return a[0] * b[0] - a[1] * b[1], a[0] * b[1] + a[1] * b[0]


def conj_times(a, b):
    return a[0] * b[0] + a[1] * b[1], a[0] * b[1] - a[1] * b[0]


SMEM = pl.BlockSpec(memory_space=pltpu.SMEM)
VMEM = pl.BlockSpec(memory_space=pltpu.VMEM)
HBM = pl.BlockSpec(memory_space=pltpu.HBM)


def in_hbm(value):
    return pltpu.with_memory_space_constraint(value, pltpu.HBM)


def pick_kernel(near, steps, ids_ref, list_ref, tile_ref, *refs):
    width = list_ref.shape[-1] // 2
    lower, column = lax.div(ids_ref[2], width), lax.rem(ids_ref[2], width)
    row = 1 - lower if near else lower
    sems = refs[-1]
    copies = []
    for i, step in enumerate(steps):
        member = row * width + lax.rem(column + step, width)
        copy = pltpu.make_async_copy(
            tile_ref.at[list_ref[0, 0, member]], refs[i], sems.at[i]
        )
        copy.start()
        copies.append(copy)
    for copy in copies:
        copy.wait()


def pick_tiles(ids, send_list, tiles, near, steps):
    return pl.pallas_call(
        partial(pick_kernel, near, steps),
        in_specs=[SMEM, SMEM, HBM],
        out_specs=[VMEM] * len(steps),
        out_shape=[jax.ShapeDtypeStruct(tiles.shape[1:], F32)] * len(steps),
        scratch_shapes=[pltpu.SemaphoreType.DMA((len(steps),))],
        compiler_params=SMALL,
        name="pick_tiles",
    )(ids, send_list, in_hbm(tiles))


def select_kernel(wanted, groups, ids_ref, *refs):
    steps = sorted({step for pieces in wanted for step, _, _ in pieces})
    notes = dict(zip(steps, refs))
    own = dict(zip(steps, refs[len(steps) :]))
    nears = dict(zip(steps, refs[2 * len(steps) :]))
    terms = refs[3 * len(steps) : len(refs) - len(wanted)]
    outs = refs[len(refs) - len(wanted) :]
    n = own[steps[0]].shape[-1]
    sides = n // LANES
    here = ids_ref[2]
    near = lax.rem(here + groups // 2, groups)
    for pieces, out_ref in zip(wanted, outs):
        for place, (step, part, added) in enumerate(pieces):
            note = notes[step]
            for side in range(sides):
                u = lax.broadcasted_iota(jnp.int32, (n, LANES), 0)
                v = lax.broadcasted_iota(jnp.int32, (n, LANES), 1) + side * LANES
                low, right = u < note[0, 4], v < note[0, 5]
                owner = jnp.where(
                    low,
                    jnp.where(right, note[0, 3], note[0, 2]),
                    jnp.where(right, note[0, 1], note[0, 0]),
                )
                lanes = slice(side * LANES, (side + 1) * LANES)
                value = jnp.where(
                    owner == here,
                    own[step][part, :, lanes],
                    jnp.where(owner == near, nears[step][part, :, lanes], 0.0),
                )
                for index in added:
                    value = value + terms[index][side * n : (side + 1) * n, :]
                at = (place * sides + side) * n
                out_ref[at : at + n, :] = value


def select_cells(ids, notes, own, nears, wanted, terms=()):
    n = own[0].shape[-1]
    rows = n * (n // LANES)
    steps = sorted({step for pieces in wanted for step, _, _ in pieces})
    return pl.pallas_call(
        partial(select_kernel, wanted, lax.axis_size("tile")),
        in_specs=[SMEM] * (1 + len(steps)) + [VMEM] * (2 * len(steps) + len(terms)),
        out_specs=[VMEM] * len(wanted),
        out_shape=[jax.ShapeDtypeStruct((rows * len(pieces), LANES), F32) for pieces in wanted],
        compiler_params=SMALL,
        name="select_cells",
    )(ids, *[group[step] for group in (notes, own, nears) for step in steps], *terms)


def fetch(ids, tiles, send_list, note, ready):
    groups = lax.axis_size("tile")
    batches = lax.axis_size("batch")
    width = groups // 2
    along = lambda d: [
        (y * width + x, y * width + (x + d) % width) for y in range(2) for x in range(width)
    ]
    send = lambda block, d: lax.ppermute(block, "tile", along(d))
    far_list = lax.ppermute(send_list, "batch", [(i, i ^ 1) for i in range(batches)])
    same = [(t, (t + width) % groups) for t in range(groups)]
    other = []
    for b in range(batches):
        for t in range(groups):
            y = (b % 2) * 2 + t // width
            step = (y + 1) % 4 if y % 2 == 1 else (y - 1) % 4
            other.append(
                (b * groups + t, (b // 2 * 2 + step // 2) * groups + step % 2 * width + t % width)
            )
    notes = {0: note}
    for d in range(1, width):
        notes[d] = send(note, -d)
    first = pick_tiles(ids, send_list, tiles, True, (2, 1))
    first, far_list = lax.optimization_barrier((first, far_list))
    second = pick_tiles(ids, far_list, tiles, True, (3, 0))
    nears = {2: lax.ppermute(first[0], "tile", same)}
    nears[3] = lax.ppermute(second[0], ("batch", "tile"), other)
    later, notes = lax.optimization_barrier(((first[1], second[1]), notes))
    nears[1] = lax.ppermute(later[0], "tile", same)
    nears[0] = lax.ppermute(later[1], ("batch", "tile"), other)
    own = pick_tiles(ids, send_list, tiles, False, (2, 1, 3, 0))
    notes, ready = lax.optimization_barrier((notes, ready))
    own = dict(zip((2, 1, 3, 0), own))
    select = lambda wanted, terms=(): select_cells(ids, notes, own, nears, wanted, terms)
    far_re, far_im = select([[(2, 0, ())], [(2, 1, ())]])
    far_re, far_im = send(far_re, 1), send(far_im, -1)
    up_im = send(select([[(1, 1, ())]])[0], 1)
    down_re = send(select([[(3, 0, ())]])[0], -1)
    up_re = send(select([[(1, 0, (0,))]], (far_re,))[0], 1)
    down_im = send(select([[(3, 1, (0,))]], (far_im,))[0], -1)
    patch = select([[(0, 0, (0, 1)), (0, 1, (2, 3))]], (up_re, down_re, up_im, down_im))[0]
    return patch, ready


def roll_kernel(start_ref, probe_ref, out_ref):
    for m in range(probe_ref.shape[0]):
        for part in range(2):
            value = pltpu.roll(probe_ref[m, part], start_ref[0, 0], 0)
            out_ref[m, part] = pltpu.roll(value, start_ref[0, 1], 1)


def roll_probe(offsets, probe):
    return pl.pallas_call(
        roll_kernel,
        in_specs=[SMEM, VMEM],
        out_specs=VMEM,
        out_shape=jax.ShapeDtypeStruct(probe.shape, F32),
        compiler_params=SMALL,
        name="roll_probe",
    )(offsets, probe)


def wave_kernel(
    info_ref, own_ref, other_ref, rolled, data_ref, meta_ref, table_ref,
    out_ref, spread, far, weight, total, q0, q1, tables, sems,
):
    copies = [
        pltpu.make_async_copy(table_ref.at[i], tables.at[i], sems.at[i])
        for i in range(tables.shape[0])
    ]
    for copy in copies:
        copy.start()
    n = data_ref.shape[-1]
    modes = rolled.shape[0]
    half = modes // 2
    sides = n // LANES
    groups = out_ref.shape[0]
    batches = 2 * sides * n // 8 // groups
    cut = info_ref[6]
    y_back, x_back = lax.rem(n - info_ref[4], n), lax.rem(n - info_ref[5], n)
    first = cut == 0
    prop_left, prop_right = (tables.at[0], tables.at[1]), (tables.at[2], tables.at[3])
    far_left, far_right = (tables.at[4], tables.at[5]), (tables.at[6], tables.at[7])
    for panel in range(2 * sides):
        part, side = panel // sides, panel % sides
        own = own_ref[panel * n : (panel + 1) * n, :]
        other = other_ref[panel * n : (panel + 1) * n, :]
        lanes = slice(side * LANES, (side + 1) * LANES)
        q0[part, :, lanes] = jnp.where(first, own, other)
        q1[part, :, lanes] = jnp.where(first, other, own)
    weight[...] = -data_ref[0]
    pairs = [range(i * half, (i + 1) * half) for i in range(2)]

    for place, pair in enumerate(pairs):
        if place == 0:
            for copy in copies[:4]:
                copy.wait()
        lit = [times((rolled[m, 0], rolled[m, 1]), (q0[0], q0[1])) for m in pair]
        waves = two_sided(lit, prop_left, prop_right)
        exits = []
        for m, wave in zip(pair, waves):
            spread[m, 0], spread[m, 1] = wave
            exits.append(times((q1[0], q1[1]), wave))
        if place == 0:
            for copy in copies[4:]:
                copy.wait()
        waves = two_sided(exits, far_left, far_right)
        power = jnp.zeros((n, n), F32)
        for m, wave in zip(pair, waves):
            far[m, 0], far[m, 1] = wave
            power = power + (wave[0] * wave[0] + wave[1] * wave[1])
        weight[...] += power

    total[...] = jnp.zeros_like(total)
    for place, pair in enumerate(pairs):
        weighted = [(weight[...] * far[m, 0], weight[...] * far[m, 1]) for m in pair]
        chis = two_sided(weighted, far_right, far_left)
        for m, chi in zip(pair, chis):
            far[m, 0], far[m, 1] = chi

        @pl.when(jnp.logical_not(first))
        def _():
            for m in pair:
                term = conj_times((spread[m, 0], spread[m, 1]), (far[m, 0], far[m, 1]))
                total[0] += term[0]
                total[1] += term[1]

        @pl.when(jnp.logical_or(first, place == 1))
        def _():
            backs = [conj_times((q1[0], q1[1]), (far[m, 0], far[m, 1])) for m in pair]
            zetas = two_sided(backs, prop_right, prop_left)

            @pl.when(first)
            def _():
                for m, zeta in zip(pair, zetas):
                    term = conj_times((rolled[m, 0], rolled[m, 1]), zeta)
                    total[0] += term[0]
                    total[1] += term[1]

            @pl.when(place == cut)
            def _():
                rows = n // groups
                for slot, zeta in enumerate(zetas):
                    parts = conj_times((q0[0], q0[1]), zeta)
                    for part in range(2):
                        term = pltpu.roll(pltpu.roll(parts[part], y_back, 0), x_back, 1)
                        for side in range(sides):
                            base = batches * 8 + ((slot * 2 + part) * sides + side) * rows
                            for t in range(groups):
                                out_ref[t, base : base + rows, :] = term[
                                    t * rows : (t + 1) * rows, side * LANES : (side + 1) * LANES
                                ]

    for j in range(2 * sides * n // 8):
        b, t = j // groups, j % groups
        panel, row = divmod(j * 8, n)
        part, side = panel // sides, panel % sides
        out_ref[t, b * 8 : (b + 1) * 8, :] = total[
            part, row : row + 8, side * LANES : (side + 1) * LANES
        ]
    rows = out_ref.shape[1]
    for t in range(groups):
        out_ref[t, rows - 8 : rows, :] = meta_ref[...]


def wave_terms(info, own, other, rolled, measured, meta, groups):
    n = rolled.shape[-1]
    modes = rolled.shape[0]
    tables = jnp.asarray(np.stack(transform_tables(n)))
    g_rows = 2 * n * n // LANES // groups
    rows = g_rows + modes * n * n // LANES // groups + 8
    return pl.pallas_call(
        wave_kernel,
        in_specs=[SMEM] + [VMEM] * 5 + [HBM],
        out_specs=VMEM,
        out_shape=jax.ShapeDtypeStruct((groups, rows, LANES), F32),
        scratch_shapes=[
            pltpu.VMEM((modes, 2, n, n), F32),
            pltpu.VMEM((modes, 2, n, n), F32),
            pltpu.VMEM((n, n), F32),
            pltpu.VMEM((2, n, n), F32),
            pltpu.VMEM((2, n, n), F32),
            pltpu.VMEM((2, n, n), F32),
            pltpu.VMEM(tables.shape, BF16),
            pltpu.SemaphoreType.DMA((tables.shape[0],)),
        ],
        compiler_params=BIG,
        name="wave_terms",
    )(info, own, other, rolled, measured, meta, in_hbm(tables))


def regroup_kernel(g_tiles, p_rows, in_ref, out_ref):
    groups = in_ref.shape[0]
    batches = out_ref.shape[0]
    last = in_ref.shape[1] - 8
    for b in range(batches):
        for t in range(groups):
            out_ref[b, t * 8 : (t + 1) * 8, :] = in_ref[t, b * 8 : (b + 1) * 8, :]
        base = g_tiles * 8 + b * p_rows
        term = in_ref[0, base : base + p_rows, :]
        for t in range(1, groups):
            term = term + in_ref[t, base : base + p_rows, :]
        out_ref[b, groups * 8 : groups * 8 + p_rows, :] = term
        for t in range(groups):
            row = groups * 8 + p_rows + t
            out_ref[b, row : row + 1, :] = in_ref[t, last : last + 1, :]


def regroup(pieces, batches):
    groups, rows, _ = pieces.shape
    p_rows = (rows - 8 - batches * 8) // batches
    whole = pl.BlockSpec(memory_space=pltpu.VMEM)
    return pl.pallas_call(
        partial(regroup_kernel, batches, p_rows),
        in_specs=[whole],
        out_specs=whole,
        out_shape=jax.ShapeDtypeStruct((batches, groups * 8 + p_rows + 8, LANES), F32),
        compiler_params=SMALL,
        name="regroup",
    )(pieces)


def reduce_kernel(n, groups, p_rows, info_ref, table_ref, in_ref, out_ref, acc):
    batches = in_ref.shape[0]
    tiles = acc.shape[1] // 8
    sides = n // LANES
    place = info_ref[7]
    panel, row = lax.div(place * 8, n), lax.rem(place * 8, n)
    u = lax.broadcasted_iota(jnp.int32, (8, LANES), 0) + row
    v = lax.broadcasted_iota(jnp.int32, (8, LANES), 1) + lax.rem(panel, sides) * LANES
    acc[...] = jnp.zeros_like(acc)

    def one_batch(b, carry):
        for t in range(groups):
            at = (b * groups + t) * 8
            value = in_ref[b, t * 8 : (t + 1) * 8, :]
            low, right = u < table_ref[at + 4], v < table_ref[at + 5]
            lower, upper = jnp.where(low, value, 0.0), jnp.where(low, 0.0, value)
            corners = (
                jnp.where(right, 0.0, upper),
                jnp.where(right, upper, 0.0),
                jnp.where(right, 0.0, lower),
                jnp.where(right, lower, 0.0),
            )
            for k in range(4):
                where = pl.ds(pl.multiple_of(table_ref[at + k] * 8, 8), 8)
                acc[k, where, :] += corners[k]
        return carry

    lax.fori_loop(0, batches, one_batch, 0)
    per_owner = tiles // groups * 8
    probe_sum = in_ref[0, groups * 8 : groups * 8 + p_rows, :]
    for b in range(1, batches):
        probe_sum = probe_sum + in_ref[b, groups * 8 : groups * 8 + p_rows, :]
    for o in range(groups):
        rows = slice(o * per_owner, (o + 1) * per_owner)
        summed = (acc[0, rows, :] + acc[1, rows, :]) + (acc[2, rows, :] + acc[3, rows, :])
        for copy in range(2):
            out_ref[copy * groups + o, :per_owner, :] = summed
            out_ref[copy * groups + o, per_owner:, :] = probe_sum


def reduce_positions(info, table, pieces, n, groups, tiles):
    p_rows = pieces.shape[1] - groups * 8 - 8
    whole = pl.BlockSpec(memory_space=pltpu.VMEM)
    smem = pl.BlockSpec(memory_space=pltpu.SMEM)
    return pl.pallas_call(
        partial(reduce_kernel, n, groups, p_rows),
        in_specs=[smem, smem, whole],
        out_specs=whole,
        out_shape=jax.ShapeDtypeStruct((2 * groups, tiles * 8 // groups + p_rows, LANES), F32),
        scratch_shapes=[pltpu.VMEM((4, tiles * 8, LANES), F32)],
        compiler_params=SMALL,
        name="reduce_positions",
    )(info, table, pieces)


def pack_kernel(p_rows, place_ref, in_ref, *out_refs):
    groups = in_ref.shape[0] // 2
    t_rows = in_ref.shape[1] - p_rows
    for h in range(2):
        for t in range(groups):
            for l in range(t_rows // 8):
                at = (l * groups + t) * 8
                out_refs[h][at : at + 8, :] = in_ref[h * groups + t, l * 8 : (l + 1) * 8, :]
        out_refs[h][groups * t_rows :, :] = in_ref[h * groups + place_ref[0], t_rows:, :]


def pack(place, pieces, p_rows):
    groups = pieces.shape[0] // 2
    rows = groups * (pieces.shape[1] - p_rows) + p_rows
    whole = pl.BlockSpec(memory_space=pltpu.VMEM)
    return pl.pallas_call(
        partial(pack_kernel, p_rows),
        in_specs=[pl.BlockSpec(memory_space=pltpu.SMEM), whole],
        out_specs=[whole, whole],
        out_shape=[jax.ShapeDtypeStruct((rows, LANES), F32)] * 2,
        compiler_params=SMALL,
        name="pack",
    )(place, pieces)


def update_kernel(probe_rate, p_rows, where_ref, tile_ref, probe_ref, *refs):
    batches = where_ref.shape[0] - 2
    grads, probe_grads = refs[:batches], refs[batches : 2 * batches]
    new_tile_ref, new_probe_ref = refs[2 * batches :]
    n = tile_ref.shape[-1]
    strip_rows = new_probe_ref.shape[2]
    sides = n // LANES
    groups = n // strip_rows
    rows = groups * 8
    row_blocks = n // rows
    strips = strip_rows // p_rows
    for i in range(batches):
        batch = where_ref[i]
        panel = lax.div(batch, row_blocks)
        part, side = lax.div(panel, sides), lax.rem(panel, sides)
        at = pl.ds(pl.multiple_of(lax.rem(batch, row_blocks) * rows, rows), rows)
        lanes = pl.ds(pl.multiple_of(side * LANES, LANES), LANES)
        new_tile_ref[0, part, at, lanes] = (
            tile_ref[0, part, at, lanes] - OBJECT_RATE * grads[i][...]
        )

    @pl.when(pl.program_id(0) == 0)
    def _():
        for i in range(batches):
            batch = where_ref[i]
            panel = lax.div(batch, strips)
            field, side = lax.div(panel, sides), lax.rem(panel, sides)
            m, part = lax.div(field, 2), lax.rem(field, 2)
            at = pl.ds(pl.multiple_of(lax.rem(batch, strips) * p_rows, p_rows), p_rows)
            lanes = pl.ds(pl.multiple_of(side * LANES, LANES), LANES)
            new_probe_ref[m, part, at, lanes] = (
                probe_ref[m, part, at, lanes] - probe_rate * probe_grads[i][...]
            )


def update(where, tiles, probe, chunks, groups, p_rows, probe_rate):
    count, _, n, _ = tiles.shape
    batches = len(chunks)
    probe_shape = (probe.shape[0] // 2, 2, n // groups, n)
    tile_spec = pl.BlockSpec((1, 2, n, n), lambda i, w: (i, 0, 0, 0))
    last = chunks[0].shape[0] // p_rows - 1
    return pl.pallas_call(
        partial(update_kernel, probe_rate, p_rows),
        grid_spec=pltpu.PrefetchScalarGridSpec(
            num_scalar_prefetch=1,
            grid=(count,),
            in_specs=[
                tile_spec,
                pl.BlockSpec(probe_shape, lambda i, w: (w[batches], 0, w[batches + 1], 0)),
            ]
            + [pl.BlockSpec((groups * 8, LANES), lambda i, w: (i, 0))] * batches
            + [pl.BlockSpec((p_rows, LANES), lambda i, w: (last, 0))] * batches,
            out_specs=[tile_spec, pl.BlockSpec(probe_shape, lambda i, w: (0, 0, 0, 0))],
        ),
        out_shape=[jax.ShapeDtypeStruct(tiles.shape, F32), jax.ShapeDtypeStruct(probe_shape, F32)],
        compiler_params=SMALL,
        name="update",
    )(where, in_hbm(tiles), in_hbm(probe), *chunks, *chunks)


def local(objects, probe, measured, send_list, corner_slot, offsets):
    n = probe.shape[-1]
    half = probe.shape[0] // 2
    groups = lax.axis_size("tile")
    batches = lax.axis_size("batch")
    z_size = batches // 2
    cut = lax.axis_index("cuts")
    member = lax.axis_index("tile")
    batch = lax.axis_index("batch")
    tiles = objects[0]
    tile_count = tiles.shape[0]
    info = jnp.concatenate(
        [
            corner_slot.reshape(-1),
            offsets.reshape(-1),
            jnp.stack([cut, batch * groups + member]).astype(jnp.int32),
        ]
    )
    meta_row = jnp.concatenate(
        [send_list.reshape(-1), corner_slot.reshape(-1), offsets.reshape(-1)]
    ).astype(F32)
    meta = jnp.zeros((8, LANES), F32).at[0, : meta_row.shape[0]].set(meta_row)

    with jax.named_scope("fetch_tiles"):
        ids = jnp.stack([cut, batch, member]).astype(jnp.int32)
        note = jnp.concatenate([corner_slot, offsets], axis=1)
        ready = (roll_probe(offsets, probe), info, meta)
        own, (rolled, info, meta) = fetch(ids, tiles, send_list, note, ready)
        other = lax.ppermute(own, "cuts", [(0, 1), (1, 0)])
    with jax.named_scope("waves"):
        pieces = wave_terms(info, own, other, rolled, measured, meta, groups)
    with jax.named_scope("return_terms"):
        pieces = lax.all_to_all(pieces, "tile", split_axis=0, concat_axis=0, tiled=True)
        pieces = regroup(pieces, batches)
        pieces = lax.all_to_all(pieces, "batch", split_axis=0, concat_axis=0, tiled=True)
        last = pieces.shape[1] - 8
        notes = pieces[:, last:, : meta_row.shape[0]].astype(jnp.int32)
        lists, slots, starts = notes[..., :groups], notes[..., groups : groups + 4], notes[..., groups + 4 :]
        owners = jnp.arange(groups, dtype=jnp.int32)
        chosen = slots[:, None, :, :] == owners[None, :, None, None]
        sent = jnp.sum(jnp.where(chosen, lists[:, :, :, None], 0), axis=1)
        table = jnp.concatenate(
            [slots * tile_count + sent, starts, jnp.zeros_like(starts)], axis=-1
        ).reshape(-1)
        p_rows = last - groups * 8
        summed = reduce_positions(info, table, pieces, n, groups, groups * tile_count)
        planes = [
            [(z * 2 + h) * groups + t for h in range(2) for t in range(groups)]
            for z in range(z_size)
        ]
        summed = lax.all_to_all(
            summed, ("batch", "tile"), split_axis=0, concat_axis=0, axis_index_groups=planes, tiled=True
        )
        packed = pack(member.reshape(1).astype(jnp.int32), summed, p_rows)
    with jax.named_scope("spread_sums"):
        onward = [(i, (i + 2) % batches) for i in range(batches)]
        backward = [(i, (i - 2) % batches) for i in range(batches)]
        z = batch // 2
        rate = PROBE_RATE / math.sqrt(batches * groups * measured.shape[0])
        found = []
        ahead = [packed[0], packed[1]]
        behind = [packed[0], packed[1]]
        for h in range(2):
            found.append((z, h, packed[h]))
        for step in range(1, z_size // 2 + 1):
            final = step == z_size // 2
            for h in range(2):
                if not (final and h == 1):
                    ahead[h] = lax.ppermute(ahead[h], "batch", onward)
                    found.append((z - step, h, ahead[h]))
                if not (final and h == 0):
                    behind[h] = lax.ppermute(behind[h], "batch", backward)
                    found.append((z + step, h, behind[h]))
        places = [lax.rem(place + z_size, z_size) * 2 + h for place, h, _ in found]
        where = jnp.stack(places + [cut, member]).astype(jnp.int32)
        new_tiles, new_probe = update(
            where, tiles, probe, [chunk for _, _, chunk in found], groups, p_rows, rate
        )
    return (new_tiles[None], new_probe)


def solution(mesh):
    in_specs = (
        P("cuts", "tile", None, None, None),
        P(),
        P(("batch", "tile"), None, None),
        P("batch", "tile", None),
        P(("batch", "tile"), None),
        P(("batch", "tile"), None),
    )
    out_specs = (P("cuts", "tile", None, None, None), P("cuts", None, "tile", None))
    return jax.shard_map(local, mesh=mesh, in_specs=in_specs, out_specs=out_specs, check_vma=False)
```

```python
from functools import partial
import math

import jax
import jax.numpy as jnp
from jax import lax
from jax.experimental import pallas as pl
from jax.experimental.pallas import tpu as pltpu
from jax.sharding import PartitionSpec as P
import ml_dtypes
import numpy as np

OBJECT_RATE = 0.02
PROBE_RATE = 0.05
LANES = 128
BIG = pltpu.CompilerParams(vmem_limit_bytes=32 * 1024 * 1024)
SMALL = pltpu.CompilerParams(vmem_limit_bytes=14 * 1024 * 1024)
F32 = jnp.float32
BF16 = jnp.bfloat16


def halves(matrix):
    upper = matrix.astype(ml_dtypes.bfloat16)
    lower = (matrix - upper.astype(np.float64)).astype(ml_dtypes.bfloat16)
    return upper, lower


def block_matrices(matrix):
    re, im = matrix.real, matrix.imag
    left = np.block([[re, -im], [im, re]])
    right = np.block([[re, im], [-im, re]])
    return halves(left) + halves(right)


def transform_tables(length):
    counter = np.arange(length)
    wave = np.exp(-2j * math.pi / length * (counter[:, None] * counter[None, :] % length))
    signed = np.where(counter < length // 2, counter, counter - length)
    chirp = np.exp(-1j * math.pi / length * (signed * signed % (2 * length)))
    fresnel = (np.conj(wave) * chirp[None, :]) @ wave / length
    return block_matrices(fresnel) + block_matrices(wave / math.sqrt(length))


def split(value):
    upper = value.astype(BF16)
    lower = (value - upper.astype(F32)).astype(BF16)
    return upper, lower


def dot(a, b):
    return jnp.dot(a, b, preferred_element_type=F32)


def two_sided(fields, left, right):
    n = fields[0][0].shape[0]
    parts = [jnp.concatenate([field[part] for field in fields], axis=1) for part in range(2)]
    upper, lower = split(jnp.concatenate(parts, axis=0))
    rows = dot(left[0][...], upper) + dot(left[0][...], lower) + dot(left[1][...], upper)
    stacked = [
        jnp.concatenate([rows[:n, i * n : (i + 1) * n], rows[n:, i * n : (i + 1) * n]], axis=1)
        for i in range(len(fields))
    ]
    upper, lower = split(jnp.concatenate(stacked, axis=0))
    both = dot(upper, right[0][...]) + dot(lower, right[0][...]) + dot(upper, right[1][...])
    return [
        (both[i * n : (i + 1) * n, :n], both[i * n : (i + 1) * n, n:]) for i in range(len(fields))
    ]


def times(a, b):
    return a[0] * b[0] - a[1] * b[1], a[0] * b[1] + a[1] * b[0]


def conj_times(a, b):
    return a[0] * b[0] + a[1] * b[1], a[0] * b[1] - a[1] * b[0]


SMEM = pl.BlockSpec(memory_space=pltpu.SMEM)
VMEM = pl.BlockSpec(memory_space=pltpu.VMEM)


def in_hbm(value):
    return pltpu.with_memory_space_constraint(value, pltpu.HBM)


def pick_kernel(ids_ref, list_ref, *refs):
    count = len(refs) // 2
    for i in range(count):
        refs[count + i][...] = refs[i][0]


def pick_tiles(ids, send_list, tiles, near, steps):
    width = send_list.shape[-1] // 2

    def picked(step):
        def index(i, ids, lists):
            lower, column = lax.div(ids[2], width), lax.rem(ids[2], width)
            row = 1 - lower if near else lower
            return (lists[0, 0, row * width + lax.rem(column + step, width)], 0, 0, 0)

        return pl.BlockSpec((1,) + tiles.shape[1:], index)

    return pl.pallas_call(
        pick_kernel,
        grid_spec=pltpu.PrefetchScalarGridSpec(
            num_scalar_prefetch=2,
            grid=(1,),
            in_specs=[picked(step) for step in steps],
            out_specs=[VMEM] * len(steps),
        ),
        out_shape=[jax.ShapeDtypeStruct(tiles.shape[1:], F32)] * len(steps),
        compiler_params=SMALL,
        name="pick_tiles",
    )(ids, send_list, *[in_hbm(tiles)] * len(steps))


def select_kernel(wanted, groups, ids_ref, *refs):
    steps = sorted({step for pieces in wanted for step, _, _ in pieces})
    notes = dict(zip(steps, refs))
    own = dict(zip(steps, refs[len(steps) :]))
    nears = dict(zip(steps, refs[2 * len(steps) :]))
    terms = refs[3 * len(steps) : len(refs) - len(wanted)]
    outs = refs[len(refs) - len(wanted) :]
    n = own[steps[0]].shape[-1]
    sides = n // LANES
    here = ids_ref[2]
    near = lax.rem(here + groups // 2, groups)
    for pieces, out_ref in zip(wanted, outs):
        for place, (step, part, added) in enumerate(pieces):
            note = notes[step]
            for side in range(sides):
                u = lax.broadcasted_iota(jnp.int32, (n, LANES), 0)
                v = lax.broadcasted_iota(jnp.int32, (n, LANES), 1) + side * LANES
                low, right = u < note[0, 4], v < note[0, 5]
                owner = jnp.where(
                    low,
                    jnp.where(right, note[0, 3], note[0, 2]),
                    jnp.where(right, note[0, 1], note[0, 0]),
                )
                lanes = slice(side * LANES, (side + 1) * LANES)
                value = jnp.where(
                    owner == here,
                    own[step][part, :, lanes],
                    jnp.where(owner == near, nears[step][part, :, lanes], 0.0),
                )
                for index in added:
                    value = value + terms[index][side * n : (side + 1) * n, :]
                at = (place * sides + side) * n
                out_ref[at : at + n, :] = value


def select_cells(ids, notes, own, nears, wanted, terms=()):
    n = own[0].shape[-1]
    rows = n * (n // LANES)
    steps = sorted({step for pieces in wanted for step, _, _ in pieces})
    return pl.pallas_call(
        partial(select_kernel, wanted, lax.axis_size("tile")),
        in_specs=[SMEM] * (1 + len(steps)) + [VMEM] * (2 * len(steps) + len(terms)),
        out_specs=[VMEM] * len(wanted),
        out_shape=[jax.ShapeDtypeStruct((rows * len(pieces), LANES), F32) for pieces in wanted],
        compiler_params=SMALL,
        name="select_cells",
    )(ids, *[group[step] for group in (notes, own, nears) for step in steps], *terms)


def fetch(ids, tiles, send_list, note, ready):
    groups = lax.axis_size("tile")
    batches = lax.axis_size("batch")
    width = groups // 2
    along = lambda d: [
        (y * width + x, y * width + (x + d) % width) for y in range(2) for x in range(width)
    ]
    send = lambda block, d: lax.ppermute(block, "tile", along(d))
    far_list = lax.ppermute(send_list, "batch", [(i, i ^ 1) for i in range(batches)])
    same = [(t, (t + width) % groups) for t in range(groups)]
    other = []
    for b in range(batches):
        for t in range(groups):
            y = (b % 2) * 2 + t // width
            step = (y + 1) % 4 if y % 2 == 1 else (y - 1) % 4
            other.append(
                (b * groups + t, (b // 2 * 2 + step // 2) * groups + step % 2 * width + t % width)
            )
    notes = {0: note}
    for d in range(1, width):
        notes[d] = send(note, -d)
    first = pick_tiles(ids, send_list, tiles, True, (2, 1))
    first, far_list = lax.optimization_barrier((first, far_list))
    second = pick_tiles(ids, far_list, tiles, True, (3, 0))
    nears = {2: lax.ppermute(first[0], "tile", same)}
    nears[3] = lax.ppermute(second[0], ("batch", "tile"), other)
    later, notes = lax.optimization_barrier(((first[1], second[1]), notes))
    nears[1] = lax.ppermute(later[0], "tile", same)
    nears[0] = lax.ppermute(later[1], ("batch", "tile"), other)
    own = pick_tiles(ids, send_list, tiles, False, (2, 1, 3, 0))
    notes, ready = lax.optimization_barrier((notes, ready))
    own = dict(zip((2, 1, 3, 0), own))
    select = lambda wanted, terms=(): select_cells(ids, notes, own, nears, wanted, terms)
    far_re, far_im = select([[(2, 0, ())], [(2, 1, ())]])
    far_re, far_im = send(far_re, 1), send(far_im, -1)
    up_im = send(select([[(1, 1, ())]])[0], 1)
    down_re = send(select([[(3, 0, ())]])[0], -1)
    up_re = send(select([[(1, 0, (0,))]], (far_re,))[0], 1)
    down_im = send(select([[(3, 1, (0,))]], (far_im,))[0], -1)
    patch = select([[(0, 0, (0, 1)), (0, 1, (2, 3))]], (up_re, down_re, up_im, down_im))[0]
    return patch, ready


def roll_kernel(start_ref, probe_ref, out_ref):
    for m in range(probe_ref.shape[0]):
        for part in range(2):
            value = pltpu.roll(probe_ref[m, part], start_ref[0, 0], 0)
            out_ref[m, part] = pltpu.roll(value, start_ref[0, 1], 1)


def roll_probe(offsets, probe):
    return pl.pallas_call(
        roll_kernel,
        in_specs=[SMEM, VMEM],
        out_specs=VMEM,
        out_shape=jax.ShapeDtypeStruct(probe.shape, F32),
        compiler_params=SMALL,
        name="roll_probe",
    )(offsets, probe)


def wave_kernel(
    info_ref, own_ref, other_ref, rolled, data_ref, meta_ref, tables,
    out_ref, spread, far, weight, total, q0, q1,
):
    n = data_ref.shape[-1]
    modes = rolled.shape[0]
    half = modes // 2
    sides = n // LANES
    groups = out_ref.shape[0]
    batches = 2 * sides * n // 8 // groups
    cut = info_ref[6]
    y_back, x_back = lax.rem(n - info_ref[4], n), lax.rem(n - info_ref[5], n)
    first = cut == 0
    prop_left, prop_right = (tables.at[0], tables.at[1]), (tables.at[2], tables.at[3])
    far_left, far_right = (tables.at[4], tables.at[5]), (tables.at[6], tables.at[7])
    for panel in range(2 * sides):
        part, side = panel // sides, panel % sides
        own = own_ref[panel * n : (panel + 1) * n, :]
        other = other_ref[panel * n : (panel + 1) * n, :]
        lanes = slice(side * LANES, (side + 1) * LANES)
        q0[part, :, lanes] = jnp.where(first, own, other)
        q1[part, :, lanes] = jnp.where(first, other, own)
    weight[...] = -data_ref[0]
    pairs = [range(i * half, (i + 1) * half) for i in range(2)]

    for pair in pairs:
        lit = [times((rolled[m, 0], rolled[m, 1]), (q0[0], q0[1])) for m in pair]
        waves = two_sided(lit, prop_left, prop_right)
        exits = []
        for m, wave in zip(pair, waves):
            spread[m, 0], spread[m, 1] = wave
            exits.append(times((q1[0], q1[1]), wave))
        waves = two_sided(exits, far_left, far_right)
        power = jnp.zeros((n, n), F32)
        for m, wave in zip(pair, waves):
            far[m, 0], far[m, 1] = wave
            power = power + (wave[0] * wave[0] + wave[1] * wave[1])
        weight[...] += power

    total[...] = jnp.zeros_like(total)
    for place, pair in enumerate(pairs):
        weighted = [(weight[...] * far[m, 0], weight[...] * far[m, 1]) for m in pair]
        chis = two_sided(weighted, far_right, far_left)
        for m, chi in zip(pair, chis):
            far[m, 0], far[m, 1] = chi

        @pl.when(jnp.logical_not(first))
        def _():
            for m in pair:
                term = conj_times((spread[m, 0], spread[m, 1]), (far[m, 0], far[m, 1]))
                total[0] += term[0]
                total[1] += term[1]

        @pl.when(jnp.logical_or(first, place == 1))
        def _():
            backs = [conj_times((q1[0], q1[1]), (far[m, 0], far[m, 1])) for m in pair]
            zetas = two_sided(backs, prop_right, prop_left)

            @pl.when(first)
            def _():
                for m, zeta in zip(pair, zetas):
                    term = conj_times((rolled[m, 0], rolled[m, 1]), zeta)
                    total[0] += term[0]
                    total[1] += term[1]

            @pl.when(place == cut)
            def _():
                rows = n // groups
                for slot, zeta in enumerate(zetas):
                    parts = conj_times((q0[0], q0[1]), zeta)
                    for part in range(2):
                        term = pltpu.roll(pltpu.roll(parts[part], y_back, 0), x_back, 1)
                        for side in range(sides):
                            base = batches * 8 + ((slot * 2 + part) * sides + side) * rows
                            for t in range(groups):
                                out_ref[t, base : base + rows, :] = term[
                                    t * rows : (t + 1) * rows, side * LANES : (side + 1) * LANES
                                ]

    for j in range(2 * sides * n // 8):
        b, t = j // groups, j % groups
        panel, row = divmod(j * 8, n)
        part, side = panel // sides, panel % sides
        out_ref[t, b * 8 : (b + 1) * 8, :] = total[
            part, row : row + 8, side * LANES : (side + 1) * LANES
        ]
    rows = out_ref.shape[1]
    for t in range(groups):
        out_ref[t, rows - 8 : rows, :] = meta_ref[...]


def wave_terms(info, own, other, rolled, measured, meta, groups):
    n = rolled.shape[-1]
    modes = rolled.shape[0]
    tables = jnp.asarray(np.stack(transform_tables(n)))
    g_rows = 2 * n * n // LANES // groups
    rows = g_rows + modes * n * n // LANES // groups + 8
    return pl.pallas_call(
        wave_kernel,
        in_specs=[SMEM] + [VMEM] * 6,
        out_specs=VMEM,
        out_shape=jax.ShapeDtypeStruct((groups, rows, LANES), F32),
        scratch_shapes=[
            pltpu.VMEM((modes, 2, n, n), F32),
            pltpu.VMEM((modes, 2, n, n), F32),
            pltpu.VMEM((n, n), F32),
            pltpu.VMEM((2, n, n), F32),
            pltpu.VMEM((2, n, n), F32),
            pltpu.VMEM((2, n, n), F32),
        ],
        compiler_params=BIG,
        name="wave_terms",
    )(info, own, other, rolled, measured, meta, tables)


def regroup_kernel(g_tiles, p_rows, in_ref, out_ref):
    groups = in_ref.shape[0]
    batches = out_ref.shape[0]
    last = in_ref.shape[1] - 8
    for b in range(batches):
        for t in range(groups):
            out_ref[b, t * 8 : (t + 1) * 8, :] = in_ref[t, b * 8 : (b + 1) * 8, :]
        base = g_tiles * 8 + b * p_rows
        term = in_ref[0, base : base + p_rows, :]
        for t in range(1, groups):
            term = term + in_ref[t, base : base + p_rows, :]
        out_ref[b, groups * 8 : groups * 8 + p_rows, :] = term
        for t in range(groups):
            row = groups * 8 + p_rows + t
            out_ref[b, row : row + 1, :] = in_ref[t, last : last + 1, :]


def regroup(pieces, batches):
    groups, rows, _ = pieces.shape
    p_rows = (rows - 8 - batches * 8) // batches
    whole = pl.BlockSpec(memory_space=pltpu.VMEM)
    return pl.pallas_call(
        partial(regroup_kernel, batches, p_rows),
        in_specs=[whole],
        out_specs=whole,
        out_shape=jax.ShapeDtypeStruct((batches, groups * 8 + p_rows + 8, LANES), F32),
        compiler_params=SMALL,
        name="regroup",
    )(pieces)


def reduce_kernel(n, groups, p_rows, info_ref, table_ref, in_ref, out_ref, acc):
    batches = in_ref.shape[0]
    tiles = acc.shape[1] // 8
    sides = n // LANES
    place = info_ref[7]
    panel, row = lax.div(place * 8, n), lax.rem(place * 8, n)
    u = lax.broadcasted_iota(jnp.int32, (8, LANES), 0) + row
    v = lax.broadcasted_iota(jnp.int32, (8, LANES), 1) + lax.rem(panel, sides) * LANES
    acc[...] = jnp.zeros_like(acc)

    def one_batch(b, carry):
        for t in range(groups):
            at = (b * groups + t) * 8
            value = in_ref[b, t * 8 : (t + 1) * 8, :]
            low, right = u < table_ref[at + 4], v < table_ref[at + 5]
            lower, upper = jnp.where(low, value, 0.0), jnp.where(low, 0.0, value)
            corners = (
                jnp.where(right, 0.0, upper),
                jnp.where(right, upper, 0.0),
                jnp.where(right, 0.0, lower),
                jnp.where(right, lower, 0.0),
            )
            for k in range(4):
                where = pl.ds(pl.multiple_of(table_ref[at + k] * 8, 8), 8)
                acc[k, where, :] += corners[k]
        return carry

    lax.fori_loop(0, batches, one_batch, 0)
    per_owner = tiles // groups * 8
    probe_sum = in_ref[0, groups * 8 : groups * 8 + p_rows, :]
    for b in range(1, batches):
        probe_sum = probe_sum + in_ref[b, groups * 8 : groups * 8 + p_rows, :]
    for o in range(groups):
        rows = slice(o * per_owner, (o + 1) * per_owner)
        summed = (acc[0, rows, :] + acc[1, rows, :]) + (acc[2, rows, :] + acc[3, rows, :])
        for copy in range(2):
            out_ref[copy * groups + o, :per_owner, :] = summed
            out_ref[copy * groups + o, per_owner:, :] = probe_sum


def reduce_positions(info, table, pieces, n, groups, tiles):
    p_rows = pieces.shape[1] - groups * 8 - 8
    whole = pl.BlockSpec(memory_space=pltpu.VMEM)
    smem = pl.BlockSpec(memory_space=pltpu.SMEM)
    return pl.pallas_call(
        partial(reduce_kernel, n, groups, p_rows),
        in_specs=[smem, smem, whole],
        out_specs=whole,
        out_shape=jax.ShapeDtypeStruct((2 * groups, tiles * 8 // groups + p_rows, LANES), F32),
        scratch_shapes=[pltpu.VMEM((4, tiles * 8, LANES), F32)],
        compiler_params=SMALL,
        name="reduce_positions",
    )(info, table, pieces)


def pack_kernel(p_rows, place_ref, in_ref, *out_refs):
    groups = in_ref.shape[0] // 2
    t_rows = in_ref.shape[1] - p_rows
    for h in range(2):
        for t in range(groups):
            for l in range(t_rows // 8):
                at = (l * groups + t) * 8
                out_refs[h][at : at + 8, :] = in_ref[h * groups + t, l * 8 : (l + 1) * 8, :]
        out_refs[h][groups * t_rows :, :] = in_ref[h * groups + place_ref[0], t_rows:, :]


def pack(place, pieces, p_rows):
    groups = pieces.shape[0] // 2
    rows = groups * (pieces.shape[1] - p_rows) + p_rows
    whole = pl.BlockSpec(memory_space=pltpu.VMEM)
    return pl.pallas_call(
        partial(pack_kernel, p_rows),
        in_specs=[pl.BlockSpec(memory_space=pltpu.SMEM), whole],
        out_specs=[whole, whole],
        out_shape=[jax.ShapeDtypeStruct((rows, LANES), F32)] * 2,
        compiler_params=SMALL,
        name="pack",
    )(place, pieces)


def update_kernel(probe_rate, p_rows, where_ref, tile_ref, probe_ref, *refs):
    batches = where_ref.shape[0] - 2
    grads, probe_grads = refs[:batches], refs[batches : 2 * batches]
    new_tile_ref, new_probe_ref = refs[2 * batches :]
    n = tile_ref.shape[-1]
    strip_rows = new_probe_ref.shape[2]
    sides = n // LANES
    groups = n // strip_rows
    rows = groups * 8
    row_blocks = n // rows
    strips = strip_rows // p_rows
    for i in range(batches):
        batch = where_ref[i]
        panel = lax.div(batch, row_blocks)
        part, side = lax.div(panel, sides), lax.rem(panel, sides)
        at = pl.ds(pl.multiple_of(lax.rem(batch, row_blocks) * rows, rows), rows)
        lanes = pl.ds(pl.multiple_of(side * LANES, LANES), LANES)
        new_tile_ref[0, part, at, lanes] = (
            tile_ref[0, part, at, lanes] - OBJECT_RATE * grads[i][...]
        )

    @pl.when(pl.program_id(0) == 0)
    def _():
        for i in range(batches):
            batch = where_ref[i]
            panel = lax.div(batch, strips)
            field, side = lax.div(panel, sides), lax.rem(panel, sides)
            m, part = lax.div(field, 2), lax.rem(field, 2)
            at = pl.ds(pl.multiple_of(lax.rem(batch, strips) * p_rows, p_rows), p_rows)
            lanes = pl.ds(pl.multiple_of(side * LANES, LANES), LANES)
            new_probe_ref[m, part, at, lanes] = (
                probe_ref[m, part, at, lanes] - probe_rate * probe_grads[i][...]
            )


def update(where, tiles, probe, chunks, groups, p_rows, probe_rate):
    count, _, n, _ = tiles.shape
    batches = len(chunks)
    probe_shape = (probe.shape[0] // 2, 2, n // groups, n)
    tile_spec = pl.BlockSpec((1, 2, n, n), lambda i, w: (i, 0, 0, 0))
    last = chunks[0].shape[0] // p_rows - 1
    return pl.pallas_call(
        partial(update_kernel, probe_rate, p_rows),
        grid_spec=pltpu.PrefetchScalarGridSpec(
            num_scalar_prefetch=1,
            grid=(count,),
            in_specs=[
                tile_spec,
                pl.BlockSpec(probe_shape, lambda i, w: (w[batches], 0, w[batches + 1], 0)),
            ]
            + [pl.BlockSpec((groups * 8, LANES), lambda i, w: (i, 0))] * batches
            + [pl.BlockSpec((p_rows, LANES), lambda i, w: (last, 0))] * batches,
            out_specs=[tile_spec, pl.BlockSpec(probe_shape, lambda i, w: (0, 0, 0, 0))],
        ),
        out_shape=[jax.ShapeDtypeStruct(tiles.shape, F32), jax.ShapeDtypeStruct(probe_shape, F32)],
        compiler_params=SMALL,
        name="update",
    )(where, in_hbm(tiles), in_hbm(probe), *chunks, *chunks)


def local(objects, probe, measured, send_list, corner_slot, offsets):
    n = probe.shape[-1]
    half = probe.shape[0] // 2
    groups = lax.axis_size("tile")
    batches = lax.axis_size("batch")
    z_size = batches // 2
    cut = lax.axis_index("cuts")
    member = lax.axis_index("tile")
    batch = lax.axis_index("batch")
    tiles = objects[0]
    tile_count = tiles.shape[0]
    info = jnp.concatenate(
        [
            corner_slot.reshape(-1),
            offsets.reshape(-1),
            jnp.stack([cut, batch * groups + member]).astype(jnp.int32),
        ]
    )
    meta_row = jnp.concatenate(
        [send_list.reshape(-1), corner_slot.reshape(-1), offsets.reshape(-1)]
    ).astype(F32)
    meta = jnp.zeros((8, LANES), F32).at[0, : meta_row.shape[0]].set(meta_row)

    with jax.named_scope("fetch_tiles"):
        ids = jnp.stack([cut, batch, member]).astype(jnp.int32)
        note = jnp.concatenate([corner_slot, offsets], axis=1)
        ready = (roll_probe(offsets, probe), info, meta)
        own, (rolled, info, meta) = fetch(ids, tiles, send_list, note, ready)
        other = lax.ppermute(own, "cuts", [(0, 1), (1, 0)])
    with jax.named_scope("waves"):
        pieces = wave_terms(info, own, other, rolled, measured, meta, groups)
    with jax.named_scope("return_terms"):
        pieces = lax.all_to_all(pieces, "tile", split_axis=0, concat_axis=0, tiled=True)
        pieces = regroup(pieces, batches)
        pieces = lax.all_to_all(pieces, "batch", split_axis=0, concat_axis=0, tiled=True)
        last = pieces.shape[1] - 8
        notes = pieces[:, last:, : meta_row.shape[0]].astype(jnp.int32)
        lists, slots, starts = notes[..., :groups], notes[..., groups : groups + 4], notes[..., groups + 4 :]
        owners = jnp.arange(groups, dtype=jnp.int32)
        chosen = slots[:, None, :, :] == owners[None, :, None, None]
        sent = jnp.sum(jnp.where(chosen, lists[:, :, :, None], 0), axis=1)
        table = jnp.concatenate(
            [slots * tile_count + sent, starts, jnp.zeros_like(starts)], axis=-1
        ).reshape(-1)
        p_rows = last - groups * 8
        summed = reduce_positions(info, table, pieces, n, groups, groups * tile_count)
        planes = [
            [(z * 2 + h) * groups + t for h in range(2) for t in range(groups)]
            for z in range(z_size)
        ]
        summed = lax.all_to_all(
            summed, ("batch", "tile"), split_axis=0, concat_axis=0, axis_index_groups=planes, tiled=True
        )
        packed = pack(member.reshape(1).astype(jnp.int32), summed, p_rows)
    with jax.named_scope("spread_sums"):
        onward = [(i, (i + 2) % batches) for i in range(batches)]
        backward = [(i, (i - 2) % batches) for i in range(batches)]
        z = batch // 2
        rate = PROBE_RATE / math.sqrt(batches * groups * measured.shape[0])
        found = []
        ahead = [packed[0], packed[1]]
        behind = [packed[0], packed[1]]
        for h in range(2):
            found.append((z, h, packed[h]))
        for step in range(1, z_size // 2 + 1):
            final = step == z_size // 2
            for h in range(2):
                if not (final and h == 1):
                    ahead[h] = lax.ppermute(ahead[h], "batch", onward)
                    found.append((z - step, h, ahead[h]))
                if not (final and h == 0):
                    behind[h] = lax.ppermute(behind[h], "batch", backward)
                    found.append((z + step, h, behind[h]))
        places = [lax.rem(place + z_size, z_size) * 2 + h for place, h, _ in found]
        where = jnp.stack(places + [cut, member]).astype(jnp.int32)
        new_tiles, new_probe = update(
            where, tiles, probe, [chunk for _, _, chunk in found], groups, p_rows, rate
        )
    return (new_tiles[None], new_probe)


def solution(mesh):
    in_specs = (
        P("cuts", "tile", None, None, None),
        P(),
        P(("batch", "tile"), None, None),
        P("batch", "tile", None),
        P(("batch", "tile"), None),
        P(("batch", "tile"), None),
    )
    out_specs = (P("cuts", "tile", None, None, None), P("cuts", None, "tile", None))
    return jax.shard_map(local, mesh=mesh, in_specs=in_specs, out_specs=out_specs, check_vma=False)
```

```python
from functools import partial
import math

import jax
import jax.numpy as jnp
from jax import lax
from jax.experimental import pallas as pl
from jax.experimental.pallas import tpu as pltpu
from jax.sharding import PartitionSpec as P
import ml_dtypes
import numpy as np

OBJECT_RATE = 0.02
PROBE_RATE = 0.05
LANES = 128
BIG = pltpu.CompilerParams(vmem_limit_bytes=32 * 1024 * 1024)
SMALL = pltpu.CompilerParams(vmem_limit_bytes=14 * 1024 * 1024)
F32 = jnp.float32
BF16 = jnp.bfloat16


def halves(matrix):
    upper = matrix.astype(ml_dtypes.bfloat16)
    lower = (matrix - upper.astype(np.float64)).astype(ml_dtypes.bfloat16)
    return upper, lower


def matrix_parts(matrix):
    return halves(matrix.real) + halves(matrix.imag)


def transform_parts(length):
    counter = np.arange(length)
    wave = np.exp(-2j * math.pi / length * (counter[:, None] * counter[None, :] % length))
    signed = np.where(counter < length // 2, counter, counter - length)
    chirp = np.exp(-1j * math.pi / length * (signed * signed % (2 * length)))
    fresnel = (np.conj(wave) * chirp[None, :]) @ wave / length
    return np.stack(matrix_parts(fresnel) + matrix_parts(wave / math.sqrt(length)))


def split(value):
    upper = value.astype(BF16)
    lower = (value - upper.astype(F32)).astype(BF16)
    return upper, lower


def dot(a, b):
    return jnp.dot(a, b, preferred_element_type=F32)


def two_sided(fields, left, right):
    n = fields[0][0].shape[0]
    parts = [jnp.concatenate([field[part] for field in fields], axis=1) for part in range(2)]
    upper, lower = split(jnp.concatenate(parts, axis=0))
    rows = dot(left[0][...], upper) + dot(left[0][...], lower) + dot(left[1][...], upper)
    stacked = [
        jnp.concatenate([rows[:n, i * n : (i + 1) * n], rows[n:, i * n : (i + 1) * n]], axis=1)
        for i in range(len(fields))
    ]
    upper, lower = split(jnp.concatenate(stacked, axis=0))
    both = dot(upper, right[0][...]) + dot(lower, right[0][...]) + dot(upper, right[1][...])
    return [
        (both[i * n : (i + 1) * n, :n], both[i * n : (i + 1) * n, n:]) for i in range(len(fields))
    ]


def times(a, b):
    return a[0] * b[0] - a[1] * b[1], a[0] * b[1] + a[1] * b[0]


def conj_times(a, b):
    return a[0] * b[0] + a[1] * b[1], a[0] * b[1] - a[1] * b[0]


SMEM = pl.BlockSpec(memory_space=pltpu.SMEM)
VMEM = pl.BlockSpec(memory_space=pltpu.VMEM)
HBM = pl.BlockSpec(memory_space=pltpu.HBM)


def in_hbm(value):
    return pltpu.with_memory_space_constraint(value, pltpu.HBM)


def pick_kernel(ids_ref, list_ref, *refs):
    count = len(refs) // 2
    for i in range(count):
        refs[count + i][...] = refs[i][0]


def pick_tiles(ids, send_list, tiles, near, steps):
    width = send_list.shape[-1] // 2

    def picked(step):
        def index(i, ids, lists):
            lower, column = lax.div(ids[2], width), lax.rem(ids[2], width)
            row = 1 - lower if near else lower
            return (lists[0, 0, row * width + lax.rem(column + step, width)], 0, 0, 0)

        return pl.BlockSpec((1,) + tiles.shape[1:], index)

    return pl.pallas_call(
        pick_kernel,
        grid_spec=pltpu.PrefetchScalarGridSpec(
            num_scalar_prefetch=2,
            grid=(1,),
            in_specs=[picked(step) for step in steps],
            out_specs=[VMEM] * len(steps),
        ),
        out_shape=[jax.ShapeDtypeStruct(tiles.shape[1:], F32)] * len(steps),
        compiler_params=SMALL,
        name="pick_tiles",
    )(ids, send_list, *[in_hbm(tiles)] * len(steps))


def select_kernel(wanted, groups, ids_ref, *refs):
    steps = sorted({step for pieces in wanted for step, _, _ in pieces})
    notes = dict(zip(steps, refs))
    own = dict(zip(steps, refs[len(steps) :]))
    nears = dict(zip(steps, refs[2 * len(steps) :]))
    terms = refs[3 * len(steps) : len(refs) - len(wanted)]
    outs = refs[len(refs) - len(wanted) :]
    n = own[steps[0]].shape[-1]
    sides = n // LANES
    here = ids_ref[2]
    near = lax.rem(here + groups // 2, groups)
    for pieces, out_ref in zip(wanted, outs):
        for place, (step, part, added) in enumerate(pieces):
            note = notes[step]
            for side in range(sides):
                u = lax.broadcasted_iota(jnp.int32, (n, LANES), 0)
                v = lax.broadcasted_iota(jnp.int32, (n, LANES), 1) + side * LANES
                low, right = u < note[0, 4], v < note[0, 5]
                owner = jnp.where(
                    low,
                    jnp.where(right, note[0, 3], note[0, 2]),
                    jnp.where(right, note[0, 1], note[0, 0]),
                )
                lanes = slice(side * LANES, (side + 1) * LANES)
                value = jnp.where(
                    owner == here,
                    own[step][part, :, lanes],
                    jnp.where(owner == near, nears[step][part, :, lanes], 0.0),
                )
                for index in added:
                    value = value + terms[index][side * n : (side + 1) * n, :]
                at = (place * sides + side) * n
                out_ref[at : at + n, :] = value


def select_cells(ids, notes, own, nears, wanted, terms=()):
    n = own[0].shape[-1]
    rows = n * (n // LANES)
    steps = sorted({step for pieces in wanted for step, _, _ in pieces})
    return pl.pallas_call(
        partial(select_kernel, wanted, lax.axis_size("tile")),
        in_specs=[SMEM] * (1 + len(steps)) + [VMEM] * (2 * len(steps) + len(terms)),
        out_specs=[VMEM] * len(wanted),
        out_shape=[jax.ShapeDtypeStruct((rows * len(pieces), LANES), F32) for pieces in wanted],
        compiler_params=SMALL,
        name="select_cells",
    )(ids, *[group[step] for group in (notes, own, nears) for step in steps], *terms)


def fetch(ids, tiles, send_list, note, ready):
    groups = lax.axis_size("tile")
    batches = lax.axis_size("batch")
    width = groups // 2
    along = lambda d: [
        (y * width + x, y * width + (x + d) % width) for y in range(2) for x in range(width)
    ]
    send = lambda block, d: lax.ppermute(block, "tile", along(d))
    far_list = lax.ppermute(send_list, "batch", [(i, i ^ 1) for i in range(batches)])
    same = [(t, (t + width) % groups) for t in range(groups)]
    other = []
    for b in range(batches):
        for t in range(groups):
            y = (b % 2) * 2 + t // width
            step = (y + 1) % 4 if y % 2 == 1 else (y - 1) % 4
            other.append(
                (b * groups + t, (b // 2 * 2 + step // 2) * groups + step % 2 * width + t % width)
            )
    notes = {0: note}
    for d in range(1, width):
        notes[d] = send(note, -d)
    first = pick_tiles(ids, send_list, tiles, True, (2, 1))
    first, far_list = lax.optimization_barrier((first, far_list))
    second = pick_tiles(ids, far_list, tiles, True, (3, 0))
    nears = {2: lax.ppermute(first[0], "tile", same)}
    nears[3] = lax.ppermute(second[0], ("batch", "tile"), other)
    later, notes = lax.optimization_barrier(((first[1], second[1]), notes))
    nears[1] = lax.ppermute(later[0], "tile", same)
    nears[0] = lax.ppermute(later[1], ("batch", "tile"), other)
    own = pick_tiles(ids, send_list, tiles, False, (2, 1, 3, 0))
    notes, ready = lax.optimization_barrier((notes, ready))
    own = dict(zip((2, 1, 3, 0), own))
    select = lambda wanted, terms=(): select_cells(ids, notes, own, nears, wanted, terms)
    far_re, far_im = select([[(2, 0, ())], [(2, 1, ())]])
    far_re, far_im = send(far_re, 1), send(far_im, -1)
    up_im = send(select([[(1, 1, ())]])[0], 1)
    down_re = send(select([[(3, 0, ())]])[0], -1)
    up_re = send(select([[(1, 0, (0,))]], (far_re,))[0], 1)
    down_im = send(select([[(3, 1, (0,))]], (far_im,))[0], -1)
    patch = select([[(0, 0, (0, 1)), (0, 1, (2, 3))]], (up_re, down_re, up_im, down_im))[0]
    return patch, ready


def prepare_kernel(start_ref, probe_ref, part_ref, rolled_ref, table_ref):
    n = probe_ref.shape[-1]
    for m in range(probe_ref.shape[0]):
        for part in range(2):
            value = pltpu.roll(probe_ref[m, part], start_ref[0, 0], 0)
            rolled_ref[m, part] = pltpu.roll(value, start_ref[0, 1], 1)
    for transform in range(part_ref.shape[0] // 4):
        for low in range(2):
            re = part_ref[transform * 4 + low]
            im = part_ref[transform * 4 + 2 + low]
            left, right = transform * 4 + low, transform * 4 + 2 + low
            for table, upper_right, lower_left in ((left, -im, im), (right, im, -im)):
                table_ref[table, :n, :n] = re
                table_ref[table, n:, n:] = re
                table_ref[table, :n, n:] = upper_right
                table_ref[table, n:, :n] = lower_left


def prepare(offsets, probe):
    parts = jnp.asarray(transform_parts(probe.shape[-1]))
    count, n, _ = parts.shape
    return pl.pallas_call(
        prepare_kernel,
        in_specs=[SMEM, VMEM, VMEM],
        out_specs=[VMEM, VMEM],
        out_shape=[
            jax.ShapeDtypeStruct(probe.shape, F32),
            jax.ShapeDtypeStruct((count, 2 * n, 2 * n), BF16),
        ],
        compiler_params=SMALL,
        name="prepare",
    )(offsets, probe, parts)


def wave_kernel(
    info_ref, own_ref, other_ref, rolled, data_ref, meta_ref, tables,
    out_ref, spread, far, weight, total, q0, q1,
):
    n = data_ref.shape[-1]
    modes = rolled.shape[0]
    half = modes // 2
    sides = n // LANES
    groups = out_ref.shape[0]
    batches = 2 * sides * n // 8 // groups
    cut = info_ref[6]
    y_back, x_back = lax.rem(n - info_ref[4], n), lax.rem(n - info_ref[5], n)
    first = cut == 0
    prop_left, prop_right = (tables.at[0], tables.at[1]), (tables.at[2], tables.at[3])
    far_left, far_right = (tables.at[4], tables.at[5]), (tables.at[6], tables.at[7])
    for panel in range(2 * sides):
        part, side = panel // sides, panel % sides
        own = own_ref[panel * n : (panel + 1) * n, :]
        other = other_ref[panel * n : (panel + 1) * n, :]
        lanes = slice(side * LANES, (side + 1) * LANES)
        q0[part, :, lanes] = jnp.where(first, own, other)
        q1[part, :, lanes] = jnp.where(first, other, own)
    weight[...] = -data_ref[0]
    pairs = [range(i * half, (i + 1) * half) for i in range(2)]

    for pair in pairs:
        lit = [times((rolled[m, 0], rolled[m, 1]), (q0[0], q0[1])) for m in pair]
        waves = two_sided(lit, prop_left, prop_right)
        exits = []
        for m, wave in zip(pair, waves):
            spread[m, 0], spread[m, 1] = wave
            exits.append(times((q1[0], q1[1]), wave))
        waves = two_sided(exits, far_left, far_right)
        power = jnp.zeros((n, n), F32)
        for m, wave in zip(pair, waves):
            far[m, 0], far[m, 1] = wave
            power = power + (wave[0] * wave[0] + wave[1] * wave[1])
        weight[...] += power

    total[...] = jnp.zeros_like(total)
    for place, pair in enumerate(pairs):
        weighted = [(weight[...] * far[m, 0], weight[...] * far[m, 1]) for m in pair]
        chis = two_sided(weighted, far_right, far_left)
        for m, chi in zip(pair, chis):
            far[m, 0], far[m, 1] = chi

        @pl.when(jnp.logical_not(first))
        def _():
            for m in pair:
                term = conj_times((spread[m, 0], spread[m, 1]), (far[m, 0], far[m, 1]))
                total[0] += term[0]
                total[1] += term[1]

        @pl.when(jnp.logical_or(first, place == 1))
        def _():
            backs = [conj_times((q1[0], q1[1]), (far[m, 0], far[m, 1])) for m in pair]
            zetas = two_sided(backs, prop_right, prop_left)

            @pl.when(first)
            def _():
                for m, zeta in zip(pair, zetas):
                    term = conj_times((rolled[m, 0], rolled[m, 1]), zeta)
                    total[0] += term[0]
                    total[1] += term[1]

            @pl.when(place == cut)
            def _():
                rows = n // groups
                for slot, zeta in enumerate(zetas):
                    parts = conj_times((q0[0], q0[1]), zeta)
                    for part in range(2):
                        term = pltpu.roll(pltpu.roll(parts[part], y_back, 0), x_back, 1)
                        for side in range(sides):
                            base = batches * 8 + ((slot * 2 + part) * sides + side) * rows
                            for t in range(groups):
                                out_ref[t, base : base + rows, :] = term[
                                    t * rows : (t + 1) * rows, side * LANES : (side + 1) * LANES
                                ]

    for j in range(2 * sides * n // 8):
        b, t = j // groups, j % groups
        panel, row = divmod(j * 8, n)
        part, side = panel // sides, panel % sides
        out_ref[t, b * 8 : (b + 1) * 8, :] = total[
            part, row : row + 8, side * LANES : (side + 1) * LANES
        ]
    rows = out_ref.shape[1]
    for t in range(groups):
        out_ref[t, rows - 8 : rows, :] = meta_ref[...]


def wave_terms(info, own, other, rolled, measured, meta, tables, groups):
    n = rolled.shape[-1]
    modes = rolled.shape[0]
    g_rows = 2 * n * n // LANES // groups
    rows = g_rows + modes * n * n // LANES // groups + 8
    return pl.pallas_call(
        wave_kernel,
        in_specs=[SMEM] + [VMEM] * 6,
        out_specs=VMEM,
        out_shape=jax.ShapeDtypeStruct((groups, rows, LANES), F32),
        scratch_shapes=[
            pltpu.VMEM((modes, 2, n, n), F32),
            pltpu.VMEM((modes, 2, n, n), F32),
            pltpu.VMEM((n, n), F32),
            pltpu.VMEM((2, n, n), F32),
            pltpu.VMEM((2, n, n), F32),
            pltpu.VMEM((2, n, n), F32),
        ],
        compiler_params=BIG,
        name="wave_terms",
    )(info, own, other, rolled, measured, meta, tables)


def regroup_kernel(g_tiles, p_rows, in_ref, out_ref):
    groups = in_ref.shape[0]
    batches = out_ref.shape[0]
    last = in_ref.shape[1] - 8
    for b in range(batches):
        for t in range(groups):
            out_ref[b, t * 8 : (t + 1) * 8, :] = in_ref[t, b * 8 : (b + 1) * 8, :]
        base = g_tiles * 8 + b * p_rows
        term = in_ref[0, base : base + p_rows, :]
        for t in range(1, groups):
            term = term + in_ref[t, base : base + p_rows, :]
        out_ref[b, groups * 8 : groups * 8 + p_rows, :] = term
        for t in range(groups):
            row = groups * 8 + p_rows + t
            out_ref[b, row : row + 1, :] = in_ref[t, last : last + 1, :]


def regroup(pieces, batches):
    groups, rows, _ = pieces.shape
    p_rows = (rows - 8 - batches * 8) // batches
    whole = pl.BlockSpec(memory_space=pltpu.VMEM)
    return pl.pallas_call(
        partial(regroup_kernel, batches, p_rows),
        in_specs=[whole],
        out_specs=whole,
        out_shape=jax.ShapeDtypeStruct((batches, groups * 8 + p_rows + 8, LANES), F32),
        compiler_params=SMALL,
        name="regroup",
    )(pieces)


def reduce_kernel(n, groups, p_rows, info_ref, table_ref, in_ref, out_ref, acc):
    batches = in_ref.shape[0]
    tiles = acc.shape[1] // 8
    sides = n // LANES
    place = info_ref[7]
    panel, row = lax.div(place * 8, n), lax.rem(place * 8, n)
    u = lax.broadcasted_iota(jnp.int32, (8, LANES), 0) + row
    v = lax.broadcasted_iota(jnp.int32, (8, LANES), 1) + lax.rem(panel, sides) * LANES
    acc[...] = jnp.zeros_like(acc)

    def one_batch(b, carry):
        for t in range(groups):
            at = (b * groups + t) * 8
            value = in_ref[b, t * 8 : (t + 1) * 8, :]
            low, right = u < table_ref[at + 4], v < table_ref[at + 5]
            lower, upper = jnp.where(low, value, 0.0), jnp.where(low, 0.0, value)
            corners = (
                jnp.where(right, 0.0, upper),
                jnp.where(right, upper, 0.0),
                jnp.where(right, 0.0, lower),
                jnp.where(right, lower, 0.0),
            )
            for k in range(4):
                where = pl.ds(pl.multiple_of(table_ref[at + k] * 8, 8), 8)
                acc[k, where, :] += corners[k]
        return carry

    lax.fori_loop(0, batches, one_batch, 0)
    per_owner = tiles // groups * 8
    probe_sum = in_ref[0, groups * 8 : groups * 8 + p_rows, :]
    for b in range(1, batches):
        probe_sum = probe_sum + in_ref[b, groups * 8 : groups * 8 + p_rows, :]
    for o in range(groups):
        rows = slice(o * per_owner, (o + 1) * per_owner)
        summed = (acc[0, rows, :] + acc[1, rows, :]) + (acc[2, rows, :] + acc[3, rows, :])
        for copy in range(2):
            out_ref[copy * groups + o, :per_owner, :] = summed
            out_ref[copy * groups + o, per_owner:, :] = probe_sum


def reduce_positions(info, table, pieces, n, groups, tiles):
    p_rows = pieces.shape[1] - groups * 8 - 8
    whole = pl.BlockSpec(memory_space=pltpu.VMEM)
    smem = pl.BlockSpec(memory_space=pltpu.SMEM)
    return pl.pallas_call(
        partial(reduce_kernel, n, groups, p_rows),
        in_specs=[smem, smem, whole],
        out_specs=whole,
        out_shape=jax.ShapeDtypeStruct((2 * groups, tiles * 8 // groups + p_rows, LANES), F32),
        scratch_shapes=[pltpu.VMEM((4, tiles * 8, LANES), F32)],
        compiler_params=SMALL,
        name="reduce_positions",
    )(info, table, pieces)


def pack_kernel(p_rows, place_ref, in_ref, *out_refs):
    groups = in_ref.shape[0] // 2
    t_rows = in_ref.shape[1] - p_rows
    for h in range(2):
        for t in range(groups):
            for l in range(t_rows // 8):
                at = (l * groups + t) * 8
                out_refs[h][at : at + 8, :] = in_ref[h * groups + t, l * 8 : (l + 1) * 8, :]
        out_refs[h][groups * t_rows :, :] = in_ref[h * groups + place_ref[0], t_rows:, :]


def pack(place, pieces, p_rows):
    groups = pieces.shape[0] // 2
    rows = groups * (pieces.shape[1] - p_rows) + p_rows
    whole = pl.BlockSpec(memory_space=pltpu.VMEM)
    return pl.pallas_call(
        partial(pack_kernel, p_rows),
        in_specs=[pl.BlockSpec(memory_space=pltpu.SMEM), whole],
        out_specs=[whole, whole],
        out_shape=[jax.ShapeDtypeStruct((rows, LANES), F32)] * 2,
        compiler_params=SMALL,
        name="pack",
    )(place, pieces)


def update_kernel(probe_rate, p_rows, where_ref, tile_ref, probe_ref, *refs):
    batches = where_ref.shape[0] - 2
    grads = refs[:batches]
    new_tile_ref, new_probe_ref, held, held_probe, in_sems, out_sems, probe_sem = refs[batches:]
    count, _, n, _ = held.shape
    half, _, strip_rows, _ = held_probe.shape
    sides = n // LANES
    groups = n // strip_rows
    rows = groups * 8
    row_blocks = n // rows
    strips = strip_rows // p_rows
    arrivals, leavings = [], []
    for l in range(count):
        arrivals.append(pltpu.make_async_copy(tile_ref.at[l], held.at[l], in_sems.at[l]))
        leavings.append(pltpu.make_async_copy(held.at[l], new_tile_ref.at[l], out_sems.at[l]))
    cut, member = where_ref[batches], where_ref[batches + 1]
    at = pl.ds(pl.multiple_of(member * strip_rows, strip_rows), strip_rows)
    probe_copy = pltpu.make_async_copy(
        probe_ref.at[pl.ds(cut * half, half), :, at, :], held_probe, probe_sem
    )
    for copy in arrivals:
        copy.start()
    probe_copy.start()
    for l in range(count):
        arrivals[l].wait()
        for i in range(batches):
            batch = where_ref[i]
            panel = lax.div(batch, row_blocks)
            part, side = lax.div(panel, sides), lax.rem(panel, sides)
            at = pl.ds(pl.multiple_of(lax.rem(batch, row_blocks) * rows, rows), rows)
            lanes = pl.ds(pl.multiple_of(side * LANES, LANES), LANES)
            held[l, part, at, lanes] = (
                held[l, part, at, lanes] - OBJECT_RATE * grads[i][l * rows : (l + 1) * rows, :]
            )
        leavings[l].start()
    probe_copy.wait()
    for i in range(batches):
        batch = where_ref[i]
        panel = lax.div(batch, strips)
        field, side = lax.div(panel, sides), lax.rem(panel, sides)
        m, part = lax.div(field, 2), lax.rem(field, 2)
        at = pl.ds(pl.multiple_of(lax.rem(batch, strips) * p_rows, p_rows), p_rows)
        lanes = pl.ds(pl.multiple_of(side * LANES, LANES), LANES)
        new_probe_ref[m, part, at, lanes] = (
            held_probe[m, part, at, lanes] - probe_rate * grads[i][count * rows :, :]
        )
    for copy in leavings:
        copy.wait()


def update(where, tiles, probe, chunks, groups, p_rows, probe_rate):
    count, _, n, _ = tiles.shape
    probe_shape = (probe.shape[0] // 2, 2, n // groups, n)
    return pl.pallas_call(
        partial(update_kernel, probe_rate, p_rows),
        in_specs=[SMEM, HBM, HBM] + [VMEM] * len(chunks),
        out_specs=[HBM, VMEM],
        out_shape=[jax.ShapeDtypeStruct(tiles.shape, F32), jax.ShapeDtypeStruct(probe_shape, F32)],
        scratch_shapes=[
            pltpu.VMEM(tiles.shape, F32),
            pltpu.VMEM(probe_shape, F32),
            pltpu.SemaphoreType.DMA((count,)),
            pltpu.SemaphoreType.DMA((count,)),
            pltpu.SemaphoreType.DMA,
        ],
        compiler_params=SMALL,
        name="update",
    )(where, in_hbm(tiles), in_hbm(probe), *chunks)


def local(objects, probe, measured, send_list, corner_slot, offsets):
    n = probe.shape[-1]
    half = probe.shape[0] // 2
    groups = lax.axis_size("tile")
    batches = lax.axis_size("batch")
    z_size = batches // 2
    cut = lax.axis_index("cuts")
    member = lax.axis_index("tile")
    batch = lax.axis_index("batch")
    tiles = objects[0]
    tile_count = tiles.shape[0]
    info = jnp.concatenate(
        [
            corner_slot.reshape(-1),
            offsets.reshape(-1),
            jnp.stack([cut, batch * groups + member]).astype(jnp.int32),
        ]
    )
    meta_row = jnp.concatenate(
        [send_list.reshape(-1), corner_slot.reshape(-1), offsets.reshape(-1)]
    ).astype(F32)
    meta = jnp.zeros((8, LANES), F32).at[0, : meta_row.shape[0]].set(meta_row)

    with jax.named_scope("fetch_tiles"):
        ids = jnp.stack([cut, batch, member]).astype(jnp.int32)
        note = jnp.concatenate([corner_slot, offsets], axis=1)
        ready = (prepare(offsets, probe), info, meta)
        own, ((rolled, tables), info, meta) = fetch(ids, tiles, send_list, note, ready)
        other = lax.ppermute(own, "cuts", [(0, 1), (1, 0)])
    with jax.named_scope("waves"):
        pieces = wave_terms(info, own, other, rolled, measured, meta, tables, groups)
    with jax.named_scope("return_terms"):
        pieces = lax.all_to_all(pieces, "tile", split_axis=0, concat_axis=0, tiled=True)
        pieces = regroup(pieces, batches)
        pieces = lax.all_to_all(pieces, "batch", split_axis=0, concat_axis=0, tiled=True)
        last = pieces.shape[1] - 8
        notes = pieces[:, last:, : meta_row.shape[0]].astype(jnp.int32)
        lists, slots, starts = notes[..., :groups], notes[..., groups : groups + 4], notes[..., groups + 4 :]
        owners = jnp.arange(groups, dtype=jnp.int32)
        chosen = slots[:, None, :, :] == owners[None, :, None, None]
        sent = jnp.sum(jnp.where(chosen, lists[:, :, :, None], 0), axis=1)
        table = jnp.concatenate(
            [slots * tile_count + sent, starts, jnp.zeros_like(starts)], axis=-1
        ).reshape(-1)
        p_rows = last - groups * 8
        summed = reduce_positions(info, table, pieces, n, groups, groups * tile_count)
        planes = [
            [(z * 2 + h) * groups + t for h in range(2) for t in range(groups)]
            for z in range(z_size)
        ]
        summed = lax.all_to_all(
            summed, ("batch", "tile"), split_axis=0, concat_axis=0, axis_index_groups=planes, tiled=True
        )
        packed = pack(member.reshape(1).astype(jnp.int32), summed, p_rows)
    with jax.named_scope("spread_sums"):
        onward = [(i, (i + 2) % batches) for i in range(batches)]
        backward = [(i, (i - 2) % batches) for i in range(batches)]
        z = batch // 2
        rate = PROBE_RATE / math.sqrt(batches * groups * measured.shape[0])
        found = []
        ahead = [packed[0], packed[1]]
        behind = [packed[0], packed[1]]
        for h in range(2):
            found.append((z, h, packed[h]))
        for step in range(1, z_size // 2 + 1):
            final = step == z_size // 2
            for h in range(2):
                if not (final and h == 1):
                    ahead[h] = lax.ppermute(ahead[h], "batch", onward)
                    found.append((z - step, h, ahead[h]))
                if not (final and h == 0):
                    behind[h] = lax.ppermute(behind[h], "batch", backward)
                    found.append((z + step, h, behind[h]))
        places = [lax.rem(place + z_size, z_size) * 2 + h for place, h, _ in found]
        where = jnp.stack(places + [cut, member]).astype(jnp.int32)
        new_tiles, new_probe = update(
            where, tiles, probe, [chunk for _, _, chunk in found], groups, p_rows, rate
        )
    return (new_tiles[None], new_probe)


def solution(mesh):
    in_specs = (
        P("cuts", "tile", None, None, None),
        P(),
        P(("batch", "tile"), None, None),
        P("batch", "tile", None),
        P(("batch", "tile"), None),
        P(("batch", "tile"), None),
    )
    out_specs = (P("cuts", "tile", None, None, None), P("cuts", None, "tile", None))
    return jax.shard_map(local, mesh=mesh, in_specs=in_specs, out_specs=out_specs, check_vma=False)
```

```python
from functools import partial
import math

import jax
import jax.numpy as jnp
from jax import lax
from jax.experimental import pallas as pl
from jax.experimental.pallas import tpu as pltpu
from jax.sharding import PartitionSpec as P
import ml_dtypes
import numpy as np

OBJECT_RATE = 0.02
PROBE_RATE = 0.05
LANES = 128
BIG = pltpu.CompilerParams(vmem_limit_bytes=32 * 1024 * 1024)
SMALL = pltpu.CompilerParams(vmem_limit_bytes=14 * 1024 * 1024)
F32 = jnp.float32
BF16 = jnp.bfloat16


def halves(matrix):
    upper = matrix.astype(ml_dtypes.bfloat16)
    lower = (matrix - upper.astype(np.float64)).astype(ml_dtypes.bfloat16)
    return upper, lower


def matrix_parts(matrix):
    return halves(matrix.real) + halves(matrix.imag)


def transform_parts(length):
    counter = np.arange(length)
    wave = np.exp(-2j * math.pi / length * (counter[:, None] * counter[None, :] % length))
    signed = np.where(counter < length // 2, counter, counter - length)
    chirp = np.exp(-1j * math.pi / length * (signed * signed % (2 * length)))
    fresnel = (np.conj(wave) * chirp[None, :]) @ wave / length
    return np.stack(matrix_parts(fresnel) + matrix_parts(wave / math.sqrt(length)))


def split(value):
    upper = value.astype(BF16)
    lower = (value - upper.astype(F32)).astype(BF16)
    return upper, lower


def dot(a, b):
    return jnp.dot(a, b, preferred_element_type=F32)


def two_sided(fields, left, right):
    n = fields[0][0].shape[0]
    parts = [jnp.concatenate([field[part] for field in fields], axis=1) for part in range(2)]
    upper, lower = split(jnp.concatenate(parts, axis=0))
    rows = dot(left[0][...], upper) + dot(left[0][...], lower) + dot(left[1][...], upper)
    stacked = [
        jnp.concatenate([rows[:n, i * n : (i + 1) * n], rows[n:, i * n : (i + 1) * n]], axis=1)
        for i in range(len(fields))
    ]
    upper, lower = split(jnp.concatenate(stacked, axis=0))
    both = dot(upper, right[0][...]) + dot(lower, right[0][...]) + dot(upper, right[1][...])
    return [
        (both[i * n : (i + 1) * n, :n], both[i * n : (i + 1) * n, n:]) for i in range(len(fields))
    ]


def times(a, b):
    return a[0] * b[0] - a[1] * b[1], a[0] * b[1] + a[1] * b[0]


def conj_times(a, b):
    return a[0] * b[0] + a[1] * b[1], a[0] * b[1] - a[1] * b[0]


SMEM = pl.BlockSpec(memory_space=pltpu.SMEM)
VMEM = pl.BlockSpec(memory_space=pltpu.VMEM)
HBM = pl.BlockSpec(memory_space=pltpu.HBM)


def in_hbm(value):
    return pltpu.with_memory_space_constraint(value, pltpu.HBM)


def pick_kernel(ids_ref, list_ref, *refs):
    count = len(refs) // 2
    for i in range(count):
        refs[count + i][...] = refs[i][0]


def pick_tiles(ids, send_list, tiles, near, steps):
    width = send_list.shape[-1] // 2

    def picked(step):
        def index(i, ids, lists):
            lower, column = lax.div(ids[2], width), lax.rem(ids[2], width)
            row = 1 - lower if near else lower
            return (lists[0, 0, row * width + lax.rem(column + step, width)], 0, 0, 0)

        return pl.BlockSpec((1,) + tiles.shape[1:], index)

    return pl.pallas_call(
        pick_kernel,
        grid_spec=pltpu.PrefetchScalarGridSpec(
            num_scalar_prefetch=2,
            grid=(1,),
            in_specs=[picked(step) for step in steps],
            out_specs=[VMEM] * len(steps),
        ),
        out_shape=[jax.ShapeDtypeStruct(tiles.shape[1:], F32)] * len(steps),
        compiler_params=SMALL,
        name="pick_tiles",
    )(ids, send_list, *[in_hbm(tiles)] * len(steps))


def select_kernel(wanted, groups, ids_ref, *refs):
    steps = sorted({step for pieces in wanted for step, _, _ in pieces})
    notes = dict(zip(steps, refs))
    own = dict(zip(steps, refs[len(steps) :]))
    nears = dict(zip(steps, refs[2 * len(steps) :]))
    terms = refs[3 * len(steps) : len(refs) - len(wanted)]
    outs = refs[len(refs) - len(wanted) :]
    n = own[steps[0]].shape[-1]
    sides = n // LANES
    here = ids_ref[2]
    near = lax.rem(here + groups // 2, groups)
    for pieces, out_ref in zip(wanted, outs):
        for place, (step, part, added) in enumerate(pieces):
            note = notes[step]
            for side in range(sides):
                u = lax.broadcasted_iota(jnp.int32, (n, LANES), 0)
                v = lax.broadcasted_iota(jnp.int32, (n, LANES), 1) + side * LANES
                low, right = u < note[0, 4], v < note[0, 5]
                owner = jnp.where(
                    low,
                    jnp.where(right, note[0, 3], note[0, 2]),
                    jnp.where(right, note[0, 1], note[0, 0]),
                )
                lanes = slice(side * LANES, (side + 1) * LANES)
                value = jnp.where(
                    owner == here,
                    own[step][part, :, lanes],
                    jnp.where(owner == near, nears[step][part, :, lanes], 0.0),
                )
                for index in added:
                    value = value + terms[index][side * n : (side + 1) * n, :]
                at = (place * sides + side) * n
                out_ref[at : at + n, :] = value


def select_cells(ids, notes, own, nears, wanted, terms=()):
    n = own[0].shape[-1]
    rows = n * (n // LANES)
    steps = sorted({step for pieces in wanted for step, _, _ in pieces})
    return pl.pallas_call(
        partial(select_kernel, wanted, lax.axis_size("tile")),
        in_specs=[SMEM] * (1 + len(steps)) + [VMEM] * (2 * len(steps) + len(terms)),
        out_specs=[VMEM] * len(wanted),
        out_shape=[jax.ShapeDtypeStruct((rows * len(pieces), LANES), F32) for pieces in wanted],
        compiler_params=SMALL,
        name="select_cells",
    )(ids, *[group[step] for group in (notes, own, nears) for step in steps], *terms)


def fetch(ids, tiles, send_list, note, ready):
    groups = lax.axis_size("tile")
    batches = lax.axis_size("batch")
    width = groups // 2
    along = lambda d: [
        (y * width + x, y * width + (x + d) % width) for y in range(2) for x in range(width)
    ]
    send = lambda block, d: lax.ppermute(block, "tile", along(d))
    far_list = lax.ppermute(send_list, "batch", [(i, i ^ 1) for i in range(batches)])
    same = [(t, (t + width) % groups) for t in range(groups)]
    other = []
    for b in range(batches):
        for t in range(groups):
            y = (b % 2) * 2 + t // width
            step = (y + 1) % 4 if y % 2 == 1 else (y - 1) % 4
            other.append(
                (b * groups + t, (b // 2 * 2 + step // 2) * groups + step % 2 * width + t % width)
            )
    notes = {0: note}
    for d in range(1, width):
        notes[d] = send(note, -d)
    first = pick_tiles(ids, send_list, tiles, True, (2, 1))
    first, far_list = lax.optimization_barrier((first, far_list))
    second = pick_tiles(ids, far_list, tiles, True, (3, 0))
    nears = {2: lax.ppermute(first[0], "tile", same)}
    nears[3] = lax.ppermute(second[0], ("batch", "tile"), other)
    later, notes = lax.optimization_barrier(((first[1], second[1]), notes))
    nears[1] = lax.ppermute(later[0], "tile", same)
    nears[0] = lax.ppermute(later[1], ("batch", "tile"), other)
    own = pick_tiles(ids, send_list, tiles, False, (2, 1, 3, 0))
    own = dict(zip((2, 1, 3, 0), own))
    select = lambda wanted, terms=(): select_cells(ids, notes, own, nears, wanted, terms)
    far_re, far_im = select([[(2, 0, ())], [(2, 1, ())]])
    far_re, far_im = send(far_re, 1), send(far_im, -1)
    far_re, far_im, ready = lax.optimization_barrier((far_re, far_im, ready))
    up_im = send(select([[(1, 1, ())]])[0], 1)
    down_re = send(select([[(3, 0, ())]])[0], -1)
    up_re = send(select([[(1, 0, (0,))]], (far_re,))[0], 1)
    down_im = send(select([[(3, 1, (0,))]], (far_im,))[0], -1)
    patch = select([[(0, 0, (0, 1)), (0, 1, (2, 3))]], (up_re, down_re, up_im, down_im))[0]
    return patch, ready


def prepare_kernel(start_ref, probe_ref, part_ref, rolled_ref, table_ref):
    n = probe_ref.shape[-1]
    for m in range(probe_ref.shape[0]):
        for part in range(2):
            value = pltpu.roll(probe_ref[m, part], start_ref[0, 0], 0)
            rolled_ref[m, part] = pltpu.roll(value, start_ref[0, 1], 1)
    for transform in range(part_ref.shape[0] // 4):
        for low in range(2):
            re = part_ref[transform * 4 + low]
            im = part_ref[transform * 4 + 2 + low]
            left, right = transform * 4 + low, transform * 4 + 2 + low
            for table, upper_right, lower_left in ((left, -im, im), (right, im, -im)):
                table_ref[table, :n, :n] = re
                table_ref[table, n:, n:] = re
                table_ref[table, :n, n:] = upper_right
                table_ref[table, n:, :n] = lower_left


def prepare(offsets, probe):
    parts = jnp.asarray(transform_parts(probe.shape[-1]))
    count, n, _ = parts.shape
    return pl.pallas_call(
        prepare_kernel,
        in_specs=[SMEM, VMEM, VMEM],
        out_specs=[VMEM, VMEM],
        out_shape=[
            jax.ShapeDtypeStruct(probe.shape, F32),
            jax.ShapeDtypeStruct((count, 2 * n, 2 * n), BF16),
        ],
        compiler_params=SMALL,
        name="prepare",
    )(offsets, probe, parts)


def wave_kernel(
    info_ref, own_ref, other_ref, rolled, data_ref, meta_ref, tables,
    out_ref, spread, far, weight, total, q0, q1,
):
    n = data_ref.shape[-1]
    modes = rolled.shape[0]
    half = modes // 2
    sides = n // LANES
    groups = out_ref.shape[0]
    batches = 2 * sides * n // 8 // groups
    cut = info_ref[6]
    y_back, x_back = lax.rem(n - info_ref[4], n), lax.rem(n - info_ref[5], n)
    first = cut == 0
    prop_left, prop_right = (tables.at[0], tables.at[1]), (tables.at[2], tables.at[3])
    far_left, far_right = (tables.at[4], tables.at[5]), (tables.at[6], tables.at[7])
    for panel in range(2 * sides):
        part, side = panel // sides, panel % sides
        own = own_ref[panel * n : (panel + 1) * n, :]
        other = other_ref[panel * n : (panel + 1) * n, :]
        lanes = slice(side * LANES, (side + 1) * LANES)
        q0[part, :, lanes] = jnp.where(first, own, other)
        q1[part, :, lanes] = jnp.where(first, other, own)
    weight[...] = -data_ref[0]
    pairs = [range(i * half, (i + 1) * half) for i in range(2)]

    for pair in pairs:
        lit = [times((rolled[m, 0], rolled[m, 1]), (q0[0], q0[1])) for m in pair]
        waves = two_sided(lit, prop_left, prop_right)
        exits = []
        for m, wave in zip(pair, waves):
            spread[m, 0], spread[m, 1] = wave
            exits.append(times((q1[0], q1[1]), wave))
        waves = two_sided(exits, far_left, far_right)
        power = jnp.zeros((n, n), F32)
        for m, wave in zip(pair, waves):
            far[m, 0], far[m, 1] = wave
            power = power + (wave[0] * wave[0] + wave[1] * wave[1])
        weight[...] += power

    total[...] = jnp.zeros_like(total)
    for place, pair in enumerate(pairs):
        weighted = [(weight[...] * far[m, 0], weight[...] * far[m, 1]) for m in pair]
        chis = two_sided(weighted, far_right, far_left)
        for m, chi in zip(pair, chis):
            far[m, 0], far[m, 1] = chi

        @pl.when(jnp.logical_not(first))
        def _():
            for m in pair:
                term = conj_times((spread[m, 0], spread[m, 1]), (far[m, 0], far[m, 1]))
                total[0] += term[0]
                total[1] += term[1]

        @pl.when(jnp.logical_or(first, place == 1))
        def _():
            backs = [conj_times((q1[0], q1[1]), (far[m, 0], far[m, 1])) for m in pair]
            zetas = two_sided(backs, prop_right, prop_left)

            @pl.when(first)
            def _():
                for m, zeta in zip(pair, zetas):
                    term = conj_times((rolled[m, 0], rolled[m, 1]), zeta)
                    total[0] += term[0]
                    total[1] += term[1]

            @pl.when(place == cut)
            def _():
                rows = n // groups
                for slot, zeta in enumerate(zetas):
                    parts = conj_times((q0[0], q0[1]), zeta)
                    for part in range(2):
                        term = pltpu.roll(pltpu.roll(parts[part], y_back, 0), x_back, 1)
                        for side in range(sides):
                            base = batches * 8 + ((slot * 2 + part) * sides + side) * rows
                            for t in range(groups):
                                out_ref[t, base : base + rows, :] = term[
                                    t * rows : (t + 1) * rows, side * LANES : (side + 1) * LANES
                                ]

    for j in range(2 * sides * n // 8):
        b, t = j // groups, j % groups
        panel, row = divmod(j * 8, n)
        part, side = panel // sides, panel % sides
        out_ref[t, b * 8 : (b + 1) * 8, :] = total[
            part, row : row + 8, side * LANES : (side + 1) * LANES
        ]
    rows = out_ref.shape[1]
    for t in range(groups):
        out_ref[t, rows - 8 : rows, :] = meta_ref[...]


def wave_terms(info, own, other, rolled, measured, meta, tables, groups):
    n = rolled.shape[-1]
    modes = rolled.shape[0]
    g_rows = 2 * n * n // LANES // groups
    rows = g_rows + modes * n * n // LANES // groups + 8
    return pl.pallas_call(
        wave_kernel,
        in_specs=[SMEM] + [VMEM] * 6,
        out_specs=VMEM,
        out_shape=jax.ShapeDtypeStruct((groups, rows, LANES), F32),
        scratch_shapes=[
            pltpu.VMEM((modes, 2, n, n), F32),
            pltpu.VMEM((modes, 2, n, n), F32),
            pltpu.VMEM((n, n), F32),
            pltpu.VMEM((2, n, n), F32),
            pltpu.VMEM((2, n, n), F32),
            pltpu.VMEM((2, n, n), F32),
        ],
        compiler_params=BIG,
        name="wave_terms",
    )(info, own, other, rolled, measured, meta, tables)


def regroup_kernel(g_tiles, p_rows, in_ref, out_ref):
    groups = in_ref.shape[0]
    batches = out_ref.shape[0]
    last = in_ref.shape[1] - 8
    for b in range(batches):
        for t in range(groups):
            out_ref[b, t * 8 : (t + 1) * 8, :] = in_ref[t, b * 8 : (b + 1) * 8, :]
        base = g_tiles * 8 + b * p_rows
        term = in_ref[0, base : base + p_rows, :]
        for t in range(1, groups):
            term = term + in_ref[t, base : base + p_rows, :]
        out_ref[b, groups * 8 : groups * 8 + p_rows, :] = term
        for t in range(groups):
            row = groups * 8 + p_rows + t
            out_ref[b, row : row + 1, :] = in_ref[t, last : last + 1, :]


def regroup(pieces, batches):
    groups, rows, _ = pieces.shape
    p_rows = (rows - 8 - batches * 8) // batches
    whole = pl.BlockSpec(memory_space=pltpu.VMEM)
    return pl.pallas_call(
        partial(regroup_kernel, batches, p_rows),
        in_specs=[whole],
        out_specs=whole,
        out_shape=jax.ShapeDtypeStruct((batches, groups * 8 + p_rows + 8, LANES), F32),
        compiler_params=SMALL,
        name="regroup",
    )(pieces)


def reduce_kernel(n, groups, p_rows, info_ref, table_ref, in_ref, out_ref, acc):
    batches = in_ref.shape[0]
    tiles = acc.shape[1] // 8
    sides = n // LANES
    place = info_ref[7]
    panel, row = lax.div(place * 8, n), lax.rem(place * 8, n)
    u = lax.broadcasted_iota(jnp.int32, (8, LANES), 0) + row
    v = lax.broadcasted_iota(jnp.int32, (8, LANES), 1) + lax.rem(panel, sides) * LANES
    acc[...] = jnp.zeros_like(acc)

    def one_batch(b, carry):
        for t in range(groups):
            at = (b * groups + t) * 8
            value = in_ref[b, t * 8 : (t + 1) * 8, :]
            low, right = u < table_ref[at + 4], v < table_ref[at + 5]
            lower, upper = jnp.where(low, value, 0.0), jnp.where(low, 0.0, value)
            corners = (
                jnp.where(right, 0.0, upper),
                jnp.where(right, upper, 0.0),
                jnp.where(right, 0.0, lower),
                jnp.where(right, lower, 0.0),
            )
            for k in range(4):
                where = pl.ds(pl.multiple_of(table_ref[at + k] * 8, 8), 8)
                acc[k, where, :] += corners[k]
        return carry

    lax.fori_loop(0, batches, one_batch, 0)
    per_owner = tiles // groups * 8
    probe_sum = in_ref[0, groups * 8 : groups * 8 + p_rows, :]
    for b in range(1, batches):
        probe_sum = probe_sum + in_ref[b, groups * 8 : groups * 8 + p_rows, :]
    for o in range(groups):
        rows = slice(o * per_owner, (o + 1) * per_owner)
        summed = (acc[0, rows, :] + acc[1, rows, :]) + (acc[2, rows, :] + acc[3, rows, :])
        for copy in range(2):
            out_ref[copy * groups + o, :per_owner, :] = summed
            out_ref[copy * groups + o, per_owner:, :] = probe_sum


def reduce_positions(info, table, pieces, n, groups, tiles):
    p_rows = pieces.shape[1] - groups * 8 - 8
    whole = pl.BlockSpec(memory_space=pltpu.VMEM)
    smem = pl.BlockSpec(memory_space=pltpu.SMEM)
    return pl.pallas_call(
        partial(reduce_kernel, n, groups, p_rows),
        in_specs=[smem, smem, whole],
        out_specs=whole,
        out_shape=jax.ShapeDtypeStruct((2 * groups, tiles * 8 // groups + p_rows, LANES), F32),
        scratch_shapes=[pltpu.VMEM((4, tiles * 8, LANES), F32)],
        compiler_params=SMALL,
        name="reduce_positions",
    )(info, table, pieces)


def pack_kernel(p_rows, place_ref, in_ref, *out_refs):
    groups = in_ref.shape[0] // 2
    t_rows = in_ref.shape[1] - p_rows
    for h in range(2):
        for t in range(groups):
            for l in range(t_rows // 8):
                at = (l * groups + t) * 8
                out_refs[h][at : at + 8, :] = in_ref[h * groups + t, l * 8 : (l + 1) * 8, :]
        out_refs[h][groups * t_rows :, :] = in_ref[h * groups + place_ref[0], t_rows:, :]


def pack(place, pieces, p_rows):
    groups = pieces.shape[0] // 2
    rows = groups * (pieces.shape[1] - p_rows) + p_rows
    whole = pl.BlockSpec(memory_space=pltpu.VMEM)
    return pl.pallas_call(
        partial(pack_kernel, p_rows),
        in_specs=[pl.BlockSpec(memory_space=pltpu.SMEM), whole],
        out_specs=[whole, whole],
        out_shape=[jax.ShapeDtypeStruct((rows, LANES), F32)] * 2,
        compiler_params=SMALL,
        name="pack",
    )(place, pieces)


def update_kernel(probe_rate, p_rows, where_ref, tile_ref, probe_ref, *refs):
    batches = where_ref.shape[0] - 2
    grads = refs[:batches]
    new_tile_ref, new_probe_ref, held, held_probe, in_sems, out_sems, probe_sem = refs[batches:]
    count, _, n, _ = held.shape
    half, _, strip_rows, _ = held_probe.shape
    sides = n // LANES
    groups = n // strip_rows
    rows = groups * 8
    row_blocks = n // rows
    strips = strip_rows // p_rows
    arrivals, leavings = [], []
    for l in range(count):
        arrivals.append(pltpu.make_async_copy(tile_ref.at[l], held.at[l], in_sems.at[l]))
        leavings.append(pltpu.make_async_copy(held.at[l], new_tile_ref.at[l], out_sems.at[l]))
    cut, member = where_ref[batches], where_ref[batches + 1]
    at = pl.ds(pl.multiple_of(member * strip_rows, strip_rows), strip_rows)
    probe_copy = pltpu.make_async_copy(
        probe_ref.at[pl.ds(cut * half, half), :, at, :], held_probe, probe_sem
    )
    for copy in arrivals:
        copy.start()
    probe_copy.start()
    for l in range(count):
        arrivals[l].wait()
        for i in range(batches):
            batch = where_ref[i]
            panel = lax.div(batch, row_blocks)
            part, side = lax.div(panel, sides), lax.rem(panel, sides)
            at = pl.ds(pl.multiple_of(lax.rem(batch, row_blocks) * rows, rows), rows)
            lanes = pl.ds(pl.multiple_of(side * LANES, LANES), LANES)
            held[l, part, at, lanes] = (
                held[l, part, at, lanes] - OBJECT_RATE * grads[i][l * rows : (l + 1) * rows, :]
            )
        leavings[l].start()
    probe_copy.wait()
    for i in range(batches):
        batch = where_ref[i]
        panel = lax.div(batch, strips)
        field, side = lax.div(panel, sides), lax.rem(panel, sides)
        m, part = lax.div(field, 2), lax.rem(field, 2)
        at = pl.ds(pl.multiple_of(lax.rem(batch, strips) * p_rows, p_rows), p_rows)
        lanes = pl.ds(pl.multiple_of(side * LANES, LANES), LANES)
        new_probe_ref[m, part, at, lanes] = (
            held_probe[m, part, at, lanes] - probe_rate * grads[i][count * rows :, :]
        )
    for copy in leavings:
        copy.wait()


def update(where, tiles, probe, chunks, groups, p_rows, probe_rate):
    count, _, n, _ = tiles.shape
    probe_shape = (probe.shape[0] // 2, 2, n // groups, n)
    return pl.pallas_call(
        partial(update_kernel, probe_rate, p_rows),
        in_specs=[SMEM, HBM, HBM] + [VMEM] * len(chunks),
        out_specs=[HBM, VMEM],
        out_shape=[jax.ShapeDtypeStruct(tiles.shape, F32), jax.ShapeDtypeStruct(probe_shape, F32)],
        scratch_shapes=[
            pltpu.VMEM(tiles.shape, F32),
            pltpu.VMEM(probe_shape, F32),
            pltpu.SemaphoreType.DMA((count,)),
            pltpu.SemaphoreType.DMA((count,)),
            pltpu.SemaphoreType.DMA,
        ],
        compiler_params=SMALL,
        name="update",
    )(where, in_hbm(tiles), in_hbm(probe), *chunks)


def local(objects, probe, measured, send_list, corner_slot, offsets):
    n = probe.shape[-1]
    half = probe.shape[0] // 2
    groups = lax.axis_size("tile")
    batches = lax.axis_size("batch")
    z_size = batches // 2
    cut = lax.axis_index("cuts")
    member = lax.axis_index("tile")
    batch = lax.axis_index("batch")
    tiles = objects[0]
    tile_count = tiles.shape[0]
    info = jnp.concatenate(
        [
            corner_slot.reshape(-1),
            offsets.reshape(-1),
            jnp.stack([cut, batch * groups + member]).astype(jnp.int32),
        ]
    )
    meta_row = jnp.concatenate(
        [send_list.reshape(-1), corner_slot.reshape(-1), offsets.reshape(-1)]
    ).astype(F32)
    meta = jnp.zeros((8, LANES), F32).at[0, : meta_row.shape[0]].set(meta_row)

    with jax.named_scope("fetch_tiles"):
        ids = jnp.stack([cut, batch, member]).astype(jnp.int32)
        note = jnp.concatenate([corner_slot, offsets], axis=1)
        ready = (prepare(offsets, probe), info, meta)
        own, ((rolled, tables), info, meta) = fetch(ids, tiles, send_list, note, ready)
        other = lax.ppermute(own, "cuts", [(0, 1), (1, 0)])
    with jax.named_scope("waves"):
        pieces = wave_terms(info, own, other, rolled, measured, meta, tables, groups)
    with jax.named_scope("return_terms"):
        pieces = lax.all_to_all(pieces, "tile", split_axis=0, concat_axis=0, tiled=True)
        pieces = regroup(pieces, batches)
        pieces = lax.all_to_all(pieces, "batch", split_axis=0, concat_axis=0, tiled=True)
        last = pieces.shape[1] - 8
        notes = pieces[:, last:, : meta_row.shape[0]].astype(jnp.int32)
        lists, slots, starts = notes[..., :groups], notes[..., groups : groups + 4], notes[..., groups + 4 :]
        owners = jnp.arange(groups, dtype=jnp.int32)
        chosen = slots[:, None, :, :] == owners[None, :, None, None]
        sent = jnp.sum(jnp.where(chosen, lists[:, :, :, None], 0), axis=1)
        table = jnp.concatenate(
            [slots * tile_count + sent, starts, jnp.zeros_like(starts)], axis=-1
        ).reshape(-1)
        p_rows = last - groups * 8
        summed = reduce_positions(info, table, pieces, n, groups, groups * tile_count)
        planes = [
            [(z * 2 + h) * groups + t for h in range(2) for t in range(groups)]
            for z in range(z_size)
        ]
        summed = lax.all_to_all(
            summed, ("batch", "tile"), split_axis=0, concat_axis=0, axis_index_groups=planes, tiled=True
        )
        packed = pack(member.reshape(1).astype(jnp.int32), summed, p_rows)
    with jax.named_scope("spread_sums"):
        onward = [(i, (i + 2) % batches) for i in range(batches)]
        backward = [(i, (i - 2) % batches) for i in range(batches)]
        z = batch // 2
        rate = PROBE_RATE / math.sqrt(batches * groups * measured.shape[0])
        found = []
        ahead = [packed[0], packed[1]]
        behind = [packed[0], packed[1]]
        for h in range(2):
            found.append((z, h, packed[h]))
        for step in range(1, z_size // 2 + 1):
            final = step == z_size // 2
            for h in range(2):
                if not (final and h == 1):
                    ahead[h] = lax.ppermute(ahead[h], "batch", onward)
                    found.append((z - step, h, ahead[h]))
                if not (final and h == 0):
                    behind[h] = lax.ppermute(behind[h], "batch", backward)
                    found.append((z + step, h, behind[h]))
        places = [lax.rem(place + z_size, z_size) * 2 + h for place, h, _ in found]
        where = jnp.stack(places + [cut, member]).astype(jnp.int32)
        new_tiles, new_probe = update(
            where, tiles, probe, [chunk for _, _, chunk in found], groups, p_rows, rate
        )
    return (new_tiles[None], new_probe)


def solution(mesh):
    in_specs = (
        P("cuts", "tile", None, None, None),
        P(),
        P(("batch", "tile"), None, None),
        P("batch", "tile", None),
        P(("batch", "tile"), None),
        P(("batch", "tile"), None),
    )
    out_specs = (P("cuts", "tile", None, None, None), P("cuts", None, "tile", None))
    return jax.shard_map(local, mesh=mesh, in_specs=in_specs, out_specs=out_specs, check_vma=False)
```
